128 devices in a mesh: gx: 16 (over x, z), gy: 8 (over y, core).
Axes of the slice: x: 4, y: 4, z: 4, core: 2. Of those that a mesh axis runs over, the one named last changes fastest.
Arguments:
- mean_field: float32 [16, 256, 2048], P(None, 'gx', 'gy'), may hold values from -6 to 6
- mode_fields: float32 [16, 16, 256, 2048], P(None, None, 'gx', 'gy'), may hold values from -6 to 6
- velocity_east: float32 [16, 256, 2048], P(None, 'gx', 'gy'), may hold values from -6 to 6
- velocity_north: float32 [16, 256, 2048], P(None, 'gx', 'gy'), may hold values from -6 to 6
- flag_east: int32 [16, 256, 2048], P(None, 'gx', 'gy'), may hold values 0 or 1
- flag_north: int32 [16, 256, 2048], P(None, 'gx', 'gy'), may hold values 0 or 1
- ocean_mask: int32 [16, 256, 2048], P(None, 'gx', 'gy'), may hold values 0 or 1
Outputs:
- mean_next: float32 [16, 256, 2048], P(None, 'gx', 'gy')
- modes_next: float32 [16, 16, 256, 2048], P(None, None, 'gx', 'gy')
- factor: float32 [16, 16], replicated
The draws below stay inside these ranges and needn't reach their ends.
Inputs may be any that keep to these rules, and one draw needn't show every extreme that they name: `flag_east`: 1 takes the five-point upwind value biased to the cell of lower index beside the face, 0 the one biased to the higher. `flag_north`: as for the first dimension. `ocean_mask`: 1 marks ocean, 0 land.
All inputs are finite; a program needn't handle non-finite values. No bound on the sum of `flag_east` or of `flag_north` or of `ocean_mask` on one device may be relied on, other than what follows from the above.
Results may differ from the reference program's by a relative error of at most 0.0003.
Values sent between devices are 32-bit elements; how exact they have to be, the bound alone decides.
No kernel may reach another device: no remote copies, remote signals or barrier semaphores. Data moves between devices by JAX's collectives and lax.ppermute only.
A program may use at most 128 MiB of HBM per device.

```python
import jax
import jax.numpy as jnp
from jax import lax

M = 16
NZ = 16
NX = 256
NY = 2048


def with_ends(values, stream_key, low, high):
    spot = [jax.random.randint(jax.random.fold_in(stream_key, axis), (), 0, length) for axis, length in enumerate(values.shape)]
    main_axis = values.shape.index(max(values.shape))
    next_to = spot[:main_axis] + [(spot[main_axis] + 1) % values.shape[main_axis]] + spot[main_axis + 1:]
    return values.at[tuple(spot)].set(low).at[tuple(next_to)].set(high)


def block_scale(rng, shape, cuts, least, top_value):
    loudness = 1.0
    for position, parts in cuts:
        heights = jax.random.uniform(jax.random.fold_in(jax.random.fold_in(rng, 6), position), (parts,), jnp.float32, least / len(cuts), top_value / len(cuts))
        loudness = loudness * jnp.repeat(jnp.exp(heights), shape[position] // parts).reshape((-1,) + (1,) * (len(shape) - 1 - position))
    return loudness


def scatter_about(rng, dims, width, bound, cuts=(), held_as=jnp.bfloat16):
    result = width * jax.random.normal(rng, dims, jnp.float32)
    if cuts:
        result = result * block_scale(rng, dims, cuts, -0.22, 0.18)
    return jnp.clip(result, -bound, bound).astype(held_as)


def setup_inputs(seed: int = 0) -> dict:
    key_of = jax.random.split(jax.random.key(seed), 8)
    return {
        "mean_field": scatter_about(key_of[0], (NZ, NX, NY), 1.0, 6.0, ((1, 16), (2, 8)), jnp.float32),
        "mode_fields": scatter_about(key_of[1], (M, NZ, NX, NY), 1.0, 6.0, ((2, 16), (3, 8)), jnp.float32),
        "velocity_east": scatter_about(key_of[2], (NZ, NX, NY), 1.0, 6.0, ((1, 16), (2, 8)), jnp.float32),
        "velocity_north": scatter_about(key_of[3], (NZ, NX, NY), 1.0, 6.0, ((1, 16), (2, 8)), jnp.float32),
        "flag_east": with_ends((jax.random.randint(key_of[4], (NZ, NX, NY), 0, 2) < 1).astype(jnp.int32), jax.random.fold_in(key_of[4], 1), 0, 1),
        "flag_north": with_ends((jax.random.randint(key_of[5], (NZ, NX, NY), 0, 2) < 1).astype(jnp.int32), jax.random.fold_in(key_of[5], 1), 0, 1),
        "ocean_mask": with_ends((jax.random.randint(key_of[6], (NZ, NX, NY), 0, 10) < 9).astype(jnp.int32), jax.random.fold_in(key_of[6], 1), 0, 1),
    }


time_step = 0.1
horiz_diff = 0.05
vert_diff = 0.2

def cells_at(values, axis_dim, first_face, face_count, offset):
    start_index = first_face + offset + 3
    return lax.slice_in_dim(values, start_index, start_index + face_count, axis=axis_dim)

def face_fluxes(values, openness, pos_speed, neg_speed, axis_dim, first_face, face_count):
    centre = cells_at(values, axis_dim, first_face, face_count, 0)
    upper_one = cells_at(values, axis_dim, first_face, face_count, 1)
    lower_one = cells_at(values, axis_dim, first_face, face_count, -1)
    upper_two = cells_at(values, axis_dim, first_face, face_count, 2)
    left_side = (2.0 * cells_at(values, axis_dim, first_face, face_count, -2) - 13.0 * lower_one + 47.0 * centre + 27.0 * upper_one - 3.0 * upper_two) / 60.0
    right_side = (2.0 * cells_at(values, axis_dim, first_face, face_count, 3) - 13.0 * upper_two + 47.0 * upper_one + 27.0 * centre - 3.0 * lower_one) / 60.0
    return openness * (pos_speed * left_side + neg_speed * right_side - horiz_diff * (upper_one - centre))

def direction_fluxes(channels, pos_speed, neg_speed, axis_dim, first_face, face_count):
    mask_part = channels[-1]
    field_part = channels[:-1]
    openness = cells_at(mask_part, axis_dim - 1, first_face, face_count, 0) * cells_at(mask_part, axis_dim - 1, first_face, face_count, 1)
    return face_fluxes(field_part, openness, pos_speed, neg_speed, axis_dim, first_face, face_count)

def lower_inverse(lower_factor):
    order_size = lower_factor.shape[0]
    identity = jnp.eye(order_size, dtype=lower_factor.dtype)
    rows_out = []
    for row_index in range(order_size):
        partial_value = identity[row_index]
        for col_index in range(row_index):
            partial_value = partial_value - lower_factor[row_index, col_index] * rows_out[col_index]
        rows_out.append(partial_value / lower_factor[row_index, row_index])
    return jnp.stack(rows_out)

def reference(mean_field, mode_fields, velocity_east, velocity_north, flag_east, flag_north, ocean_mask):
    fields = jnp.concatenate([mean_field[None], mode_fields], axis=0)
    wet_cells = ocean_mask.astype(jnp.float32)
    east_flag = flag_east.astype(jnp.float32)
    north_flag = flag_north.astype(jnp.float32)
    pos_east = velocity_east * east_flag
    neg_east = velocity_east * (1.0 - east_flag)
    pos_north = velocity_north * north_flag
    neg_north = velocity_north * (1.0 - north_flag)
    levels = fields.shape[1]
    size_x = fields.shape[2]
    size_y = fields.shape[3]

    def level_tendency(level_index):
        fields_here = lax.dynamic_index_in_dim(fields, level_index, 1, keepdims=False)
        level_above = lax.dynamic_index_in_dim(fields, jnp.minimum(level_index + 1, levels - 1), 1, keepdims=False)
        level_below = lax.dynamic_index_in_dim(fields, jnp.maximum(level_index - 1, 0), 1, keepdims=False)
        planes = [lax.dynamic_index_in_dim(plane, level_index, 0, keepdims=False) for plane in (wet_cells, pos_east, neg_east, pos_north, neg_north)]
        stacked = jnp.concatenate([fields_here] + [plane[None] for plane in planes], axis=0)
        padded = jnp.pad(stacked, ((0, 0), (3, 3), (3, 3)))
        across_x = padded[:, :, 3:-3]
        flux_east = direction_fluxes(across_x[:-4], cells_at(across_x[-4], 0, -1, size_x + 1, 0), cells_at(across_x[-3], 0, -1, size_x + 1, 0), 1, -1, size_x + 1)
        tend_x = flux_east[:, :-1] - flux_east[:, 1:]
        across_y = padded[:, 3:-3, :]
        flux_north = direction_fluxes(across_y[:-4], cells_at(across_y[-2], 1, -1, size_y + 1, 0), cells_at(across_y[-1], 1, -1, size_y + 1, 0), 2, -1, size_y + 1)
        tend_y = flux_north[:, :, :-1] - flux_north[:, :, 1:]
        up_flux = jnp.where(level_index < levels - 1, vert_diff * (level_above - fields_here), 0.0)
        down_flux = jnp.where(level_index > 0, vert_diff * (fields_here - level_below), 0.0)
        return planes[0] * (tend_x + tend_y + (up_flux - down_flux))
    per_level = lax.map(level_tendency, jnp.arange(levels, dtype=jnp.int32))
    tendency = jnp.moveaxis(per_level, 0, 1)
    mean_next = mean_field + time_step * tendency[0]
    mode_count = mode_fields.shape[0]
    flat_modes = mode_fields.reshape(mode_count, -1)
    flat_tend = tendency[1:].reshape(mode_count, -1)
    cell_count = float(flat_modes.shape[1])
    highest = lax.Precision.HIGHEST
    projection = jnp.dot(flat_modes, flat_tend.T, precision=highest) / cell_count
    growth = flat_tend - jnp.dot(projection.T, flat_modes, precision=highest)
    updated = flat_modes + time_step * growth
    gram_matrix = jnp.dot(updated, updated.T, precision=highest) / cell_count
    lower_factor = jnp.linalg.cholesky(gram_matrix)
    inverse = lower_inverse(lower_factor)
    modes_next = jnp.dot(inverse, updated, precision=highest).reshape(mode_fields.shape)
    return (mean_next, modes_next, lower_factor.T)
```

```python
import jax
import jax.numpy as jnp
from jax import lax
from jax.experimental import pallas as pl
from jax.experimental.pallas import tpu as pltpu
from jax.sharding import PartitionSpec as P

time_step = 0.1
horiz_diff = 0.05
vert_diff = 0.2

M = 16
F = 17
NZ = 16
BX = 16
LANES = 128
ROWS = 3 * NZ
ZG = 2
HIGH = lax.Precision.HIGHEST
f32 = jnp.float32
bf16 = jnp.bfloat16

ANY = pl.BlockSpec(memory_space=pl.ANY)
VMEM = pl.BlockSpec(memory_space=pltpu.VMEM)


def params():
    return pltpu.CompilerParams(vmem_limit_bytes=56 * 1024 * 1024)


def cost(flops, nbytes):
    return pl.CostEstimate(flops=flops, bytes_accessed=nbytes, transcendentals=0)


def rolled(value, shift, axis):
    shift = shift % value.shape[axis]
    return value if shift == 0 else pltpu.roll(value, shift, axis)


def lane_ids():
    return lax.broadcasted_iota(jnp.int32, (8, LANES), 1)


def row_ids():
    return lax.broadcasted_iota(jnp.int32, (8, LANES), 0)


def lane_half(ref, half):
    where = (slice(None),) * (len(ref.shape) - 1) + (pl.ds(LANES * half, LANES),)
    return ref.at[where]


def pack_rows(get, first_row):
    rows = row_ids()
    tiles = []
    for out in range(3):
        tile = None
        for z in range(8):
            low, high = max(3 * z, 8 * out), min(3 * z + 3, 8 * out + 8)
            if low >= high:
                continue
            piece = rolled(get(z), 3 * z - 8 * out - first_row, 0)
            tile = piece if tile is None else jnp.where(rows >= low - 8 * out, piece, tile)
        tiles.append(tile)
    return tiles


def pack_columns(get, shift_of):
    slot = lane_ids() // 4
    parts = [jnp.zeros((8, LANES), f32) for _ in range(4)]
    for k in range(2 * NZ):
        moved = rolled(get(k), shift_of(k), 1)
        parts[k % 4] = jnp.where(slot == k, moved, parts[k % 4])
    out = parts[0]
    for k in range(1, 4):
        out = jnp.where(slot % 4 == k, parts[k], out)
    return out


def pack_kernel(modes, mean, vn, fn, mask, up, down, east, west, X, V, I, sems):
    copies = []
    for chunk in range(4):
        for half in range(2):
            copies.append(
                pltpu.make_async_copy(
                    lane_half(modes, half).at[pl.ds(4 * chunk, 4)],
                    X.at[half, pl.ds(4 * chunk, 4)],
                    sems.at[len(copies)],
                )
            )
    for source, target in (
        (mean, lambda half: X.at[half, M]),
        (vn, lambda half: V.at[half]),
        (fn, lambda half: I.at[0, half]),
        (mask, lambda half: I.at[1, half]),
    ):
        for half in range(2):
            copies.append(
                pltpu.make_async_copy(lane_half(source, half), target(half), sems.at[len(copies)])
            )
    for copy in copies:
        copy.start()

    def field(f, carry):
        for half in range(2):
            for zh in range(2):
                for target, tile, first in ((up, 1, 5), (down, 0, 0)):
                    tiles = pack_rows(
                        lambda z: X[half, f, 8 * zh + z, 8 * tile : 8 * tile + 8, :], first
                    )
                    for t in range(3):
                        target[half, f, 24 * zh + 8 * t : 24 * zh + 8 * t + 8, :] = tiles[t]
        def tile_of(half):
            return lambda k: X[half, f, k // 2, 8 * (k % 2) : 8 * (k % 2) + 8, :]
        east[f] = pack_columns(tile_of(1), lambda k: 4 * k - 125)
        west[f] = pack_columns(tile_of(0), lambda k: 4 * k)
        return carry

    for chunk in range(4):
        copies[2 * chunk].wait()
        copies[2 * chunk + 1].wait()
        lax.fori_loop(4 * chunk, 4 * chunk + 4, field, 0)
    for copy in copies[8:]:
        copy.wait()
    lax.fori_loop(M, F, field, 0)
    for index, plane in enumerate(
        (
            lambda half, k: V[half, k // 2, 8 * (k % 2) : 8 * (k % 2) + 8, :],
            lambda half, k: I[0, half, k // 2, 8 * (k % 2) : 8 * (k % 2) + 8, :].astype(f32),
            lambda half, k: I[1, half, k // 2, 8 * (k % 2) : 8 * (k % 2) + 8, :].astype(f32),
        )
    ):
        east[F + index] = pack_columns(lambda k: plane(1, k), lambda k: 4 * k - 125)
        west[F + index] = pack_columns(lambda k: plane(0, k), lambda k: 4 * k)


def pack(modes, mean, vn, fn, mask):
    rows = jax.ShapeDtypeStruct((2, F, ROWS, LANES), f32)
    columns = jax.ShapeDtypeStruct((F + 3, 8, LANES), f32)
    return pl.pallas_call(
        pack_kernel,
        out_shape=(rows, rows, columns, columns),
        in_specs=[ANY] * 5,
        out_specs=(VMEM,) * 4,
        scratch_shapes=[
            pltpu.VMEM((2, F, NZ, BX, LANES), f32),
            pltpu.VMEM((2, NZ, BX, LANES), f32),
            pltpu.VMEM((2, 2, NZ, BX, LANES), jnp.int32),
            pltpu.SemaphoreType.DMA((16,)),
        ],
        compiler_params=params(),
        cost_estimate=cost(10**7, 7 * 10**6),
        name="pack",
    )(modes, mean, vn, fn, mask)


def along_lanes(first, second, outer, offset):
    lanes = lane_ids()
    a, b, c = (rolled(v, -offset, 1) for v in (first, second, outer))
    if offset > 0:
        inside = lanes < LANES - offset
        return jnp.where(inside, a, b), jnp.where(inside, b, c)
    outside = lanes < -offset
    return jnp.where(outside, c, a), jnp.where(outside, a, b)


def cell_weights(a_low, b_low, d_low, a_high, b_high, d_high):
    return (
        2.0 * a_low,
        -13.0 * a_low - 3.0 * b_low - 2.0 * a_high,
        47.0 * a_low + 27.0 * b_low + d_low + 13.0 * a_high + 3.0 * b_high,
        27.0 * a_low + 47.0 * b_low - d_low - 47.0 * a_high - 27.0 * b_high - d_high,
        -3.0 * a_low - 13.0 * b_low - 27.0 * a_high - 47.0 * b_high + d_high,
        2.0 * b_low + 3.0 * a_high + 13.0 * b_high,
        -2.0 * b_high,
    )


def face_parts(openness, speed, flag):
    scaled = openness * speed * (1.0 / 60.0)
    return scaled * flag, scaled * (1.0 - flag), horiz_diff * openness


def split(value):
    high = value.astype(bf16)
    return high, (value - high.astype(f32)).astype(bf16)


def add_products(acc, high, low):
    dims = (((1,), (1,)), ((), ()))
    acc[0:256, :] += lax.dot_general(high, high, dims, preferred_element_type=f32)
    acc[256:512, :] += lax.dot_general(low, high, dims, preferred_element_type=f32)


def field_sums(acc):
    rows = lax.broadcasted_iota(jnp.int32, (512, 256), 0)
    columns = lax.broadcasted_iota(jnp.int32, (512, 256), 1)
    kept = jnp.where(rows % 8 == columns % 8, acc[...], 0.0)
    by_row = jnp.sum(kept.reshape(64, 8, 256), axis=1)
    gather = (
        lax.broadcasted_iota(jnp.int32, (256, 32), 0) // 8
        == lax.broadcasted_iota(jnp.int32, (256, 32), 1)
    ).astype(f32)
    return jnp.dot(by_row, gather, precision=HIGH, preferred_element_type=f32)


def interior_kernel(
    modes, mean, ve, vn, fe, fn, mask, lower, upper, west, east,
    high_out, low_out, edge_out, weights_out, mean_out, sums_out,
    X, VE, FE, W, VN, FN, T, Z, acc, sems,
):
    zero_tile = jnp.zeros((8, LANES), f32)

    def clear(f, carry):
        for half in range(2):
            for z in range(NZ):
                X[half, f, z, 0:8, :] = zero_tile
                X[half, f, z, 24:32, :] = zero_tile
        return carry

    lax.fori_loop(0, F, clear, 0)
    for half in range(2):
        for z in range(NZ):
            lanes = slice(LANES * half, LANES * half + LANES)
            spread = lambda row: jnp.broadcast_to(row, (8, LANES))
            VE[half, z, 0:8, :] = spread(lower[0, z : z + 1, lanes])
            FE[half, z, 0:8, :] = spread(lower[1, z : z + 1, lanes])
            W[half, z, 0:8, :] = spread(lower[2, z : z + 1, lanes]).astype(jnp.int32)
            W[half, z, 24:32, :] = spread(upper[z : z + 1, lanes]).astype(jnp.int32)
    acc[...] = jnp.zeros((512, 256), f32)

    copies = []
    body = pl.ds(8, BX)
    for half in range(2):
        for source, target in (
            (modes, X.at[half, pl.ds(0, M), :, body]),
            (mean, X.at[half, M, :, body]),
            (ve, VE.at[half, :, body]),
            (mask, W.at[half, :, body]),
            (vn, VN.at[half]),
            (fn, FN.at[0, half]),
            (fe, FN.at[1, half]),
        ):
            copies.append(
                pltpu.make_async_copy(lane_half(source, half), target, sems.at[len(copies)])
            )
    for copy in copies:
        copy.start()
    for copy in copies:
        copy.wait()

    lanes = lane_ids()
    rows = row_ids()

    def level(z, carry):
        gain_up = jnp.where(z < NZ - 1, vert_diff, 0.0).astype(f32)
        gain_down = jnp.where(z > 0, vert_diff, 0.0).astype(f32)
        z_up = jnp.minimum(z + 1, NZ - 1)
        z_down = jnp.maximum(z - 1, 0)
        for half in range(2):
            for xt in range(2):
                FE[half, z, 8 + 8 * xt : 16 + 8 * xt, :] = FN[
                    1, half, z, 8 * xt : 8 * xt + 8, :
                ].astype(f32)
        for xt in range(2):
            start = 8 + 8 * xt
            slot = 2 * z + xt
            after_shift = lax.rem(LANES - 4 * slot, LANES)
            before_shift = LANES - 3 - 4 * slot

            def outer(index):
                return jnp.where(
                    lanes < 64,
                    pltpu.roll(east[index], after_shift, 1),
                    pltpu.roll(west[index], before_shift, 1),
                )

            def at(ref, half, offset):
                return ref[half, z, start + offset : start + offset + 8, :]

            wet = [at(W, half, 0).astype(f32) for half in range(2)]
            wx = []
            for half in range(2):
                before = wet[half] * at(W, half, -1).astype(f32)
                after = wet[half] * at(W, half, 1).astype(f32)
                wx.append(
                    cell_weights(
                        *face_parts(before, at(VE, half, -1), at(FE, half, -1)),
                        *face_parts(after, at(VE, half, 0), at(FE, half, 0)),
                    )
                )
            wet_out = outer(F + 2)
            following = along_lanes(wet[0], wet[1], wet_out, 1)
            own = [
                face_parts(
                    wet[half] * following[half],
                    VN[half, z, 8 * xt : 8 * xt + 8, :],
                    FN[0, half, z, 8 * xt : 8 * xt + 8, :].astype(f32),
                )
                for half in range(2)
            ]
            beyond = face_parts(wet_out * rolled(wet[0], -1, 1), outer(F), outer(F + 1))
            before = [along_lanes(own[0][i], own[1][i], beyond[i], -1) for i in range(3)]
            wy = [
                cell_weights(*(before[i][half] for i in range(3)), *own[half]) for half in range(2)
            ]
            centre = [
                wx[half][3] + wy[half][3] - (gain_up + gain_down) * wet[half] for half in range(2)
            ]
            w_up = [gain_up * wet[half] for half in range(2)]
            w_down = [gain_down * wet[half] for half in range(2)]
            for half in range(2):
                for d in range(1, 4):
                    if xt == 0:
                        weights_out[half, z, d - 1] = jnp.where(rows < d, wx[half][3 - d], 0.0)
                    else:
                        weights_out[half, z, d - 1] += jnp.where(
                            rows >= 8 - d, wx[half][3 + d], 0.0
                        )
            for f in range(F):
                own_cells = [X[half, f, z, start : start + 8, :] for half in range(2)]
                total = [
                    centre[half] * own_cells[half]
                    + w_up[half] * X[half, f, z_up, start : start + 8, :]
                    + w_down[half] * X[half, f, z_down, start : start + 8, :]
                    for half in range(2)
                ]
                edge = outer(f)
                for offset in (-3, -2, -1, 1, 2, 3):
                    moved = along_lanes(own_cells[0], own_cells[1], edge, offset)
                    for half in range(2):
                        total[half] += wx[half][3 + offset] * X[
                            half, f, z, start + offset : start + offset + 8, :
                        ]
                        total[half] += wy[half][3 + offset] * moved[half]
                for half in range(2):
                    columns = slice(LANES * half, LANES * half + LANES)
                    if f == M:
                        mean_out[z, 8 * xt : 8 * xt + 8, columns] = (
                            own_cells[half] + time_step * total[half]
                        )
                    elif xt == 0:
                        T[half, f] = total[half]
                    else:
                        near = T[half, f]
                        cells = X[half, f, z, 8:16, :]
                        low_rows = rows < 4
                        Z[8 * f : 8 * f + 8, columns] = jnp.where(
                            low_rows, own_cells[half], cells
                        )
                        Z[128 + 8 * f : 136 + 8 * f, columns] = jnp.where(
                            low_rows, total[half], near
                        )
                        edge_out[z, 8 * f : 8 * f + 8, columns] = jnp.where(
                            low_rows, cells, own_cells[half]
                        )
                        edge_out[z, 128 + 8 * f : 136 + 8 * f, columns] = jnp.where(
                            low_rows, near, total[half]
                        )
        high, low = split(Z[...])
        high_out[z] = high
        low_out[z] = low
        add_products(acc, high, low)
        return carry

    lax.fori_loop(0, NZ, level, 0)
    sums_out[...] = field_sums(acc)


def interior(modes, mean, ve, vn, fe, fn, mask, lower, upper, west, east):
    parts = jax.ShapeDtypeStruct((NZ, 256, 256), bf16)
    return pl.pallas_call(
        interior_kernel,
        out_shape=(
            parts,
            parts,
            jax.ShapeDtypeStruct((NZ, 256, 256), f32),
            jax.ShapeDtypeStruct((2, NZ, 3, 8, LANES), f32),
            jax.ShapeDtypeStruct(mean.shape, f32),
            jax.ShapeDtypeStruct((64, 32), f32),
        ),
        in_specs=[ANY] * 7 + [VMEM] * 4,
        out_specs=(VMEM,) * 6,
        scratch_shapes=[
            pltpu.VMEM((2, F, NZ, 32, LANES), f32),
            pltpu.VMEM((2, NZ, 32, LANES), f32),
            pltpu.VMEM((2, NZ, 32, LANES), f32),
            pltpu.VMEM((2, NZ, 32, LANES), jnp.int32),
            pltpu.VMEM((2, NZ, BX, LANES), f32),
            pltpu.VMEM((2, 2, NZ, BX, LANES), jnp.int32),
            pltpu.VMEM((2, M, 8, LANES), f32),
            pltpu.VMEM((256, 256), f32),
            pltpu.VMEM((512, 256), f32),
            pltpu.SemaphoreType.DMA((14,)),
        ],
        compiler_params=params(),
        cost_estimate=cost(10**10, 4 * 10**7),
        name="interior",
    )(modes, mean, ve, vn, fe, fn, mask, lower, upper, west, east)


def edge_kernel(
    below, above, edge_in, weights, mean_in, sums_in,
    high_out, low_out, mean_out, sums_out, HL, HU, E, acc, sems,
):
    copies = [
        pltpu.make_async_copy(below, HL.at[:, :, pl.ds(0, ROWS)], sems.at[0]),
        pltpu.make_async_copy(above, HU.at[:, :, pl.ds(8, ROWS)], sems.at[1]),
        pltpu.make_async_copy(edge_in, E, sems.at[2]),
    ]
    for half in range(2):
        for f in range(F):
            HL[half, f, ROWS : ROWS + 8, :] = jnp.zeros((8, LANES), f32)
            HU[half, f, 0:8, :] = jnp.zeros((8, LANES), f32)
    for copy in copies:
        copy.start()
    acc[...] = jnp.zeros((512, 256), f32)
    for copy in copies:
        copy.wait()
    low_rows = row_ids() < 4

    def change(f, half, z):
        total = None
        for d in range(1, 4):
            first = 3 * z + 3 - d
            second = 3 * z + d
            cells = jnp.where(
                low_rows, HL[half, f, first : first + 8, :], HU[half, f, second : second + 8, :]
            )
            term = weights[half, z, d - 1] * cells
            total = term if total is None else total + term
        return total

    def mode(f, carry):
        place = pl.ds(pl.multiple_of(128 + 8 * f, 8), 8)
        for half in range(2):
            columns = slice(LANES * half, LANES * half + LANES)
            for z in range(NZ):
                E[z, place, columns] += change(f, half, z)
        return carry

    lax.fori_loop(0, M, mode, 0)
    for half in range(2):
        columns = slice(LANES * half, LANES * half + LANES)
        for z in range(NZ):
            step = time_step * change(M, half, z)
            mean_out[z, 0:8, columns] = mean_in[z, 0:8, columns] + jnp.where(low_rows, step, 0.0)
            mean_out[z, 8:16, columns] = mean_in[z, 8:16, columns] + jnp.where(low_rows, 0.0, step)

    def level(z, carry):
        high, low = split(E[z])
        high_out[z] = high
        low_out[z] = low
        add_products(acc, high, low)
        return carry

    lax.fori_loop(0, NZ, level, 0)
    sums = sums_in[...] + field_sums(acc)
    identity = (
        lax.broadcasted_iota(jnp.int32, (32, 32), 0) == lax.broadcasted_iota(jnp.int32, (32, 32), 1)
    ).astype(f32)
    turned = lax.dot_general(
        identity, sums[32:64], (((1,), (1,)), ((), ())), precision=HIGH, preferred_element_type=f32
    )
    sums_out[...] = sums[0:32] + sums[32:64] + turned


def edges(below, above, edge_in, weights, mean_in, sums_in):
    parts = jax.ShapeDtypeStruct((NZ, 256, 256), bf16)
    return pl.pallas_call(
        edge_kernel,
        out_shape=(
            parts,
            parts,
            jax.ShapeDtypeStruct(mean_in.shape, f32),
            jax.ShapeDtypeStruct((32, 32), f32),
        ),
        in_specs=[ANY] * 3 + [VMEM] * 3,
        out_specs=(VMEM,) * 4,
        scratch_shapes=[
            pltpu.VMEM((2, F, ROWS + 8, LANES), f32),
            pltpu.VMEM((2, F, ROWS + 8, LANES), f32),
            pltpu.VMEM((NZ, 256, 256), f32),
            pltpu.VMEM((512, 256), f32),
            pltpu.SemaphoreType.DMA((3,)),
        ],
        compiler_params=params(),
        cost_estimate=cost(10**9, 10**7),
        name="edges",
    )(below, above, edge_in, weights, mean_in, sums_in)


def factor_and_map(sums, cell_count):
    inner = sums * (1.0 / cell_count)
    row = lax.broadcasted_iota(jnp.int32, (M, 2 * M), 0)
    column = lax.broadcasted_iota(jnp.int32, (M, 2 * M), 1)
    update = jnp.where(
        column < M,
        jnp.where(column == row, 1.0, 0.0) - time_step * inner[M : 2 * M, :],
        jnp.where(column == row + M, time_step, 0.0),
    )
    half_way = jnp.dot(update, inner, precision=HIGH, preferred_element_type=f32)
    gram = lax.dot_general(
        half_way, update, (((1,), (1,)), ((), ())), precision=HIGH, preferred_element_type=f32
    )
    row_g = lax.broadcasted_iota(jnp.int32, (M, M), 0)
    column_g = lax.broadcasted_iota(jnp.int32, (M, M), 1)
    left, right = gram, update
    for j in range(M):
        pivot = jnp.sum(jnp.where(column_g == j, left, 0.0), axis=1, keepdims=True)
        scale = 1.0 / jnp.sqrt(pivot[j : j + 1, :])
        left_row = left[j : j + 1, :] * scale
        right_row = right[j : j + 1, :] * scale
        share = jnp.where(row_g[:, 0:1] > j, pivot * scale, 0.0)
        left = jnp.where(row_g == j, left_row, left - share * left_row)
        right = jnp.where(row == j, right_row, right - share * right_row)
    return jnp.where(column_g >= row_g, left, 0.0), right


def spread_map(part):
    tall = (
        lax.broadcasted_iota(jnp.int32, (8 * M, M), 0) // 8
        == lax.broadcasted_iota(jnp.int32, (8 * M, M), 1)
    ).astype(bf16)
    wide = (
        lax.broadcasted_iota(jnp.int32, (2 * M, 256), 1) // 8
        == lax.broadcasted_iota(jnp.int32, (2 * M, 256), 0)
    ).astype(bf16)
    rows = jnp.dot(tall, part, preferred_element_type=f32).astype(bf16)
    full = jnp.dot(rows, wide, preferred_element_type=f32)
    row = lax.broadcasted_iota(jnp.int32, (8 * M, 256), 0)
    column = lax.broadcasted_iota(jnp.int32, (8 * M, 256), 1)
    return jnp.where(row % 8 == column % 8, full, 0.0).astype(bf16)


def make_apply_kernel(cell_count):
    def apply_kernel(sums, high_i, low_i, high_e, low_e, out, factor_out, maps):
        @pl.when(pl.program_id(0) == 0)
        def _():
            factor, mapping = factor_and_map(sums[...], cell_count)
            factor_out[...] = factor
            high, low = split(mapping)
            maps[0:128, :] = spread_map(high)
            maps[128:256, :] = spread_map(low)

        low_rows = lax.broadcasted_iota(jnp.int32, (M, 8, 256), 1) < 4
        for z in range(ZG):
            results = []
            for high, low in ((high_i, low_i), (high_e, low_e)):
                first = jnp.dot(maps[...], high[z], preferred_element_type=f32)
                second = jnp.dot(maps[0:128, :], low[z], preferred_element_type=f32)
                results.append((first[0:128] + first[128:256] + second).reshape(M, 8, 256))
            inner, edge = results
            out[:, z, 0:8, :] = jnp.where(low_rows, edge, inner)
            out[:, z, 8:16, :] = jnp.where(low_rows, inner, edge)

    return apply_kernel


def apply_map(sums, high_i, low_i, high_e, low_e, cell_count):
    block = pl.BlockSpec((ZG, 256, 256), lambda i: (i, 0, 0))
    return pl.pallas_call(
        make_apply_kernel(cell_count),
        grid=(NZ // ZG,),
        out_shape=(
            jax.ShapeDtypeStruct((M, NZ, BX, 256), f32),
            jax.ShapeDtypeStruct((M, M), f32),
        ),
        in_specs=[pl.BlockSpec((32, 32), lambda i: (0, 0)), block, block, block, block],
        out_specs=(
            pl.BlockSpec((M, ZG, BX, 256), lambda i: (0, i, 0, 0)),
            pl.BlockSpec((M, M), lambda i: (0, 0)),
        ),
        scratch_shapes=[pltpu.VMEM((256, 256), bf16)],
        compiler_params=params(),
        cost_estimate=cost(10**9, 13 * 10**6),
        name="apply",
    )(sums, high_i, low_i, high_e, low_e)


def onward(value, axis):
    size = lax.axis_size(axis)
    return lax.ppermute(value, axis, [(i, i + 1) for i in range(size - 1)])


def backward(value, axis):
    size = lax.axis_size(axis)
    return lax.ppermute(value, axis, [(i + 1, i) for i in range(size - 1)])


def exchanged(value, axes, distance):
    size = lax.axis_size(axes)
    return lax.ppermute(value, axes, [(i, i ^ distance) for i in range(size)])


def shards(
    mean_field, mode_fields, velocity_east, velocity_north, flag_east, flag_north, ocean_mask
):
    axes = ("gx", "gy")
    last = BX - 1
    lower_send = jnp.stack(
        [
            velocity_east[:, last],
            flag_east[:, last].astype(f32),
            ocean_mask[:, last].astype(f32),
        ]
    )
    lower = onward(lower_send, "gx")
    upper = backward(ocean_mask[:, 0].astype(f32), "gx")
    up, down, east_send, west_send = pack(
        mode_fields, mean_field, velocity_north, flag_north, ocean_mask
    )
    below = onward(up, "gx")
    above = backward(down, "gx")
    west = onward(east_send, "gy")
    east = backward(west_send, "gy")
    high_i, low_i, edge, weights, mean_part, sums_i = interior(
        mode_fields, mean_field, velocity_east, velocity_north, flag_east, flag_north,
        ocean_mask, lower, upper, west, east,
    )
    high_e, low_e, mean_next, sums = edges(below, above, edge, weights, mean_part, sums_i)
    for distance in (1, 2, 6, 8, 24, 32, 96):
        sums = sums + exchanged(sums, axes, distance)
    cell_count = float(NZ * BX * 256 * lax.axis_size("gx") * lax.axis_size("gy"))
    modes_next, factor = apply_map(sums, high_i, low_i, high_e, low_e, cell_count)
    return (mean_next, modes_next, factor)


def solution(mesh):
    plane = P(None, "gx", "gy")
    return jax.shard_map(
        shards,
        mesh=mesh,
        in_specs=(plane, P(None, None, "gx", "gy"), plane, plane, plane, plane, plane),
        out_specs=(plane, P(None, None, "gx", "gy"), P()),
        check_vma=False,
    )
```

```python
import jax
import jax.numpy as jnp
from jax import lax
from jax.experimental import pallas as pl
from jax.experimental.pallas import tpu as pltpu
from jax.sharding import PartitionSpec as P

time_step = 0.1
horiz_diff = 0.05
vert_diff = 0.2

M = 16
F = 17
NZ = 16
BX = 16
LANES = 128
ROWS = 3 * NZ
SLOTS = 4
HIGH = lax.Precision.HIGHEST
f32 = jnp.float32
bf16 = jnp.bfloat16

ANY = pl.BlockSpec(memory_space=pl.ANY)
VMEM = pl.BlockSpec(memory_space=pltpu.VMEM)


def params(mib):
    return pltpu.CompilerParams(vmem_limit_bytes=mib * 1024 * 1024)


def cost(flops, nbytes):
    return pl.CostEstimate(flops=flops, bytes_accessed=nbytes, transcendentals=0)


def rolled(value, shift, axis):
    shift = shift % value.shape[axis]
    return value if shift == 0 else pltpu.roll(value, shift, axis)


def lane_ids():
    return lax.broadcasted_iota(jnp.int32, (8, LANES), 1)


def row_ids():
    return lax.broadcasted_iota(jnp.int32, (8, LANES), 0)


def lane_half(ref, half):
    where = (slice(None),) * (len(ref.shape) - 1) + (pl.ds(LANES * half, LANES),)
    return ref.at[where]


def pack_rows(get, first_row):
    rows = row_ids()
    tiles = []
    for out in range(3):
        tile = None
        for z in range(8):
            low, high = max(3 * z, 8 * out), min(3 * z + 3, 8 * out + 8)
            if low >= high:
                continue
            piece = rolled(get(z), 3 * z - 8 * out - first_row, 0)
            tile = piece if tile is None else jnp.where(rows >= low - 8 * out, piece, tile)
        tiles.append(tile)
    return tiles


def pack_columns(get, shift_of):
    slot = lane_ids() // 4
    parts = [jnp.zeros((8, LANES), f32) for _ in range(4)]
    for k in range(2 * NZ):
        moved = rolled(get(k), shift_of(k), 1)
        parts[k % 4] = jnp.where(slot == k, moved, parts[k % 4])
    out = parts[0]
    for k in range(1, 4):
        out = jnp.where(slot % 4 == k, parts[k], out)
    return out


def pack_kernel(
    modes, mean, ve, vn, fe, fn, mask, up, down, east, west, lower, upper, X, V, I, sems
):
    copies = []
    for chunk in range(4):
        for half in range(2):
            copies.append(
                pltpu.make_async_copy(
                    lane_half(modes, half).at[pl.ds(4 * chunk, 4)],
                    X.at[half, pl.ds(4 * chunk, 4)],
                    sems.at[len(copies)],
                )
            )
    for source, target in (
        (mean, lambda half: X.at[half, M]),
        (vn, lambda half: V.at[0, half]),
        (ve, lambda half: V.at[1, half]),
        (fn, lambda half: I.at[0, half]),
        (mask, lambda half: I.at[1, half]),
        (fe, lambda half: I.at[2, half]),
    ):
        for half in range(2):
            copies.append(
                pltpu.make_async_copy(lane_half(source, half), target(half), sems.at[len(copies)])
            )
    for copy in copies:
        copy.start()

    def field(f, carry):
        for half in range(2):
            for zh in range(2):
                for target, tile, first in ((up, 1, 5), (down, 0, 0)):
                    tiles = pack_rows(
                        lambda z: X[half, f, 8 * zh + z, 8 * tile : 8 * tile + 8, :], first
                    )
                    for t in range(3):
                        target[half, f, zh, 8 * t : 8 * t + 8, :] = tiles[t]
        def tile_of(half):
            return lambda k: X[half, f, k // 2, 8 * (k % 2) : 8 * (k % 2) + 8, :]
        east[f] = pack_columns(tile_of(1), lambda k: 4 * k - 125)
        west[f] = pack_columns(tile_of(0), lambda k: 4 * k)
        return carry

    for chunk in range(4):
        copies[2 * chunk].wait()
        copies[2 * chunk + 1].wait()
        lax.fori_loop(4 * chunk, 4 * chunk + 4, field, 0)
    for copy in copies[8:]:
        copy.wait()
    lax.fori_loop(M, F, field, 0)
    for index, plane in enumerate(
        (
            lambda half, k: V[0, half, k // 2, 8 * (k % 2) : 8 * (k % 2) + 8, :],
            lambda half, k: I[0, half, k // 2, 8 * (k % 2) : 8 * (k % 2) + 8, :].astype(f32),
            lambda half, k: I[1, half, k // 2, 8 * (k % 2) : 8 * (k % 2) + 8, :].astype(f32),
        )
    ):
        east[F + index] = pack_columns(lambda k: plane(1, k), lambda k: 4 * k - 125)
        west[F + index] = pack_columns(lambda k: plane(0, k), lambda k: 4 * k)
    rows = row_ids()
    for half in range(2):
        for zh in range(2):
            tiles = [jnp.zeros((8, LANES), f32) for _ in range(4)]
            for z in range(8):
                level = 8 * zh + z
                sources = (
                    rolled(V[1, half, level, 8:16, :], z - 7, 0),
                    rolled(I[2, half, level, 8:16, :].astype(f32), z - 7, 0),
                    rolled(I[1, half, level, 8:16, :].astype(f32), z - 7, 0),
                    rolled(I[1, half, level, 0:8, :].astype(f32), z, 0),
                )
                tiles = [jnp.where(rows == z, new, old) for new, old in zip(sources, tiles)]
            place = slice(8 * zh, 8 * zh + 8), slice(LANES * half, LANES * half + LANES)
            for index in range(3):
                lower[index, place[0], place[1]] = tiles[index]
            upper[place[0], place[1]] = tiles[3]


def pack(modes, mean, ve, vn, fe, fn, mask):
    rows = jax.ShapeDtypeStruct((2, F, 2, ROWS // 2, LANES), f32)
    columns = jax.ShapeDtypeStruct((F + 3, 8, LANES), f32)
    return pl.pallas_call(
        pack_kernel,
        out_shape=(
            rows,
            rows,
            columns,
            columns,
            jax.ShapeDtypeStruct((3, NZ, 2 * LANES), f32),
            jax.ShapeDtypeStruct((NZ, 2 * LANES), f32),
        ),
        in_specs=[ANY] * 7,
        out_specs=(VMEM,) * 6,
        scratch_shapes=[
            pltpu.VMEM((2, F, NZ, BX, LANES), f32),
            pltpu.VMEM((2, 2, NZ, BX, LANES), f32),
            pltpu.VMEM((3, 2, NZ, BX, LANES), jnp.int32),
            pltpu.SemaphoreType.DMA((20,)),
        ],
        compiler_params=params(12),
        cost_estimate=cost(10**7, 7 * 10**6),
        name="pack",
    )(modes, mean, ve, vn, fe, fn, mask)


def along_lanes(first, second, outer, offset):
    lanes = lane_ids()
    a, b, c = (rolled(v, -offset, 1) for v in (first, second, outer))
    if offset > 0:
        inside = lanes < LANES - offset
        return jnp.where(inside, a, b), jnp.where(inside, b, c)
    outside = lanes < -offset
    return jnp.where(outside, c, a), jnp.where(outside, a, b)


def cell_weights(a_low, b_low, d_low, a_high, b_high, d_high):
    return (
        2.0 * a_low,
        -13.0 * a_low - 3.0 * b_low - 2.0 * a_high,
        47.0 * a_low + 27.0 * b_low + d_low + 13.0 * a_high + 3.0 * b_high,
        27.0 * a_low + 47.0 * b_low - d_low - 47.0 * a_high - 27.0 * b_high - d_high,
        -3.0 * a_low - 13.0 * b_low - 27.0 * a_high - 47.0 * b_high + d_high,
        2.0 * b_low + 3.0 * a_high + 13.0 * b_high,
        -2.0 * b_high,
    )


def face_parts(openness, speed, flag):
    scaled = openness * speed * (1.0 / 60.0)
    return scaled * flag, scaled * (1.0 - flag), horiz_diff * openness


def split(value):
    high = value.astype(bf16)
    return high, (value - high.astype(f32)).astype(bf16)


def add_products(acc, high, low):
    dims = (((1,), (1,)), ((), ()))
    acc[0:256, :] += lax.dot_general(high, high, dims, preferred_element_type=f32)
    acc[256:512, :] += lax.dot_general(low, high, dims, preferred_element_type=f32)


def field_sums(acc):
    rows = lax.broadcasted_iota(jnp.int32, (512, 256), 0)
    columns = lax.broadcasted_iota(jnp.int32, (512, 256), 1)
    kept = jnp.where(rows % 8 == columns % 8, acc[...], 0.0)
    by_row = jnp.sum(kept.reshape(64, 8, 256), axis=1)
    gather = (
        lax.broadcasted_iota(jnp.int32, (256, 32), 0) // 8
        == lax.broadcasted_iota(jnp.int32, (256, 32), 1)
    ).astype(f32)
    return jnp.dot(by_row, gather, precision=HIGH, preferred_element_type=f32)


def interior_kernel(
    modes, mean, ve, vn, fe, fn, mask, lower, upper, west, east,
    high_out, low_out, edge_out, weights_out, mean_out, sums_out,
    X, VE, FE, W, VN, FN, H, T, Z, acc, sems,
):
    zero_tile = jnp.zeros((8, LANES), f32)

    def clear(f, carry):
        for half in range(2):
            for z in range(NZ):
                X[half, f, z, 0:8, :] = zero_tile
                X[half, f, z, 24:32, :] = zero_tile
        return carry

    lax.fori_loop(0, F, clear, 0)
    for half in range(2):
        for z in range(NZ):
            lanes = slice(LANES * half, LANES * half + LANES)
            spread = lambda row: jnp.broadcast_to(row, (8, LANES))
            VE[half, z, 0:8, :] = spread(lower[0, z : z + 1, lanes])
            FE[half, z, 0:8, :] = spread(lower[1, z : z + 1, lanes])
            W[half, z, 0:8, :] = spread(lower[2, z : z + 1, lanes]).astype(jnp.int32)
            W[half, z, 24:32, :] = spread(upper[z : z + 1, lanes]).astype(jnp.int32)
    acc[...] = jnp.zeros((512, 256), f32)
    lanes = lane_ids()
    rows = row_ids()

    copies = []
    body = pl.ds(8, BX)
    for half in range(2):
        for source, target in (
            (modes, X.at[half, pl.ds(0, M), :, body]),
            (mean, X.at[half, M, :, body]),
            (ve, VE.at[half, :, body]),
            (mask, W.at[half, :, body]),
            (vn, VN.at[half]),
            (fn, FN.at[0, half]),
            (fe, FN.at[1, half]),
        ):
            copies.append(
                pltpu.make_async_copy(lane_half(source, half), target, sems.at[len(copies)])
            )
    for copy in copies:
        copy.start()

    def beside(f, carry):
        after, before = east[f], west[f]
        for k in range(2 * NZ):
            H[f, k] = jnp.where(
                lanes < 64, rolled(after, -4 * k, 1), rolled(before, LANES - 3 - 4 * k, 1)
            )
        return carry

    lax.fori_loop(0, F + 3, beside, 0)
    for copy in copies:
        copy.wait()

    def level(z, carry):
        gain_up = jnp.where(z < NZ - 1, vert_diff, 0.0).astype(f32)
        gain_down = jnp.where(z > 0, vert_diff, 0.0).astype(f32)
        z_up = jnp.minimum(z + 1, NZ - 1)
        z_down = jnp.maximum(z - 1, 0)
        for half in range(2):
            for xt in range(2):
                FE[half, z, 8 + 8 * xt : 16 + 8 * xt, :] = FN[
                    1, half, z, 8 * xt : 8 * xt + 8, :
                ].astype(f32)
        for xt in range(2):
            start = 8 + 8 * xt

            def outer(index):
                return H[index, 2 * z + xt]

            def at(ref, half, offset):
                return ref[half, z, start + offset : start + offset + 8, :]

            wet = [at(W, half, 0).astype(f32) for half in range(2)]
            wx = []
            for half in range(2):
                before = wet[half] * at(W, half, -1).astype(f32)
                after = wet[half] * at(W, half, 1).astype(f32)
                wx.append(
                    cell_weights(
                        *face_parts(before, at(VE, half, -1), at(FE, half, -1)),
                        *face_parts(after, at(VE, half, 0), at(FE, half, 0)),
                    )
                )
            wet_out = outer(F + 2)
            following = along_lanes(wet[0], wet[1], wet_out, 1)
            own = [
                face_parts(
                    wet[half] * following[half],
                    VN[half, z, 8 * xt : 8 * xt + 8, :],
                    FN[0, half, z, 8 * xt : 8 * xt + 8, :].astype(f32),
                )
                for half in range(2)
            ]
            beyond = face_parts(wet_out * rolled(wet[0], -1, 1), outer(F), outer(F + 1))
            before = [along_lanes(own[0][i], own[1][i], beyond[i], -1) for i in range(3)]
            wy = [
                cell_weights(*(before[i][half] for i in range(3)), *own[half]) for half in range(2)
            ]
            centre = [
                wx[half][3] + wy[half][3] - (gain_up + gain_down) * wet[half] for half in range(2)
            ]
            w_up = [gain_up * wet[half] for half in range(2)]
            w_down = [gain_down * wet[half] for half in range(2)]
            for half in range(2):
                for d in range(1, 4):
                    if xt == 0:
                        weights_out[half, z, d - 1] = jnp.where(rows < d, wx[half][3 - d], 0.0)
                    else:
                        weights_out[half, z, d - 1] += jnp.where(
                            rows >= 8 - d, wx[half][3 + d], 0.0
                        )
            for f in range(F):
                own_cells = [X[half, f, z, start : start + 8, :] for half in range(2)]
                total = [
                    centre[half] * own_cells[half]
                    + w_up[half] * X[half, f, z_up, start : start + 8, :]
                    + w_down[half] * X[half, f, z_down, start : start + 8, :]
                    for half in range(2)
                ]
                edge = outer(f)
                for offset in (-3, -2, -1, 1, 2, 3):
                    moved = along_lanes(own_cells[0], own_cells[1], edge, offset)
                    for half in range(2):
                        total[half] += wx[half][3 + offset] * X[
                            half, f, z, start + offset : start + offset + 8, :
                        ]
                        total[half] += wy[half][3 + offset] * moved[half]
                for half in range(2):
                    columns = slice(LANES * half, LANES * half + LANES)
                    if f == M:
                        mean_out[z, 8 * xt : 8 * xt + 8, columns] = (
                            own_cells[half] + time_step * total[half]
                        )
                    elif xt == 0:
                        T[half, f] = total[half]
                    else:
                        near = T[half, f]
                        cells = X[half, f, z, 8:16, :]
                        low_rows = rows < 4
                        Z[8 * f : 8 * f + 8, columns] = jnp.where(
                            low_rows, own_cells[half], cells
                        )
                        Z[128 + 8 * f : 136 + 8 * f, columns] = jnp.where(
                            low_rows, total[half], near
                        )
                        edge_out[z, 8 * f : 8 * f + 8, columns] = jnp.where(
                            low_rows, cells, own_cells[half]
                        )
                        edge_out[z, 128 + 8 * f : 136 + 8 * f, columns] = jnp.where(
                            low_rows, near, total[half]
                        )
        high, low = split(Z[...])
        high_out[z] = high
        low_out[z] = low
        add_products(acc, high, low)
        return carry

    lax.fori_loop(0, NZ, level, 0)
    sums_out[...] = field_sums(acc)


def interior(modes, mean, ve, vn, fe, fn, mask, lower, upper, west, east):
    parts = jax.ShapeDtypeStruct((NZ, 256, 256), bf16)
    return pl.pallas_call(
        interior_kernel,
        out_shape=(
            parts,
            parts,
            jax.ShapeDtypeStruct((NZ, 256, 256), f32),
            jax.ShapeDtypeStruct((2, NZ, 3, 8, LANES), f32),
            jax.ShapeDtypeStruct(mean.shape, f32),
            jax.ShapeDtypeStruct((64, 32), f32),
        ),
        in_specs=[ANY] * 7 + [VMEM] * 4,
        out_specs=(VMEM,) * 6,
        scratch_shapes=[
            pltpu.VMEM((2, F, NZ, 32, LANES), f32),
            pltpu.VMEM((2, NZ, 32, LANES), f32),
            pltpu.VMEM((2, NZ, 32, LANES), f32),
            pltpu.VMEM((2, NZ, 32, LANES), jnp.int32),
            pltpu.VMEM((2, NZ, BX, LANES), f32),
            pltpu.VMEM((2, 2, NZ, BX, LANES), jnp.int32),
            pltpu.VMEM((F + 3, 2 * NZ, 8, LANES), f32),
            pltpu.VMEM((2, M, 8, LANES), f32),
            pltpu.VMEM((256, 256), f32),
            pltpu.VMEM((512, 256), f32),
            pltpu.SemaphoreType.DMA((14,)),
        ],
        compiler_params=params(28),
        cost_estimate=cost(10**6, 10**6),
        name="interior",
    )(modes, mean, ve, vn, fe, fn, mask, lower, upper, west, east)


def edge_kernel(
    below, above, edge_in, weights, mean_in, sums_in,
    high_out, low_out, mean_out, sums_out, Z, acc,
):
    acc[...] = jnp.zeros((512, 256), f32)
    low_rows = row_ids() < 4

    def rows_from(ref, half, f, zh, first):
        start = min(max(first, 0), 16)
        return rolled(ref[half, f, zh, start : start + 8, :], start - first, 0)

    def group(zh, carry):
        for zi in range(8):
            z = 8 * zh + zi
            for half in range(2):
                columns = slice(LANES * half, LANES * half + LANES)
                gains = [weights[half, z, d - 1] for d in range(1, 4)]
                for f in range(F):
                    change = None
                    for d in range(1, 4):
                        cells = jnp.where(
                            low_rows,
                            rows_from(below, half, f, zh, 3 * zi + 3 - d),
                            rows_from(above, half, f, zh, 3 * zi + d - 8),
                        )
                        term = gains[d - 1] * cells
                        change = term if change is None else change + term
                    if f < M:
                        place = slice(8 * f, 8 * f + 8)
                        Z[place, columns] = edge_in[z, 128 + 8 * f : 136 + 8 * f, columns] + change
                    else:
                        step = time_step * change
                        mean_out[z, 0:8, columns] = mean_in[z, 0:8, columns] + jnp.where(
                            low_rows, step, 0.0
                        )
                        mean_out[z, 8:16, columns] = mean_in[z, 8:16, columns] + jnp.where(
                            low_rows, 0.0, step
                        )
            high, low = split(jnp.concatenate([edge_in[z, 0:128, :], Z[...]], axis=0))
            high_out[z] = high
            low_out[z] = low
            add_products(acc, high, low)
        return carry

    lax.fori_loop(0, 2, group, 0)
    sums = sums_in[...] + field_sums(acc)
    identity = (
        lax.broadcasted_iota(jnp.int32, (32, 32), 0) == lax.broadcasted_iota(jnp.int32, (32, 32), 1)
    ).astype(f32)
    turned = lax.dot_general(
        identity, sums[32:64], (((1,), (1,)), ((), ())), precision=HIGH, preferred_element_type=f32
    )
    sums_out[...] = sums[0:32] + sums[32:64] + turned


def edges(below, above, edge_in, weights, mean_in, sums_in):
    parts = jax.ShapeDtypeStruct((NZ, 256, 256), bf16)
    return pl.pallas_call(
        edge_kernel,
        out_shape=(
            parts,
            parts,
            jax.ShapeDtypeStruct(mean_in.shape, f32),
            jax.ShapeDtypeStruct((32, 32), f32),
        ),
        in_specs=[VMEM] * 6,
        out_specs=(VMEM,) * 4,
        scratch_shapes=[
            pltpu.VMEM((128, 256), f32),
            pltpu.VMEM((512, 256), f32),
        ],
        compiler_params=params(16),
        cost_estimate=cost(10**9, 10**7),
        name="edges",
    )(below, above, edge_in, weights, mean_in, sums_in)


def factor_and_map(sums, cell_count):
    inner = sums * (1.0 / cell_count)
    row = lax.broadcasted_iota(jnp.int32, (M, 2 * M), 0)
    column = lax.broadcasted_iota(jnp.int32, (M, 2 * M), 1)
    update = jnp.where(
        column < M,
        jnp.where(column == row, 1.0, 0.0) - time_step * inner[M : 2 * M, :],
        jnp.where(column == row + M, time_step, 0.0),
    )
    half_way = jnp.dot(update, inner, precision=HIGH, preferred_element_type=f32)
    gram = lax.dot_general(
        half_way, update, (((1,), (1,)), ((), ())), precision=HIGH, preferred_element_type=f32
    )
    row_g = lax.broadcasted_iota(jnp.int32, (M, M), 0)
    column_g = lax.broadcasted_iota(jnp.int32, (M, M), 1)
    left, right = gram, update
    for j in range(M):
        pivot = jnp.sum(jnp.where(column_g == j, left, 0.0), axis=1, keepdims=True)
        scale = 1.0 / jnp.sqrt(pivot[j : j + 1, :])
        left_row = left[j : j + 1, :] * scale
        right_row = right[j : j + 1, :] * scale
        share = jnp.where(row_g[:, 0:1] > j, pivot * scale, 0.0)
        left = jnp.where(row_g == j, left_row, left - share * left_row)
        right = jnp.where(row == j, right_row, right - share * right_row)
    return jnp.where(column_g >= row_g, left, 0.0), right


def spread_map(part):
    tall = (
        lax.broadcasted_iota(jnp.int32, (8 * M, M), 0) // 8
        == lax.broadcasted_iota(jnp.int32, (8 * M, M), 1)
    ).astype(bf16)
    wide = (
        lax.broadcasted_iota(jnp.int32, (2 * M, 256), 1) // 8
        == lax.broadcasted_iota(jnp.int32, (2 * M, 256), 0)
    ).astype(bf16)
    rows = jnp.dot(tall, part, preferred_element_type=f32).astype(bf16)
    full = jnp.dot(rows, wide, preferred_element_type=f32)
    row = lax.broadcasted_iota(jnp.int32, (8 * M, 256), 0)
    column = lax.broadcasted_iota(jnp.int32, (8 * M, 256), 1)
    return jnp.where(row % 8 == column % 8, full, 0.0).astype(bf16)


def make_apply_kernel(cell_count):
    def apply_kernel(sums, high_i, low_i, high_e, low_e, out, factor_out, maps, new, sems):
        factor, mapping = factor_and_map(sums[...], cell_count)
        factor_out[...] = factor
        high, low = split(mapping)
        maps[0:128, :] = spread_map(high)
        maps[128:256, :] = spread_map(low)
        low_rows = lax.broadcasted_iota(jnp.int32, (M, 8, 256), 1) < 4

        def put(z, slot):
            return pltpu.make_async_copy(new.at[slot], out.at[:, z], sems.at[slot])

        def level(z, carry):
            slot = lax.rem(z, SLOTS)

            @pl.when(z >= SLOTS)
            def _():
                put(z - SLOTS, slot).wait()

            results = []
            for high, low in ((high_i, low_i), (high_e, low_e)):
                first = jnp.dot(maps[...], high[z], preferred_element_type=f32)
                second = jnp.dot(maps[0:128, :], low[z], preferred_element_type=f32)
                results.append((first[0:128] + first[128:256] + second).reshape(M, 8, 256))
            inner, edge = results
            new[slot, :, 0:8, :] = jnp.where(low_rows, edge, inner)
            new[slot, :, 8:16, :] = jnp.where(low_rows, inner, edge)
            put(z, slot).start()
            return carry

        lax.fori_loop(0, NZ, level, 0)
        for z in range(NZ - SLOTS, NZ):
            put(z, z % SLOTS).wait()

    return apply_kernel


def apply_map(sums, high_i, low_i, high_e, low_e, cell_count):
    return pl.pallas_call(
        make_apply_kernel(cell_count),
        out_shape=(
            jax.ShapeDtypeStruct((M, NZ, BX, 256), f32),
            jax.ShapeDtypeStruct((M, M), f32),
        ),
        in_specs=[VMEM] * 5,
        out_specs=(ANY, VMEM),
        scratch_shapes=[
            pltpu.VMEM((256, 256), bf16),
            pltpu.VMEM((SLOTS, M, BX, 256), f32),
            pltpu.SemaphoreType.DMA((SLOTS,)),
        ],
        compiler_params=params(12),
        cost_estimate=cost(10**9, 13 * 10**6),
        name="apply",
    )(sums, high_i, low_i, high_e, low_e)


def onward(value, axis):
    size = lax.axis_size(axis)
    return lax.ppermute(value, axis, [(i, i + 1) for i in range(size - 1)])


def backward(value, axis):
    size = lax.axis_size(axis)
    return lax.ppermute(value, axis, [(i + 1, i) for i in range(size - 1)])


def exchanged(value, axes, distance):
    size = lax.axis_size(axes)
    return lax.ppermute(value, axes, [(i, i ^ distance) for i in range(size)])


def shards(
    mean_field, mode_fields, velocity_east, velocity_north, flag_east, flag_north, ocean_mask
):
    axes = ("gx", "gy")
    up, down, east_send, west_send, lower_send, upper_send = pack(
        mode_fields, mean_field, velocity_east, velocity_north, flag_east, flag_north, ocean_mask
    )
    below = onward(up, "gx")
    above = backward(down, "gx")
    lower = onward(lower_send, "gx")
    upper = backward(upper_send, "gx")
    west = onward(east_send, "gy")
    east = backward(west_send, "gy")
    high_i, low_i, edge, weights, mean_part, sums_i = interior(
        mode_fields, mean_field, velocity_east, velocity_north, flag_east, flag_north,
        ocean_mask, lower, upper, west, east,
    )
    high_e, low_e, mean_next, sums = edges(below, above, edge, weights, mean_part, sums_i)
    for distance in (1, 2, 6, 8, 24, 32, 96):
        sums = sums + exchanged(sums, axes, distance)
    cell_count = float(NZ * BX * 256 * lax.axis_size("gx") * lax.axis_size("gy"))
    modes_next, factor = apply_map(sums, high_i, low_i, high_e, low_e, cell_count)
    return (mean_next, modes_next, factor)


def solution(mesh):
    plane = P(None, "gx", "gy")
    return jax.shard_map(
        shards,
        mesh=mesh,
        in_specs=(plane, P(None, None, "gx", "gy"), plane, plane, plane, plane, plane),
        out_specs=(plane, P(None, None, "gx", "gy"), P()),
        check_vma=False,
    )
```

```python
import jax
import jax.numpy as jnp
from jax import lax
from jax.experimental import pallas as pl
from jax.experimental.pallas import tpu as pltpu
from jax.sharding import PartitionSpec as P

time_step = 0.1
horiz_diff = 0.05
vert_diff = 0.2

M = 16
F = 17
NZ = 16
BX = 16
LANES = 128
ROWS = 3 * NZ
SLOTS = 4
TAIL = 8 + 8 * F
HIGH = lax.Precision.HIGHEST
f32 = jnp.float32
bf16 = jnp.bfloat16

ANY = pl.BlockSpec(memory_space=pl.ANY)
VMEM = pl.BlockSpec(memory_space=pltpu.VMEM)


def params(mib):
    return pltpu.CompilerParams(vmem_limit_bytes=mib * 1024 * 1024)


def cost(flops, nbytes):
    return pl.CostEstimate(flops=flops, bytes_accessed=nbytes, transcendentals=0)


def rolled(value, shift, axis):
    shift = shift % value.shape[axis]
    return value if shift == 0 else pltpu.roll(value, shift, axis)


def lane_ids():
    return lax.broadcasted_iota(jnp.int32, (8, LANES), 1)


def row_ids():
    return lax.broadcasted_iota(jnp.int32, (8, LANES), 0)


def lane_half(ref, half):
    where = (slice(None),) * (len(ref.shape) - 1) + (pl.ds(LANES * half, LANES),)
    return ref.at[where]


def pack_rows(get, first_row):
    rows = row_ids()
    tiles = []
    for out in range(3):
        tile = None
        for z in range(8):
            low, high = max(3 * z, 8 * out), min(3 * z + 3, 8 * out + 8)
            if low >= high:
                continue
            piece = rolled(get(z), 3 * z - 8 * out - first_row, 0)
            tile = piece if tile is None else jnp.where(rows >= low - 8 * out, piece, tile)
        tiles.append(tile)
    return tiles


def pack_columns(get, shift_of):
    slot = lane_ids() // 4
    parts = [jnp.zeros((8, LANES), f32) for _ in range(4)]
    for k in range(2 * NZ):
        moved = rolled(get(k), shift_of(k), 1)
        parts[k % 4] = jnp.where(slot == k, moved, parts[k % 4])
    out = parts[0]
    for k in range(1, 4):
        out = jnp.where(slot % 4 == k, parts[k], out)
    return out


def pack_kernel(
    modes, mean, ve, vn, fe, fn, mask, up, down, east, west, X, V, I, sems
):
    copies = []
    for chunk in range(4):
        for half in range(2):
            copies.append(
                pltpu.make_async_copy(
                    lane_half(modes, half).at[pl.ds(4 * chunk, 4)],
                    X.at[half, pl.ds(4 * chunk, 4)],
                    sems.at[len(copies)],
                )
            )
    for source, target in (
        (mean, lambda half: X.at[half, M]),
        (vn, lambda half: V.at[0, half]),
        (ve, lambda half: V.at[1, half]),
        (fn, lambda half: I.at[0, half]),
        (mask, lambda half: I.at[1, half]),
        (fe, lambda half: I.at[2, half]),
    ):
        for half in range(2):
            copies.append(
                pltpu.make_async_copy(lane_half(source, half), target(half), sems.at[len(copies)])
            )
    for copy in copies:
        copy.start()

    def field(f, carry):
        for half in range(2):
            for zh in range(2):
                for target, tile, first in ((up, 1, 5), (down, 0, 0)):
                    tiles = pack_rows(
                        lambda z: X[half, f, 8 * zh + z, 8 * tile : 8 * tile + 8, :], first
                    )
                    for t in range(3):
                        target[half, f, zh, 8 * t : 8 * t + 8, :] = tiles[t]
        def tile_of(half):
            return lambda k: X[half, f, k // 2, 8 * (k % 2) : 8 * (k % 2) + 8, :]
        east[f] = pack_columns(tile_of(1), lambda k: 4 * k - 125)
        west[f] = pack_columns(tile_of(0), lambda k: 4 * k)
        return carry

    for chunk in range(4):
        copies[2 * chunk].wait()
        copies[2 * chunk + 1].wait()
        lax.fori_loop(4 * chunk, 4 * chunk + 4, field, 0)
    for copy in copies[8:]:
        copy.wait()
    lax.fori_loop(M, F, field, 0)
    for index, plane in enumerate(
        (
            lambda half, k: V[0, half, k // 2, 8 * (k % 2) : 8 * (k % 2) + 8, :],
            lambda half, k: I[0, half, k // 2, 8 * (k % 2) : 8 * (k % 2) + 8, :].astype(f32),
            lambda half, k: I[1, half, k // 2, 8 * (k % 2) : 8 * (k % 2) + 8, :].astype(f32),
        )
    ):
        east[F + index] = pack_columns(lambda k: plane(1, k), lambda k: 4 * k - 125)
        west[F + index] = pack_columns(lambda k: plane(0, k), lambda k: 4 * k)
    rows = row_ids()
    for half in range(2):
        for zh in range(2):

            def last_row(z):
                level = 8 * zh + z
                speed = rolled(V[1, half, level, 8:16, :], -2, 0)
                flag = rolled(I[2, half, level, 8:16, :].astype(f32), -1, 0)
                wet = I[1, half, level, 8:16, :].astype(f32)
                return jnp.where(rows == 5, speed, jnp.where(rows == 6, flag, wet))

            for target, get, first in (
                (up, last_row, 5),
                (down, lambda z: I[1, half, 8 * zh + z, 0:8, :].astype(f32), 0),
            ):
                tiles = pack_rows(get, first)
                for t in range(3):
                    target[half, F, zh, 8 * t : 8 * t + 8, :] = tiles[t]


def pack(modes, mean, ve, vn, fe, fn, mask):
    rows = jax.ShapeDtypeStruct((2, F + 1, 2, ROWS // 2, LANES), f32)
    columns = jax.ShapeDtypeStruct((F + 3, 8, LANES), f32)
    return pl.pallas_call(
        pack_kernel,
        out_shape=(
            rows,
            rows,
            columns,
            columns,
        ),
        in_specs=[ANY] * 7,
        out_specs=(VMEM,) * 4,
        scratch_shapes=[
            pltpu.VMEM((2, F, NZ, BX, LANES), f32),
            pltpu.VMEM((2, 2, NZ, BX, LANES), f32),
            pltpu.VMEM((3, 2, NZ, BX, LANES), jnp.int32),
            pltpu.SemaphoreType.DMA((20,)),
        ],
        compiler_params=params(62),
        cost_estimate=cost(10**7, 7 * 10**6),
        name="pack",
    )(modes, mean, ve, vn, fe, fn, mask)


def along_lanes(first, second, outer, offset):
    lanes = lane_ids()
    a, b, c = (rolled(v, -offset, 1) for v in (first, second, outer))
    if offset > 0:
        inside = lanes < LANES - offset
        return jnp.where(inside, a, b), jnp.where(inside, b, c)
    outside = lanes < -offset
    return jnp.where(outside, c, a), jnp.where(outside, a, b)


def cell_weights(a_low, b_low, d_low, a_high, b_high, d_high):
    return (
        2.0 * a_low,
        -13.0 * a_low - 3.0 * b_low - 2.0 * a_high,
        47.0 * a_low + 27.0 * b_low + d_low + 13.0 * a_high + 3.0 * b_high,
        27.0 * a_low + 47.0 * b_low - d_low - 47.0 * a_high - 27.0 * b_high - d_high,
        -3.0 * a_low - 13.0 * b_low - 27.0 * a_high - 47.0 * b_high + d_high,
        2.0 * b_low + 3.0 * a_high + 13.0 * b_high,
        -2.0 * b_high,
    )


def face_parts(openness, speed, flag):
    scaled = openness * speed * (1.0 / 60.0)
    return scaled * flag, scaled * (1.0 - flag), horiz_diff * openness


def split(value):
    high = value.astype(bf16)
    return high, (value - high.astype(f32)).astype(bf16)


def add_products(acc, high, low):
    dims = (((1,), (1,)), ((), ()))
    acc[0:256, :] += lax.dot_general(high, high, dims, preferred_element_type=f32)
    acc[256:512, :] += lax.dot_general(low, high, dims, preferred_element_type=f32)


def field_sums(acc):
    rows = lax.broadcasted_iota(jnp.int32, (512, 256), 0)
    columns = lax.broadcasted_iota(jnp.int32, (512, 256), 1)
    kept = jnp.where(rows % 8 == columns % 8, acc[...], 0.0)
    by_row = jnp.sum(kept.reshape(64, 8, 256), axis=1)
    gather = (
        lax.broadcasted_iota(jnp.int32, (256, 32), 0) // 8
        == lax.broadcasted_iota(jnp.int32, (256, 32), 1)
    ).astype(f32)
    return jnp.dot(by_row, gather, precision=HIGH, preferred_element_type=f32)


def interior_kernel(
    modes, mean, ve, vn, fe, fn, mask, west, east,
    high_out, low_out, edge_out, weights_out, mean_out, sums_out,
    X, VE, FE, W, VN, FN, H, T, Z, acc, sems,
):
    zero_tile = jnp.zeros((8, LANES), f32)

    def clear(f, carry):
        for half in range(2):
            for z in range(NZ):
                X[half, f, z, 0:8, :] = zero_tile
                X[half, f, z, 24:32, :] = zero_tile
        return carry

    lax.fori_loop(0, F, clear, 0)
    for half in range(2):
        for z in range(NZ):
            edge_out[z, half, 0:8, :] = zero_tile
    for half in range(2):
        for z in range(NZ):
            VE[half, z, 0:8, :] = zero_tile
            FE[half, z, 0:8, :] = zero_tile
            W[half, z, 0:8, :] = zero_tile.astype(jnp.int32)
            W[half, z, 24:32, :] = zero_tile.astype(jnp.int32)
    acc[...] = jnp.zeros((512, 256), f32)
    lanes = lane_ids()
    rows = row_ids()

    copies = []
    body = pl.ds(8, BX)
    for half in range(2):
        for source, target in (
            (modes, X.at[half, pl.ds(0, M), :, body]),
            (mean, X.at[half, M, :, body]),
            (ve, VE.at[half, :, body]),
            (mask, W.at[half, :, body]),
            (vn, VN.at[half]),
            (fn, FN.at[0, half]),
            (fe, FN.at[1, half]),
        ):
            copies.append(
                pltpu.make_async_copy(lane_half(source, half), target, sems.at[len(copies)])
            )
    for copy in copies:
        copy.start()

    def beside(f, carry):
        after, before = east[f], west[f]
        for k in range(2 * NZ):
            H[f, k] = jnp.where(
                lanes < 64, rolled(after, -4 * k, 1), rolled(before, LANES - 3 - 4 * k, 1)
            )
        return carry

    lax.fori_loop(0, F + 3, beside, 0)
    for copy in copies:
        copy.wait()

    def level(z, carry):
        gain_up = jnp.where(z < NZ - 1, vert_diff, 0.0).astype(f32)
        gain_down = jnp.where(z > 0, vert_diff, 0.0).astype(f32)
        z_up = jnp.minimum(z + 1, NZ - 1)
        z_down = jnp.maximum(z - 1, 0)
        for half in range(2):
            for xt in range(2):
                FE[half, z, 8 + 8 * xt : 16 + 8 * xt, :] = FN[
                    1, half, z, 8 * xt : 8 * xt + 8, :
                ].astype(f32)
        for xt in range(2):
            start = 8 + 8 * xt

            def outer(index):
                return H[index, 2 * z + xt]

            def at(ref, half, offset):
                return ref[half, z, start + offset : start + offset + 8, :]

            wet = [at(W, half, 0).astype(f32) for half in range(2)]
            wx = []
            for half in range(2):
                before = wet[half] * at(W, half, -1).astype(f32)
                after = wet[half] * at(W, half, 1).astype(f32)
                wx.append(
                    cell_weights(
                        *face_parts(before, at(VE, half, -1), at(FE, half, -1)),
                        *face_parts(after, at(VE, half, 0), at(FE, half, 0)),
                    )
                )
            wet_out = outer(F + 2)
            following = along_lanes(wet[0], wet[1], wet_out, 1)
            own = [
                face_parts(
                    wet[half] * following[half],
                    VN[half, z, 8 * xt : 8 * xt + 8, :],
                    FN[0, half, z, 8 * xt : 8 * xt + 8, :].astype(f32),
                )
                for half in range(2)
            ]
            beyond = face_parts(wet_out * rolled(wet[0], -1, 1), outer(F), outer(F + 1))
            before = [along_lanes(own[0][i], own[1][i], beyond[i], -1) for i in range(3)]
            wy = [
                cell_weights(*(before[i][half] for i in range(3)), *own[half]) for half in range(2)
            ]
            centre = [
                wx[half][3] + wy[half][3] - (gain_up + gain_down) * wet[half] for half in range(2)
            ]
            w_up = [gain_up * wet[half] for half in range(2)]
            w_down = [gain_down * wet[half] for half in range(2)]
            for half in range(2):
                for index, plane in enumerate((at(VE, half, 0), at(FE, half, 0), wet[half])):
                    if xt == 0:
                        weights_out[half, z, 3 + index] = plane
                    else:
                        weights_out[half, z, 3 + index] = jnp.where(
                            rows < 4, weights_out[half, z, 3 + index], plane
                        )
                for d in range(1, 4):
                    if xt == 0:
                        weights_out[half, z, d - 1] = jnp.where(rows < d, wx[half][3 - d], 0.0)
                    else:
                        weights_out[half, z, d - 1] += jnp.where(
                            rows >= 8 - d, wx[half][3 + d], 0.0
                        )
            for f in range(F):
                own_cells = [X[half, f, z, start : start + 8, :] for half in range(2)]
                total = [
                    centre[half] * own_cells[half]
                    + w_up[half] * X[half, f, z_up, start : start + 8, :]
                    + w_down[half] * X[half, f, z_down, start : start + 8, :]
                    for half in range(2)
                ]
                edge = outer(f)
                for offset in (-3, -2, -1, 1, 2, 3):
                    moved = along_lanes(own_cells[0], own_cells[1], edge, offset)
                    for half in range(2):
                        total[half] += wx[half][3 + offset] * X[
                            half, f, z, start + offset : start + offset + 8, :
                        ]
                        total[half] += wy[half][3 + offset] * moved[half]
                for half in range(2):
                    columns = slice(LANES * half, LANES * half + LANES)
                    low_rows = rows < 4
                    if xt == 1:
                        cells = X[half, f, z, 8:16, :]
                        edge_out[z, half, 8 + 8 * f : 16 + 8 * f, :] = jnp.where(
                            low_rows, cells, own_cells[half]
                        )
                    if f == M:
                        mean_out[z, 8 * xt : 8 * xt + 8, columns] = (
                            own_cells[half] + time_step * total[half]
                        )
                    elif xt == 0:
                        T[half, f] = total[half]
                    else:
                        near = T[half, f]
                        Z[8 * f : 8 * f + 8, columns] = jnp.where(
                            low_rows, own_cells[half], cells
                        )
                        Z[128 + 8 * f : 136 + 8 * f, columns] = jnp.where(
                            low_rows, total[half], near
                        )
                        place = slice(TAIL + 8 * f, TAIL + 8 * f + 8)
                        edge_out[z, half, place, :] = jnp.where(low_rows, near, total[half])
        high, low = split(Z[...])
        high_out[z] = high
        low_out[z] = low
        add_products(acc, high, low)
        return carry

    lax.fori_loop(0, NZ, level, 0)
    sums_out[...] = field_sums(acc)


def interior(modes, mean, ve, vn, fe, fn, mask, west, east):
    parts = jax.ShapeDtypeStruct((NZ, 256, 256), bf16)
    return pl.pallas_call(
        interior_kernel,
        out_shape=(
            parts,
            parts,
            jax.ShapeDtypeStruct((NZ, 2, TAIL + 8 * M, LANES), f32),
            jax.ShapeDtypeStruct((2, NZ, 6, 8, LANES), f32),
            jax.ShapeDtypeStruct(mean.shape, f32),
            jax.ShapeDtypeStruct((64, 32), f32),
        ),
        in_specs=[ANY] * 7 + [VMEM] * 2,
        out_specs=(VMEM,) * 6,
        scratch_shapes=[
            pltpu.VMEM((2, F, NZ, 32, LANES), f32),
            pltpu.VMEM((2, NZ, 32, LANES), f32),
            pltpu.VMEM((2, NZ, 32, LANES), f32),
            pltpu.VMEM((2, NZ, 32, LANES), jnp.int32),
            pltpu.VMEM((2, NZ, BX, LANES), f32),
            pltpu.VMEM((2, 2, NZ, BX, LANES), jnp.int32),
            pltpu.VMEM((F + 3, 2 * NZ, 8, LANES), f32),
            pltpu.VMEM((2, M, 8, LANES), f32),
            pltpu.VMEM((256, 256), f32),
            pltpu.VMEM((512, 256), f32),
            pltpu.SemaphoreType.DMA((14,)),
        ],
        compiler_params=params(28),
        cost_estimate=cost(10**6, 10**6),
        name="interior",
    )(modes, mean, ve, vn, fe, fn, mask, west, east)


def edge_kernel(
    below, above, edge_in, weights, mean_in, sums_in,
    high_out, low_out, mean_out, sums_out, Z, acc,
):
    acc[...] = jnp.zeros((512, 256), f32)
    rows = row_ids()
    low_rows = rows < 4
    first_row = rows == 0
    last_row = rows == 7

    def rows_from(ref, half, f, zh, first):
        start = min(max(first, 0), 16)
        return rolled(ref[half, f, zh, start : start + 8, :], start - first, 0)

    def gains_of(half, z, zh, zi):
        speed, flag, wet = (weights[half, z, 3 + i] for i in range(3))
        speed = jnp.where(first_row, rows_from(below, half, F, zh, 3 * zi), speed)
        flag = jnp.where(first_row, rows_from(below, half, F, zh, 3 * zi + 1), flag)
        beyond = jnp.where(first_row, rows_from(below, half, F, zh, 3 * zi + 2), 0.0)
        beyond = jnp.where(last_row, rows_from(above, half, F, zh, 3 * zi - 7), beyond)
        a, b, d = face_parts(beyond * wet, speed, flag)
        near, far = 47.0 * a + 27.0 * b + d, 27.0 * a + 47.0 * b - d
        left, right = -13.0 * a - 3.0 * b, -3.0 * a - 13.0 * b
        outside = (
            weights[half, z, 0] + jnp.where(first_row, near, -far),
            weights[half, z, 1] + jnp.where(first_row, left, -right),
            weights[half, z, 2] + jnp.where(first_row, 2.0 * a, -2.0 * b),
        )
        inside = (
            jnp.where(first_row, far, -near),
            jnp.where(first_row, right, -left),
            jnp.where(first_row, 2.0 * b, -2.0 * a),
        )
        return outside, inside

    def group(zh, carry):
        for zi in range(8):
            z = 8 * zh + zi
            for half in range(2):
                outside, inside = gains_of(half, z, zh, zi)
                for f in range(F):
                    base = 8 + 8 * f
                    change = inside[0] * edge_in[z, half, base : base + 8, :]
                    for d in range(1, 4):
                        cells = jnp.where(
                            low_rows,
                            rows_from(below, half, f, zh, 3 * zi + 3 - d),
                            rows_from(above, half, f, zh, 3 * zi + d - 8),
                        )
                        change = change + outside[d - 1] * cells
                    for d in range(1, 3):
                        cells = jnp.where(
                            low_rows,
                            edge_in[z, half, base + d : base + d + 8, :],
                            edge_in[z, half, base - d : base - d + 8, :],
                        )
                        change = change + inside[d] * cells
                    if f < M:
                        Z[half, 8 * f : 8 * f + 8, :] = (
                            edge_in[z, half, TAIL + 8 * f : TAIL + 8 * f + 8, :] + change
                        )
                    else:
                        columns = slice(LANES * half, LANES * half + LANES)
                        step = time_step * change
                        mean_out[z, 0:8, columns] = mean_in[z, 0:8, columns] + jnp.where(
                            low_rows, step, 0.0
                        )
                        mean_out[z, 8:16, columns] = mean_in[z, 8:16, columns] + jnp.where(
                            low_rows, 0.0, step
                        )
            halves = [
                jnp.concatenate([edge_in[z, half, 8 : 8 + 8 * M, :], Z[half]], axis=0)
                for half in range(2)
            ]
            high, low = split(jnp.concatenate(halves, axis=1))
            high_out[z] = high
            low_out[z] = low
            add_products(acc, high, low)
        return carry

    lax.fori_loop(0, 2, group, 0)
    sums = sums_in[...] + field_sums(acc)
    identity = (
        lax.broadcasted_iota(jnp.int32, (32, 32), 0) == lax.broadcasted_iota(jnp.int32, (32, 32), 1)
    ).astype(f32)
    turned = lax.dot_general(
        identity, sums[32:64], (((1,), (1,)), ((), ())), precision=HIGH, preferred_element_type=f32
    )
    sums_out[...] = sums[0:32] + sums[32:64] + turned


def edges(below, above, edge_in, weights, mean_in, sums_in):
    parts = jax.ShapeDtypeStruct((NZ, 256, 256), bf16)
    return pl.pallas_call(
        edge_kernel,
        out_shape=(
            parts,
            parts,
            jax.ShapeDtypeStruct(mean_in.shape, f32),
            jax.ShapeDtypeStruct((32, 32), f32),
        ),
        in_specs=[VMEM] * 6,
        out_specs=(VMEM,) * 4,
        scratch_shapes=[
            pltpu.VMEM((2, 8 * M, LANES), f32),
            pltpu.VMEM((512, 256), f32),
        ],
        compiler_params=params(16),
        cost_estimate=cost(10**9, 10**7),
        name="edges",
    )(below, above, edge_in, weights, mean_in, sums_in)


def factor_and_map(sums, cell_count):
    inner = sums * (1.0 / cell_count)
    row = lax.broadcasted_iota(jnp.int32, (M, 2 * M), 0)
    column = lax.broadcasted_iota(jnp.int32, (M, 2 * M), 1)
    update = jnp.where(
        column < M,
        jnp.where(column == row, 1.0, 0.0) - time_step * inner[M : 2 * M, :],
        jnp.where(column == row + M, time_step, 0.0),
    )
    half_way = jnp.dot(update, inner, precision=HIGH, preferred_element_type=f32)
    gram = lax.dot_general(
        half_way, update, (((1,), (1,)), ((), ())), precision=HIGH, preferred_element_type=f32
    )
    row_g = lax.broadcasted_iota(jnp.int32, (M, M), 0)
    column_g = lax.broadcasted_iota(jnp.int32, (M, M), 1)
    left, right = gram, update
    for j in range(M):
        pivot = jnp.sum(jnp.where(column_g == j, left, 0.0), axis=1, keepdims=True)
        scale = 1.0 / jnp.sqrt(pivot[j : j + 1, :])
        left_row = left[j : j + 1, :] * scale
        right_row = right[j : j + 1, :] * scale
        share = jnp.where(row_g[:, 0:1] > j, pivot * scale, 0.0)
        left = jnp.where(row_g == j, left_row, left - share * left_row)
        right = jnp.where(row == j, right_row, right - share * right_row)
    return jnp.where(column_g >= row_g, left, 0.0), right


def spread_map(part):
    tall = (
        lax.broadcasted_iota(jnp.int32, (8 * M, M), 0) // 8
        == lax.broadcasted_iota(jnp.int32, (8 * M, M), 1)
    ).astype(bf16)
    wide = (
        lax.broadcasted_iota(jnp.int32, (2 * M, 256), 1) // 8
        == lax.broadcasted_iota(jnp.int32, (2 * M, 256), 0)
    ).astype(bf16)
    rows = jnp.dot(tall, part, preferred_element_type=f32).astype(bf16)
    full = jnp.dot(rows, wide, preferred_element_type=f32)
    row = lax.broadcasted_iota(jnp.int32, (8 * M, 256), 0)
    column = lax.broadcasted_iota(jnp.int32, (8 * M, 256), 1)
    return jnp.where(row % 8 == column % 8, full, 0.0).astype(bf16)


def make_apply_kernel(cell_count):
    def apply_kernel(sums, high_i, low_i, high_e, low_e, out, factor_out, maps, new, sems):
        factor, mapping = factor_and_map(sums[...], cell_count)
        factor_out[...] = factor
        high, low = split(mapping)
        maps[0:128, :] = spread_map(high)
        maps[128:256, :] = spread_map(low)
        low_rows = lax.broadcasted_iota(jnp.int32, (M, 8, 256), 1) < 4

        def put(z, slot):
            return pltpu.make_async_copy(new.at[slot], out.at[:, z], sems.at[slot])

        def level(z, carry):
            slot = lax.rem(z, SLOTS)

            @pl.when(z >= SLOTS)
            def _():
                put(z - SLOTS, slot).wait()

            results = []
            for high, low in ((high_i, low_i), (high_e, low_e)):
                first = jnp.dot(maps[...], high[z], preferred_element_type=f32)
                second = jnp.dot(maps[0:128, :], low[z], preferred_element_type=f32)
                results.append((first[0:128] + first[128:256] + second).reshape(M, 8, 256))
            inner, edge = results
            new[slot, :, 0:8, :] = jnp.where(low_rows, edge, inner)
            new[slot, :, 8:16, :] = jnp.where(low_rows, inner, edge)
            put(z, slot).start()
            return carry

        lax.fori_loop(0, NZ, level, 0)
        for z in range(NZ - SLOTS, NZ):
            put(z, z % SLOTS).wait()

    return apply_kernel


def apply_map(sums, high_i, low_i, high_e, low_e, cell_count):
    return pl.pallas_call(
        make_apply_kernel(cell_count),
        out_shape=(
            jax.ShapeDtypeStruct((M, NZ, BX, 256), f32),
            jax.ShapeDtypeStruct((M, M), f32),
        ),
        in_specs=[VMEM] * 5,
        out_specs=(ANY, VMEM),
        scratch_shapes=[
            pltpu.VMEM((256, 256), bf16),
            pltpu.VMEM((SLOTS, M, BX, 256), f32),
            pltpu.SemaphoreType.DMA((SLOTS,)),
        ],
        compiler_params=params(12),
        cost_estimate=cost(10**9, 13 * 10**6),
        name="apply",
    )(sums, high_i, low_i, high_e, low_e)


def onward(value, axis):
    size = lax.axis_size(axis)
    return lax.ppermute(value, axis, [(i, i + 1) for i in range(size - 1)])


def backward(value, axis):
    size = lax.axis_size(axis)
    return lax.ppermute(value, axis, [(i + 1, i) for i in range(size - 1)])


def exchanged(value, axes, distance):
    size = lax.axis_size(axes)
    return lax.ppermute(value, axes, [(i, i ^ distance) for i in range(size)])


def shards(
    mean_field, mode_fields, velocity_east, velocity_north, flag_east, flag_north, ocean_mask
):
    axes = ("gx", "gy")
    up, down, east_send, west_send = pack(
        mode_fields, mean_field, velocity_east, velocity_north, flag_east, flag_north, ocean_mask
    )
    below = onward(up, "gx")
    above = backward(down, "gx")
    west = onward(east_send, "gy")
    east = backward(west_send, "gy")
    high_i, low_i, edge, weights, mean_part, sums_i = interior(
        mode_fields, mean_field, velocity_east, velocity_north, flag_east, flag_north,
        ocean_mask, west, east,
    )
    high_e, low_e, mean_next, sums = edges(below, above, edge, weights, mean_part, sums_i)
    for distance in (1, 2, 6, 8, 24, 32, 96):
        sums = sums + exchanged(sums, axes, distance)
    cell_count = float(NZ * BX * 256 * lax.axis_size("gx") * lax.axis_size("gy"))
    modes_next, factor = apply_map(sums, high_i, low_i, high_e, low_e, cell_count)
    return (mean_next, modes_next, factor)


def solution(mesh):
    plane = P(None, "gx", "gy")
    return jax.shard_map(
        shards,
        mesh=mesh,
        in_specs=(plane, P(None, None, "gx", "gy"), plane, plane, plane, plane, plane),
        out_specs=(plane, P(None, None, "gx", "gy"), P()),
        check_vma=False,
    )
```

```python
import jax
import jax.numpy as jnp
from jax import lax
from jax.experimental import pallas as pl
from jax.experimental.pallas import tpu as pltpu
from jax.sharding import PartitionSpec as P

time_step = 0.1
horiz_diff = 0.05
vert_diff = 0.2

M = 16
F = 17
NZ = 16
BX = 16
LANES = 128
ROWS = 3 * NZ
SLOTS = 4
TAIL = 8 + 8 * F
HIGH = lax.Precision.HIGHEST
f32 = jnp.float32
bf16 = jnp.bfloat16

ANY = pl.BlockSpec(memory_space=pl.ANY)
HBM = pl.BlockSpec(memory_space=pltpu.HBM)
VMEM = pl.BlockSpec(memory_space=pltpu.VMEM)


def params(mib):
    return pltpu.CompilerParams(vmem_limit_bytes=mib * 1024 * 1024)


def cost(flops, nbytes):
    return pl.CostEstimate(flops=flops, bytes_accessed=nbytes, transcendentals=0)


def rolled(value, shift, axis):
    shift = shift % value.shape[axis]
    return value if shift == 0 else pltpu.roll(value, shift, axis)


def lane_ids():
    return lax.broadcasted_iota(jnp.int32, (8, LANES), 1)


def row_ids():
    return lax.broadcasted_iota(jnp.int32, (8, LANES), 0)


def lane_half(ref, half):
    where = (slice(None),) * (len(ref.shape) - 1) + (pl.ds(LANES * half, LANES),)
    return ref.at[where]


def pack_rows(get, first_row):
    rows = row_ids()
    tiles = []
    for out in range(3):
        tile = None
        for z in range(8):
            low, high = max(3 * z, 8 * out), min(3 * z + 3, 8 * out + 8)
            if low >= high:
                continue
            piece = rolled(get(z), 3 * z - 8 * out - first_row, 0)
            tile = piece if tile is None else jnp.where(rows >= low - 8 * out, piece, tile)
        tiles.append(tile)
    return tiles


def pack_columns(get, shift_of):
    slot = lane_ids() // 4
    parts = [jnp.zeros((8, LANES), f32) for _ in range(4)]
    for k in range(2 * NZ):
        moved = rolled(get(k), shift_of(k), 1)
        parts[k % 4] = jnp.where(slot == k, moved, parts[k % 4])
    out = parts[0]
    for k in range(1, 4):
        out = jnp.where(slot % 4 == k, parts[k], out)
    return out


def pack_kernel(
    modes, mean, ve, vn, fe, fn, mask, up, down, east, west, X, V, I, sems
):
    copies = []
    for chunk in range(4):
        for half in range(2):
            copies.append(
                pltpu.make_async_copy(
                    lane_half(modes, half).at[pl.ds(4 * chunk, 4)],
                    X.at[half, pl.ds(4 * chunk, 4), :, pl.ds(8, BX)],
                    sems.at[len(copies)],
                )
            )
    for source, target in (
        (mean, lambda half: X.at[half, M, :, pl.ds(8, BX)]),
        (vn, lambda half: V.at[0, half]),
        (ve, lambda half: V.at[1, half]),
        (fn, lambda half: I.at[0, half]),
        (mask, lambda half: I.at[1, half]),
        (fe, lambda half: I.at[2, half]),
    ):
        for half in range(2):
            copies.append(
                pltpu.make_async_copy(lane_half(source, half), target(half), sems.at[len(copies)])
            )
    for copy in copies:
        copy.start()
    zero_tile = jnp.zeros((8, LANES), f32)

    def clear(f, carry):
        for half in range(2):
            for z in range(NZ):
                X[half, f, z, 0:8, :] = zero_tile
                X[half, f, z, 24:32, :] = zero_tile
        return carry

    lax.fori_loop(0, F, clear, 0)

    def field(f, carry):
        for half in range(2):
            for zh in range(2):
                for target, tile, first in ((up, 1, 5), (down, 0, 0)):
                    tiles = pack_rows(
                        lambda z: X[half, f, 8 * zh + z, 8 + 8 * tile : 16 + 8 * tile, :], first
                    )
                    for t in range(3):
                        target[half, f, zh, 8 * t : 8 * t + 8, :] = tiles[t]
        def tile_of(half):
            return lambda k: X[half, f, k // 2, 8 + 8 * (k % 2) : 16 + 8 * (k % 2), :]
        east[f] = pack_columns(tile_of(1), lambda k: 4 * k - 125)
        west[f] = pack_columns(tile_of(0), lambda k: 4 * k)
        return carry

    for chunk in range(4):
        copies[2 * chunk].wait()
        copies[2 * chunk + 1].wait()
        lax.fori_loop(4 * chunk, 4 * chunk + 4, field, 0)
    for copy in copies[8:]:
        copy.wait()
    lax.fori_loop(M, F, field, 0)
    for index, plane in enumerate(
        (
            lambda half, k: V[0, half, k // 2, 8 * (k % 2) : 8 * (k % 2) + 8, :],
            lambda half, k: I[0, half, k // 2, 8 * (k % 2) : 8 * (k % 2) + 8, :].astype(f32),
            lambda half, k: I[1, half, k // 2, 8 * (k % 2) : 8 * (k % 2) + 8, :].astype(f32),
        )
    ):
        east[F + index] = pack_columns(lambda k: plane(1, k), lambda k: 4 * k - 125)
        west[F + index] = pack_columns(lambda k: plane(0, k), lambda k: 4 * k)
    rows = row_ids()
    for half in range(2):
        for zh in range(2):

            def last_row(z):
                level = 8 * zh + z
                speed = rolled(V[1, half, level, 8:16, :], -2, 0)
                flag = rolled(I[2, half, level, 8:16, :].astype(f32), -1, 0)
                wet = I[1, half, level, 8:16, :].astype(f32)
                return jnp.where(rows == 5, speed, jnp.where(rows == 6, flag, wet))

            for target, get, first in (
                (up, last_row, 5),
                (down, lambda z: I[1, half, 8 * zh + z, 0:8, :].astype(f32), 0),
            ):
                tiles = pack_rows(get, first)
                for t in range(3):
                    target[half, F, zh, 8 * t : 8 * t + 8, :] = tiles[t]


def pack(modes, mean, ve, vn, fe, fn, mask):
    rows = jax.ShapeDtypeStruct((2, F + 1, 2, ROWS // 2, LANES), f32)
    columns = jax.ShapeDtypeStruct((F + 3, 8, LANES), f32)
    return pl.pallas_call(
        pack_kernel,
        out_shape=(
            rows,
            rows,
            columns,
            columns,
            jax.ShapeDtypeStruct((2, F, NZ, 32, LANES), f32),
        ),
        in_specs=[HBM] * 7,
        out_specs=(VMEM,) * 5,
        scratch_shapes=[
            pltpu.VMEM((2, 2, NZ, BX, LANES), f32),
            pltpu.VMEM((3, 2, NZ, BX, LANES), jnp.int32),
            pltpu.SemaphoreType.DMA((20,)),
        ],
        compiler_params=params(24),
        cost_estimate=cost(10**7, 7 * 10**6),
        name="pack",
    )(modes, mean, ve, vn, fe, fn, mask)


def along_lanes(first, second, outer, offset):
    lanes = lane_ids()
    a, b, c = (rolled(v, -offset, 1) for v in (first, second, outer))
    if offset > 0:
        inside = lanes < LANES - offset
        return jnp.where(inside, a, b), jnp.where(inside, b, c)
    outside = lanes < -offset
    return jnp.where(outside, c, a), jnp.where(outside, a, b)


def around_lanes(first, second, offset):
    lanes = lane_ids()
    a, b = (rolled(v, -offset, 1) for v in (first, second))
    kept = lanes < LANES - offset if offset > 0 else lanes >= -offset
    return jnp.where(kept, a, b), jnp.where(kept, b, a)


def cell_weights(a_low, b_low, d_low, a_high, b_high, d_high):
    return (
        2.0 * a_low,
        -13.0 * a_low - 3.0 * b_low - 2.0 * a_high,
        47.0 * a_low + 27.0 * b_low + d_low + 13.0 * a_high + 3.0 * b_high,
        27.0 * a_low + 47.0 * b_low - d_low - 47.0 * a_high - 27.0 * b_high - d_high,
        -3.0 * a_low - 13.0 * b_low - 27.0 * a_high - 47.0 * b_high + d_high,
        2.0 * b_low + 3.0 * a_high + 13.0 * b_high,
        -2.0 * b_high,
    )


def face_parts(openness, speed, flag):
    scaled = openness * speed * (1.0 / 60.0)
    return scaled * flag, scaled * (1.0 - flag), horiz_diff * openness


def split(value):
    high = value.astype(bf16)
    return high, (value - high.astype(f32)).astype(bf16)


def add_products(acc, high, low):
    dims = (((1,), (1,)), ((), ()))
    acc[0:256, :] += lax.dot_general(high, high, dims, preferred_element_type=f32)
    acc[256:512, :] += lax.dot_general(low, high, dims, preferred_element_type=f32)


def joined(parts):
    return jnp.concatenate([parts[z] for z in range(NZ)], axis=1)


def field_sums(acc):
    rows = lax.broadcasted_iota(jnp.int32, (512, 256), 0)
    columns = lax.broadcasted_iota(jnp.int32, (512, 256), 1)
    kept = jnp.where(rows % 8 == columns % 8, acc[...], 0.0)
    by_row = jnp.sum(kept.reshape(64, 8, 256), axis=1)
    gather = (
        lax.broadcasted_iota(jnp.int32, (256, 32), 0) // 8
        == lax.broadcasted_iota(jnp.int32, (256, 32), 1)
    ).astype(f32)
    return jnp.dot(by_row, gather, precision=HIGH, preferred_element_type=f32)


def interior_kernel(
    X, ve, vn, fe, fn, mask, west, east, own_last, own_first,
    high_out, low_out, edge_out, weights_out, mean_out, sums_out,
    VE, FE, W, VN, FN, H, G, T, Z, acc, sems,
):
    zero_tile = jnp.zeros((8, LANES), f32)
    for half in range(2):
        for z in range(NZ):
            edge_out[z, half, 0:8, :] = zero_tile
    for half in range(2):
        for z in range(NZ):
            VE[half, z, 0:8, :] = zero_tile
            FE[half, z, 0:8, :] = zero_tile
            W[half, z, 0:8, :] = zero_tile.astype(jnp.int32)
            W[half, z, 24:32, :] = zero_tile.astype(jnp.int32)
    acc[...] = jnp.zeros((512, 256), f32)
    lanes = lane_ids()
    rows = row_ids()

    copies = []
    body = pl.ds(8, BX)
    for half in range(2):
        for source, target in (
            (ve, VE.at[half, :, body]),
            (mask, W.at[half, :, body]),
            (vn, VN.at[half]),
            (fn, FN.at[0, half]),
            (fe, FN.at[1, half]),
        ):
            copies.append(
                pltpu.make_async_copy(lane_half(source, half), target, sems.at[len(copies)])
            )
    for copy in copies:
        copy.start()

    def spread(index, before, after):
        for k in range(2 * NZ):
            moved_after = rolled(after, -4 * k, 1)
            moved_before = rolled(before, LANES - 3 - 4 * k, 1)
            yield index, k, moved_before, moved_after

    for f in range(F, F + 3):
        for index, k, moved_before, moved_after in spread(f, west[f], east[f]):
            H[index, k] = jnp.where(lanes < 64, moved_after, moved_before)

    place = lanes % 4

    (v_in, f_in, w_in) = (west[F + i] for i in range(3))
    (v_own, f_own, w_own) = (own_first[F + i] for i in range(3))
    lower_of = lambda outer_plane, own: jnp.where(
        place == 0, rolled(outer_plane, -2, 1), rolled(own, 1, 1)
    )
    low_face = face_parts(
        lower_of(w_in, w_own) * w_own, lower_of(v_in, v_own), lower_of(f_in, f_own)
    )
    high_face = face_parts(w_own * rolled(w_own, -1, 1), v_own, f_own)
    first_gains = cell_weights(*low_face, *high_face)
    for d in range(1, 4):
        G[d - 1] = jnp.where(place < d, first_gains[3 - d], 0.0)
    w_next = east[F + 2]
    (v_own, f_own, w_own) = (own_last[F + i] for i in range(3))
    high_face = face_parts(
        w_own * jnp.where(place == 2, rolled(w_next, 2, 1), rolled(w_own, -1, 1)), v_own, f_own
    )
    low_face = tuple(rolled(part, 1, 1) for part in high_face)
    last_gains = cell_weights(*low_face, *high_face)
    for d in range(1, 4):
        G[2 + d] = jnp.where((place >= 3 - d) & (place < 3), last_gains[3 + d], 0.0)

    def beside(f, carry):
        before, after = west[f], east[f]
        first = (
            G[0] * rolled(before, -2, 1) + G[1] * rolled(before, -1, 1) + G[2] * before
        )
        last = G[3] * rolled(after, 2, 1) + G[4] * rolled(after, 1, 1) + G[5] * after
        for index, k, moved_last, moved_first in spread(f, last, first):
            H[index, k] = jnp.where(
                lanes < 3, moved_first, jnp.where(lanes >= LANES - 3, moved_last, 0.0)
            )
        return carry

    lax.fori_loop(0, F, beside, 0)
    for copy in copies:
        copy.wait()

    def level(z, carry):
        gain_up = jnp.where(z < NZ - 1, vert_diff, 0.0).astype(f32)
        gain_down = jnp.where(z > 0, vert_diff, 0.0).astype(f32)
        z_up = jnp.minimum(z + 1, NZ - 1)
        z_down = jnp.maximum(z - 1, 0)
        for half in range(2):
            for xt in range(2):
                FE[half, z, 8 + 8 * xt : 16 + 8 * xt, :] = FN[
                    1, half, z, 8 * xt : 8 * xt + 8, :
                ].astype(f32)
        for xt in range(2):
            start = 8 + 8 * xt

            def outer(index):
                return H[index, 2 * z + xt]

            def at(ref, half, offset):
                return ref[half, z, start + offset : start + offset + 8, :]

            wet = [at(W, half, 0).astype(f32) for half in range(2)]
            wx = []
            for half in range(2):
                before = wet[half] * at(W, half, -1).astype(f32)
                after = wet[half] * at(W, half, 1).astype(f32)
                wx.append(
                    cell_weights(
                        *face_parts(before, at(VE, half, -1), at(FE, half, -1)),
                        *face_parts(after, at(VE, half, 0), at(FE, half, 0)),
                    )
                )
            wet_out = outer(F + 2)
            following = along_lanes(wet[0], wet[1], wet_out, 1)
            own = [
                face_parts(
                    wet[half] * following[half],
                    VN[half, z, 8 * xt : 8 * xt + 8, :],
                    FN[0, half, z, 8 * xt : 8 * xt + 8, :].astype(f32),
                )
                for half in range(2)
            ]
            beyond = face_parts(wet_out * rolled(wet[0], -1, 1), outer(F), outer(F + 1))
            before = [along_lanes(own[0][i], own[1][i], beyond[i], -1) for i in range(3)]
            wy = [
                cell_weights(*(before[i][half] for i in range(3)), *own[half]) for half in range(2)
            ]
            wy = [
                [
                    jnp.where(
                        (lanes < 3 - j) if half == 0 else (lanes >= LANES + 3 - j), 0.0, wy[half][j]
                    )
                    if (half == 0) == (j < 3) and j != 3
                    else wy[half][j]
                    for j in range(7)
                ]
                for half in range(2)
            ]
            centre = [
                wx[half][3] + wy[half][3] - (gain_up + gain_down) * wet[half] for half in range(2)
            ]
            w_up = [gain_up * wet[half] for half in range(2)]
            w_down = [gain_down * wet[half] for half in range(2)]
            for half in range(2):
                for index, plane in enumerate((at(VE, half, 0), at(FE, half, 0), wet[half])):
                    if xt == 0:
                        weights_out[half, z, 3 + index] = plane
                    else:
                        weights_out[half, z, 3 + index] = jnp.where(
                            rows < 4, weights_out[half, z, 3 + index], plane
                        )
                for d in range(1, 4):
                    if xt == 0:
                        weights_out[half, z, d - 1] = jnp.where(rows < d, wx[half][3 - d], 0.0)
                    else:
                        weights_out[half, z, d - 1] += jnp.where(
                            rows >= 8 - d, wx[half][3 + d], 0.0
                        )
            for f in range(F):
                own_cells = [X[half, f, z, start : start + 8, :] for half in range(2)]
                total = [
                    centre[half] * own_cells[half]
                    + w_up[half] * X[half, f, z_up, start : start + 8, :]
                    + w_down[half] * X[half, f, z_down, start : start + 8, :]
                    for half in range(2)
                ]
                beyond_block = outer(f)
                total[0] += jnp.where(lanes < 64, beyond_block, 0.0)
                total[1] += jnp.where(lanes < 64, 0.0, beyond_block)
                for offset in (-3, -2, -1, 1, 2, 3):
                    moved = around_lanes(own_cells[0], own_cells[1], offset)
                    for half in range(2):
                        total[half] += wx[half][3 + offset] * X[
                            half, f, z, start + offset : start + offset + 8, :
                        ]
                        total[half] += wy[half][3 + offset] * moved[half]
                for half in range(2):
                    columns = slice(LANES * half, LANES * half + LANES)
                    low_rows = rows < 4
                    if xt == 1:
                        cells = X[half, f, z, 8:16, :]
                        edge_out[z, half, 8 + 8 * f : 16 + 8 * f, :] = jnp.where(
                            low_rows, cells, own_cells[half]
                        )
                    if f == M:
                        mean_out[z, 8 * xt : 8 * xt + 8, columns] = (
                            own_cells[half] + time_step * total[half]
                        )
                    elif xt == 0:
                        T[half, f] = total[half]
                    else:
                        near = T[half, f]
                        Z[8 * f : 8 * f + 8, columns] = jnp.where(
                            low_rows, own_cells[half], cells
                        )
                        Z[128 + 8 * f : 136 + 8 * f, columns] = jnp.where(
                            low_rows, total[half], near
                        )
                        place = slice(TAIL + 8 * f, TAIL + 8 * f + 8)
                        edge_out[z, half, place, :] = jnp.where(low_rows, near, total[half])
        high, low = split(Z[...])
        high_out[z] = high
        low_out[z] = low
        return carry

    lax.fori_loop(0, NZ, level, 0)
    add_products(acc, joined(high_out), joined(low_out))
    sums_out[...] = field_sums(acc)


def interior(cells, ve, vn, fe, fn, mask, west, east, own_last, own_first):
    parts = jax.ShapeDtypeStruct((NZ, 256, 256), bf16)
    return pl.pallas_call(
        interior_kernel,
        out_shape=(
            parts,
            parts,
            jax.ShapeDtypeStruct((NZ, 2, TAIL + 8 * M, LANES), f32),
            jax.ShapeDtypeStruct((2, NZ, 6, 8, LANES), f32),
            jax.ShapeDtypeStruct(ve.shape, f32),
            jax.ShapeDtypeStruct((64, 32), f32),
        ),
        in_specs=[VMEM] + [HBM] * 5 + [VMEM] * 4,
        out_specs=(VMEM,) * 6,
        scratch_shapes=[
            pltpu.VMEM((2, NZ, 32, LANES), f32),
            pltpu.VMEM((2, NZ, 32, LANES), f32),
            pltpu.VMEM((2, NZ, 32, LANES), jnp.int32),
            pltpu.VMEM((2, NZ, BX, LANES), f32),
            pltpu.VMEM((2, 2, NZ, BX, LANES), jnp.int32),
            pltpu.VMEM((F + 3, 2 * NZ, 8, LANES), f32),
            pltpu.VMEM((6, 8, LANES), f32),
            pltpu.VMEM((2, M, 8, LANES), f32),
            pltpu.VMEM((256, 256), f32),
            pltpu.VMEM((512, 256), f32),
            pltpu.SemaphoreType.DMA((10,)),
        ],
        compiler_params=params(28),
        cost_estimate=cost(10**10, 4 * 10**7),
        name="interior",
    )(cells, ve, vn, fe, fn, mask, west, east, own_last, own_first)


def edge_kernel(
    below, above, edge_in, weights, mean_in, sums_in,
    high_out, low_out, mean_out, sums_out, Z, acc,
):
    acc[...] = jnp.zeros((512, 256), f32)
    rows = row_ids()
    low_rows = rows < 4
    first_row = rows == 0
    last_row = rows == 7

    def rows_from(ref, half, f, zh, first):
        start = min(max(first, 0), 16)
        return rolled(ref[half, f, zh, start : start + 8, :], start - first, 0)

    def gains_of(half, z, zh, zi):
        speed, flag, wet = (weights[half, z, 3 + i] for i in range(3))
        speed = jnp.where(first_row, rows_from(below, half, F, zh, 3 * zi), speed)
        flag = jnp.where(first_row, rows_from(below, half, F, zh, 3 * zi + 1), flag)
        beyond = jnp.where(first_row, rows_from(below, half, F, zh, 3 * zi + 2), 0.0)
        beyond = jnp.where(last_row, rows_from(above, half, F, zh, 3 * zi - 7), beyond)
        a, b, d = face_parts(beyond * wet, speed, flag)
        near, far = 47.0 * a + 27.0 * b + d, 27.0 * a + 47.0 * b - d
        left, right = -13.0 * a - 3.0 * b, -3.0 * a - 13.0 * b
        outside = (
            weights[half, z, 0] + jnp.where(first_row, near, -far),
            weights[half, z, 1] + jnp.where(first_row, left, -right),
            weights[half, z, 2] + jnp.where(first_row, 2.0 * a, -2.0 * b),
        )
        inside = (
            jnp.where(first_row, far, -near),
            jnp.where(first_row, right, -left),
            jnp.where(first_row, 2.0 * b, -2.0 * a),
        )
        return outside, inside

    def group(zh, carry):
        for zi in range(8):
            z = 8 * zh + zi
            for half in range(2):
                outside, inside = gains_of(half, z, zh, zi)
                for f in range(F):
                    base = 8 + 8 * f
                    change = inside[0] * edge_in[z, half, base : base + 8, :]
                    for d in range(1, 4):
                        cells = jnp.where(
                            low_rows,
                            rows_from(below, half, f, zh, 3 * zi + 3 - d),
                            rows_from(above, half, f, zh, 3 * zi + d - 8),
                        )
                        change = change + outside[d - 1] * cells
                    for d in range(1, 3):
                        cells = jnp.where(
                            low_rows,
                            edge_in[z, half, base + d : base + d + 8, :],
                            edge_in[z, half, base - d : base - d + 8, :],
                        )
                        change = change + inside[d] * cells
                    if f < M:
                        Z[half, 8 * f : 8 * f + 8, :] = (
                            edge_in[z, half, TAIL + 8 * f : TAIL + 8 * f + 8, :] + change
                        )
                    else:
                        columns = slice(LANES * half, LANES * half + LANES)
                        step = time_step * change
                        mean_out[z, 0:8, columns] = mean_in[z, 0:8, columns] + jnp.where(
                            low_rows, step, 0.0
                        )
                        mean_out[z, 8:16, columns] = mean_in[z, 8:16, columns] + jnp.where(
                            low_rows, 0.0, step
                        )
            halves = [
                jnp.concatenate([edge_in[z, half, 8 : 8 + 8 * M, :], Z[half]], axis=0)
                for half in range(2)
            ]
            high, low = split(jnp.concatenate(halves, axis=1))
            high_out[z] = high
            low_out[z] = low
            add_products(acc, high, low)
        return carry

    lax.fori_loop(0, 2, group, 0)
    sums = sums_in[...] + field_sums(acc)
    identity = (
        lax.broadcasted_iota(jnp.int32, (32, 32), 0) == lax.broadcasted_iota(jnp.int32, (32, 32), 1)
    ).astype(f32)
    turned = lax.dot_general(
        identity, sums[32:64], (((1,), (1,)), ((), ())), precision=HIGH, preferred_element_type=f32
    )
    sums_out[...] = sums[0:32] + sums[32:64] + turned


def edges(below, above, edge_in, weights, mean_in, sums_in):
    parts = jax.ShapeDtypeStruct((NZ, 256, 256), bf16)
    return pl.pallas_call(
        edge_kernel,
        out_shape=(
            parts,
            parts,
            jax.ShapeDtypeStruct(mean_in.shape, f32),
            jax.ShapeDtypeStruct((32, 32), f32),
        ),
        in_specs=[VMEM] * 6,
        out_specs=(VMEM,) * 4,
        scratch_shapes=[
            pltpu.VMEM((2, 8 * M, LANES), f32),
            pltpu.VMEM((512, 256), f32),
        ],
        compiler_params=params(16),
        cost_estimate=cost(10**9, 10**7),
        name="edges",
    )(below, above, edge_in, weights, mean_in, sums_in)


def factor_and_map(sums, cell_count):
    inner = sums * (1.0 / cell_count)
    row = lax.broadcasted_iota(jnp.int32, (M, 2 * M), 0)
    column = lax.broadcasted_iota(jnp.int32, (M, 2 * M), 1)
    update = jnp.where(
        column < M,
        jnp.where(column == row, 1.0, 0.0) - time_step * inner[M : 2 * M, :],
        jnp.where(column == row + M, time_step, 0.0),
    )
    half_way = jnp.dot(update, inner, precision=HIGH, preferred_element_type=f32)
    gram = lax.dot_general(
        half_way, update, (((1,), (1,)), ((), ())), precision=HIGH, preferred_element_type=f32
    )
    row_g = lax.broadcasted_iota(jnp.int32, (M, M), 0)
    column_g = lax.broadcasted_iota(jnp.int32, (M, M), 1)
    left, right = gram, update
    for j in range(M):
        pivot = jnp.sum(jnp.where(column_g == j, left, 0.0), axis=1, keepdims=True)
        scale = 1.0 / jnp.sqrt(pivot[j : j + 1, :])
        left_row = left[j : j + 1, :] * scale
        right_row = right[j : j + 1, :] * scale
        share = jnp.where(row_g[:, 0:1] > j, pivot * scale, 0.0)
        left = jnp.where(row_g == j, left_row, left - share * left_row)
        right = jnp.where(row == j, right_row, right - share * right_row)
    return jnp.where(column_g >= row_g, left, 0.0), right


def spread_map(part):
    tall = (
        lax.broadcasted_iota(jnp.int32, (8 * M, M), 0) // 8
        == lax.broadcasted_iota(jnp.int32, (8 * M, M), 1)
    ).astype(bf16)
    wide = (
        lax.broadcasted_iota(jnp.int32, (2 * M, 256), 1) // 8
        == lax.broadcasted_iota(jnp.int32, (2 * M, 256), 0)
    ).astype(bf16)
    rows = jnp.dot(tall, part, preferred_element_type=f32).astype(bf16)
    full = jnp.dot(rows, wide, preferred_element_type=f32)
    row = lax.broadcasted_iota(jnp.int32, (8 * M, 256), 0)
    column = lax.broadcasted_iota(jnp.int32, (8 * M, 256), 1)
    return jnp.where(row % 8 == column % 8, full, 0.0).astype(bf16)


def make_apply_kernel(cell_count):
    def apply_kernel(sums, high_i, low_i, high_e, low_e, out, factor_out, maps, new, sems):
        factor, mapping = factor_and_map(sums[...], cell_count)
        factor_out[...] = factor
        high, low = split(mapping)
        maps[0:128, :] = spread_map(high)
        maps[128:256, :] = spread_map(low)
        low_rows = lax.broadcasted_iota(jnp.int32, (M, 8, 256), 1) < 4

        def put(z, slot):
            return pltpu.make_async_copy(new.at[slot], out.at[:, z], sems.at[slot])

        def level(z, carry):
            slot = lax.rem(z, SLOTS)

            @pl.when(z >= SLOTS)
            def _():
                put(z - SLOTS, slot).wait()

            results = []
            for high, low in ((high_i, low_i), (high_e, low_e)):
                first = jnp.dot(maps[...], high[z], preferred_element_type=f32)
                second = jnp.dot(maps[0:128, :], low[z], preferred_element_type=f32)
                results.append((first[0:128] + first[128:256] + second).reshape(M, 8, 256))
            inner, edge = results
            new[slot, :, 0:8, :] = jnp.where(low_rows, edge, inner)
            new[slot, :, 8:16, :] = jnp.where(low_rows, inner, edge)
            put(z, slot).start()
            return carry

        lax.fori_loop(0, NZ, level, 0)
        for z in range(NZ - SLOTS, NZ):
            put(z, z % SLOTS).wait()

    return apply_kernel


def apply_map(sums, high_i, low_i, high_e, low_e, cell_count):
    return pl.pallas_call(
        make_apply_kernel(cell_count),
        out_shape=(
            jax.ShapeDtypeStruct((M, NZ, BX, 256), f32),
            jax.ShapeDtypeStruct((M, M), f32),
        ),
        in_specs=[VMEM] * 5,
        out_specs=(ANY, VMEM),
        scratch_shapes=[
            pltpu.VMEM((256, 256), bf16),
            pltpu.VMEM((SLOTS, M, BX, 256), f32),
            pltpu.SemaphoreType.DMA((SLOTS,)),
        ],
        compiler_params=params(12),
        cost_estimate=cost(10**9, 13 * 10**6),
        name="apply",
    )(sums, high_i, low_i, high_e, low_e)


def onward(value, axis):
    size = lax.axis_size(axis)
    return lax.ppermute(value, axis, [(i, i + 1) for i in range(size - 1)])


def backward(value, axis):
    size = lax.axis_size(axis)
    return lax.ppermute(value, axis, [(i + 1, i) for i in range(size - 1)])


def exchanged(value, axes, distance):
    size = lax.axis_size(axes)
    return lax.ppermute(value, axes, [(i, i ^ distance) for i in range(size)])


def shards(
    mean_field, mode_fields, velocity_east, velocity_north, flag_east, flag_north, ocean_mask
):
    axes = ("gx", "gy")
    (
        mean_field, mode_fields, velocity_east, velocity_north, flag_east, flag_north, ocean_mask
    ) = (
        pltpu.with_memory_space_constraint(value, pltpu.HBM)
        for value in (
            mean_field, mode_fields, velocity_east, velocity_north, flag_east, flag_north,
            ocean_mask,
        )
    )
    up, down, east_send, west_send, cells = pack(
        mode_fields, mean_field, velocity_east, velocity_north, flag_east, flag_north, ocean_mask
    )
    west = onward(east_send, "gy")
    east = backward(west_send, "gy")
    below = onward(up, "gx")
    above = backward(down, "gx")
    high_i, low_i, edge, weights, mean_part, sums_i = interior(
        cells, velocity_east, velocity_north, flag_east, flag_north, ocean_mask,
        west, east, east_send, west_send,
    )
    high_e, low_e, mean_next, sums = edges(below, above, edge, weights, mean_part, sums_i)
    for distance in (1, 2, 6, 8, 24, 32, 96):
        sums = sums + exchanged(sums, axes, distance)
    cell_count = float(NZ * BX * 256 * lax.axis_size("gx") * lax.axis_size("gy"))
    modes_next, factor = apply_map(sums, high_i, low_i, high_e, low_e, cell_count)
    return (mean_next, modes_next, factor)


def solution(mesh):
    plane = P(None, "gx", "gy")
    return jax.shard_map(
        shards,
        mesh=mesh,
        in_specs=(plane, P(None, None, "gx", "gy"), plane, plane, plane, plane, plane),
        out_specs=(plane, P(None, None, "gx", "gy"), P()),
        check_vma=False,
    )
```

```python
import jax
import jax.numpy as jnp
from jax import lax
from jax.experimental import pallas as pl
from jax.experimental.pallas import tpu as pltpu
from jax.sharding import PartitionSpec as P

time_step = 0.1
horiz_diff = 0.05
vert_diff = 0.2

M = 16
F = 17
NZ = 16
BX = 16
LANES = 128
ROWS = 3 * NZ
SLOTS = 4
TAIL = 8 + 8 * F
HIGH = lax.Precision.HIGHEST
f32 = jnp.float32
bf16 = jnp.bfloat16

ANY = pl.BlockSpec(memory_space=pl.ANY)
HBM = pl.BlockSpec(memory_space=pltpu.HBM)
VMEM = pl.BlockSpec(memory_space=pltpu.VMEM)


def params(mib):
    return pltpu.CompilerParams(vmem_limit_bytes=mib * 1024 * 1024)


def cost(flops, nbytes):
    return pl.CostEstimate(flops=flops, bytes_accessed=nbytes, transcendentals=0)


def rolled(value, shift, axis):
    shift = shift % value.shape[axis]
    return value if shift == 0 else pltpu.roll(value, shift, axis)


def lane_ids():
    return lax.broadcasted_iota(jnp.int32, (8, LANES), 1)


def row_ids():
    return lax.broadcasted_iota(jnp.int32, (8, LANES), 0)


def lane_half(ref, half):
    where = (slice(None),) * (len(ref.shape) - 1) + (pl.ds(LANES * half, LANES),)
    return ref.at[where]


def pack_rows(get, first_row):
    rows = row_ids()
    tiles = []
    for out in range(3):
        tile = None
        for z in range(8):
            low, high = max(3 * z, 8 * out), min(3 * z + 3, 8 * out + 8)
            if low >= high:
                continue
            piece = rolled(get(z), 3 * z - 8 * out - first_row, 0)
            tile = piece if tile is None else jnp.where(rows >= low - 8 * out, piece, tile)
        tiles.append(tile)
    return tiles


def pack_columns(get, shift_of):
    slot = lane_ids() // 4
    parts = [jnp.zeros((8, LANES), f32) for _ in range(4)]
    for k in range(2 * NZ):
        moved = rolled(get(k), shift_of(k), 1)
        parts[k % 4] = jnp.where(slot == k, moved, parts[k % 4])
    out = parts[0]
    for k in range(1, 4):
        out = jnp.where(slot % 4 == k, parts[k], out)
    return out


def pack_kernel(
    modes, mean, ve, vn, fe, fn, mask, up, down, east, west, X, V, I, sems
):
    copies = []
    for chunk in range(4):
        for half in range(2):
            copies.append(
                pltpu.make_async_copy(
                    lane_half(modes, half).at[pl.ds(4 * chunk, 4)],
                    X.at[half, pl.ds(4 * chunk, 4), :, pl.ds(8, BX)],
                    sems.at[len(copies)],
                )
            )
    for source, target in (
        (mean, lambda half: X.at[half, M, :, pl.ds(8, BX)]),
        (vn, lambda half: V.at[0, half]),
        (ve, lambda half: V.at[1, half]),
        (fn, lambda half: I.at[0, half]),
        (mask, lambda half: I.at[1, half]),
        (fe, lambda half: I.at[2, half]),
    ):
        for half in range(2):
            copies.append(
                pltpu.make_async_copy(lane_half(source, half), target(half), sems.at[len(copies)])
            )
    for copy in copies:
        copy.start()
    zero_tile = jnp.zeros((8, LANES), f32)

    def clear(f, carry):
        for half in range(2):
            for z in range(NZ):
                X[half, f, z, 0:8, :] = zero_tile
                X[half, f, z, 24:32, :] = zero_tile
        return carry

    lax.fori_loop(0, F, clear, 0, unroll=True)

    def field(f, carry):
        for half in range(2):
            for zh in range(2):
                for target, tile, first in ((up, 1, 5), (down, 0, 0)):
                    tiles = pack_rows(
                        lambda z: X[half, f, 8 * zh + z, 8 + 8 * tile : 16 + 8 * tile, :], first
                    )
                    for t in range(3):
                        target[half, f, zh, 8 * t : 8 * t + 8, :] = tiles[t]
        def tile_of(half):
            return lambda k: X[half, f, k // 2, 8 + 8 * (k % 2) : 16 + 8 * (k % 2), :]
        east[f] = pack_columns(tile_of(1), lambda k: 4 * k - 125)
        west[f] = pack_columns(tile_of(0), lambda k: 4 * k)
        return carry

    for chunk in range(4):
        copies[2 * chunk].wait()
        copies[2 * chunk + 1].wait()
        lax.fori_loop(4 * chunk, 4 * chunk + 4, field, 0, unroll=4)
    for copy in copies[8:]:
        copy.wait()
    lax.fori_loop(M, F, field, 0)
    for index, plane in enumerate(
        (
            lambda half, k: V[0, half, k // 2, 8 * (k % 2) : 8 * (k % 2) + 8, :],
            lambda half, k: I[0, half, k // 2, 8 * (k % 2) : 8 * (k % 2) + 8, :].astype(f32),
            lambda half, k: I[1, half, k // 2, 8 * (k % 2) : 8 * (k % 2) + 8, :].astype(f32),
        )
    ):
        east[F + index] = pack_columns(lambda k: plane(1, k), lambda k: 4 * k - 125)
        west[F + index] = pack_columns(lambda k: plane(0, k), lambda k: 4 * k)
    rows = row_ids()
    for half in range(2):
        for zh in range(2):

            def last_row(z):
                level = 8 * zh + z
                speed = rolled(V[1, half, level, 8:16, :], -2, 0)
                flag = rolled(I[2, half, level, 8:16, :].astype(f32), -1, 0)
                wet = I[1, half, level, 8:16, :].astype(f32)
                return jnp.where(rows == 5, speed, jnp.where(rows == 6, flag, wet))

            for target, get, first in (
                (up, last_row, 5),
                (down, lambda z: I[1, half, 8 * zh + z, 0:8, :].astype(f32), 0),
            ):
                tiles = pack_rows(get, first)
                for t in range(3):
                    target[half, F, zh, 8 * t : 8 * t + 8, :] = tiles[t]


def pack(modes, mean, ve, vn, fe, fn, mask):
    rows = jax.ShapeDtypeStruct((2, F + 1, 2, ROWS // 2, LANES), f32)
    columns = jax.ShapeDtypeStruct((F + 3, 8, LANES), f32)
    return pl.pallas_call(
        pack_kernel,
        out_shape=(
            rows,
            rows,
            columns,
            columns,
            jax.ShapeDtypeStruct((2, F, NZ, 32, LANES), f32),
        ),
        in_specs=[HBM] * 7,
        out_specs=(VMEM,) * 5,
        scratch_shapes=[
            pltpu.VMEM((2, 2, NZ, BX, LANES), f32),
            pltpu.VMEM((3, 2, NZ, BX, LANES), jnp.int32),
            pltpu.SemaphoreType.DMA((20,)),
        ],
        compiler_params=params(24),
        cost_estimate=cost(10**7, 7 * 10**6),
        name="pack",
    )(modes, mean, ve, vn, fe, fn, mask)


def along_lanes(first, second, outer, offset):
    lanes = lane_ids()
    a, b, c = (rolled(v, -offset, 1) for v in (first, second, outer))
    if offset > 0:
        inside = lanes < LANES - offset
        return jnp.where(inside, a, b), jnp.where(inside, b, c)
    outside = lanes < -offset
    return jnp.where(outside, c, a), jnp.where(outside, a, b)


def around_lanes(first, second, offset):
    lanes = lane_ids()
    a, b = (rolled(v, -offset, 1) for v in (first, second))
    kept = lanes < LANES - offset if offset > 0 else lanes >= -offset
    return jnp.where(kept, a, b), jnp.where(kept, b, a)


def cell_weights(a_low, b_low, d_low, a_high, b_high, d_high):
    return (
        2.0 * a_low,
        -13.0 * a_low - 3.0 * b_low - 2.0 * a_high,
        47.0 * a_low + 27.0 * b_low + d_low + 13.0 * a_high + 3.0 * b_high,
        27.0 * a_low + 47.0 * b_low - d_low - 47.0 * a_high - 27.0 * b_high - d_high,
        -3.0 * a_low - 13.0 * b_low - 27.0 * a_high - 47.0 * b_high + d_high,
        2.0 * b_low + 3.0 * a_high + 13.0 * b_high,
        -2.0 * b_high,
    )


def face_parts(openness, speed, flag):
    scaled = openness * speed * (1.0 / 60.0)
    return scaled * flag, scaled * (1.0 - flag), horiz_diff * openness


def split(value):
    high = value.astype(bf16)
    return high, (value - high.astype(f32)).astype(bf16)


def add_products(acc, high, low):
    dims = (((1,), (1,)), ((), ()))
    acc[0:256, :] += lax.dot_general(high, high, dims, preferred_element_type=f32)
    acc[256:512, :] += lax.dot_general(low, high, dims, preferred_element_type=f32)


def joined(parts):
    return jnp.concatenate([parts[z] for z in range(NZ)], axis=1)


def field_sums(acc):
    rows = lax.broadcasted_iota(jnp.int32, (512, 256), 0)
    columns = lax.broadcasted_iota(jnp.int32, (512, 256), 1)
    kept = jnp.where(rows % 8 == columns % 8, acc[...], 0.0)
    by_row = jnp.sum(kept.reshape(64, 8, 256), axis=1)
    gather = (
        lax.broadcasted_iota(jnp.int32, (256, 32), 0) // 8
        == lax.broadcasted_iota(jnp.int32, (256, 32), 1)
    ).astype(f32)
    return jnp.dot(by_row, gather, precision=HIGH, preferred_element_type=f32)


def interior_kernel(
    X, ve, vn, fe, fn, mask, west, east, own_last, own_first,
    high_out, low_out, edge_out, weights_out, mean_out, sums_out,
    VE, FE, W, VN, FN, H, C, G, T, Z, acc, sems,
):
    zero_tile = jnp.zeros((8, LANES), f32)
    for half in range(2):
        for z in range(NZ):
            edge_out[z, half, 0:8, :] = zero_tile
    for half in range(2):
        for z in range(NZ):
            VE[half, z, 0:8, :] = zero_tile
            FE[half, z, 0:8, :] = zero_tile
            W[half, z, 0:8, :] = zero_tile.astype(jnp.int32)
            W[half, z, 24:32, :] = zero_tile.astype(jnp.int32)
    acc[...] = jnp.zeros((512, 256), f32)
    lanes = lane_ids()
    rows = row_ids()

    copies = []
    body = pl.ds(8, BX)
    for half in range(2):
        for source, target in (
            (ve, VE.at[half, :, body]),
            (mask, W.at[half, :, body]),
            (vn, VN.at[half]),
            (fn, FN.at[0, half]),
            (fe, FN.at[1, half]),
        ):
            copies.append(
                pltpu.make_async_copy(lane_half(source, half), target, sems.at[len(copies)])
            )
    for copy in copies:
        copy.start()

    for f in range(F, F + 3):
        after, before = east[f], west[f]
        for k in range(2 * NZ):
            H[f - F, k] = jnp.where(
                lanes < 64, rolled(after, -4 * k, 1), rolled(before, LANES - 3 - 4 * k, 1)
            )

    place = lanes % 4

    (v_in, f_in, w_in) = (west[F + i] for i in range(3))
    (v_own, f_own, w_own) = (own_first[F + i] for i in range(3))
    lower_of = lambda outer_plane, own: jnp.where(
        place == 0, rolled(outer_plane, -2, 1), rolled(own, 1, 1)
    )
    low_face = face_parts(
        lower_of(w_in, w_own) * w_own, lower_of(v_in, v_own), lower_of(f_in, f_own)
    )
    high_face = face_parts(w_own * rolled(w_own, -1, 1), v_own, f_own)
    first_gains = cell_weights(*low_face, *high_face)
    for d in range(1, 4):
        G[d - 1] = jnp.where(place < d, first_gains[3 - d], 0.0)
    w_next = east[F + 2]
    (v_own, f_own, w_own) = (own_last[F + i] for i in range(3))
    high_face = face_parts(
        w_own * jnp.where(place == 2, rolled(w_next, 2, 1), rolled(w_own, -1, 1)), v_own, f_own
    )
    low_face = tuple(rolled(part, 1, 1) for part in high_face)
    last_gains = cell_weights(*low_face, *high_face)
    for d in range(1, 4):
        G[2 + d] = jnp.where((place >= 3 - d) & (place < 3), last_gains[3 + d], 0.0)

    def beside(f):
        before, after = west[f], east[f]
        first = (
            G[0] * rolled(before, -2, 1) + G[1] * rolled(before, -1, 1) + G[2] * before
        )
        last = G[3] * rolled(after, 2, 1) + G[4] * rolled(after, 1, 1) + G[5] * after
        C[0, f] = first
        C[1, f] = rolled(last, LANES - 3, 1)

    for f in range(F):
        beside(f)
    for copy in copies:
        copy.wait()

    def level(z, carry):
        z_up = jnp.minimum(z + 1, NZ - 1)
        z_down = jnp.maximum(z - 1, 0)
        for half in range(2):
            for xt in range(2):
                FE[half, z, 8 + 8 * xt : 16 + 8 * xt, :] = FN[
                    1, half, z, 8 * xt : 8 * xt + 8, :
                ].astype(f32)
        for xt in range(2):
            start = 8 + 8 * xt

            def outer(index):
                return H[index - F, 2 * z + xt]

            def at(ref, half, offset):
                return ref[half, z, start + offset : start + offset + 8, :]

            wet = [at(W, half, 0).astype(f32) for half in range(2)]
            wx = []
            for half in range(2):
                before = wet[half] * at(W, half, -1).astype(f32)
                after = wet[half] * at(W, half, 1).astype(f32)
                wx.append(
                    cell_weights(
                        *face_parts(before, at(VE, half, -1), at(FE, half, -1)),
                        *face_parts(after, at(VE, half, 0), at(FE, half, 0)),
                    )
                )
            wet_out = outer(F + 2)
            following = along_lanes(wet[0], wet[1], wet_out, 1)
            own = [
                face_parts(
                    wet[half] * following[half],
                    VN[half, z, 8 * xt : 8 * xt + 8, :],
                    FN[0, half, z, 8 * xt : 8 * xt + 8, :].astype(f32),
                )
                for half in range(2)
            ]
            beyond = face_parts(wet_out * rolled(wet[0], -1, 1), outer(F), outer(F + 1))
            before = [along_lanes(own[0][i], own[1][i], beyond[i], -1) for i in range(3)]
            wy = [
                cell_weights(*(before[i][half] for i in range(3)), *own[half]) for half in range(2)
            ]
            wy = [
                [
                    jnp.where(
                        (lanes < 3 - j) if half == 0 else (lanes >= LANES + 3 - j), 0.0, wy[half][j]
                    )
                    if (half == 0) == (j < 3) and j != 3
                    else wy[half][j]
                    for j in range(7)
                ]
                for half in range(2)
            ]
            centre = [
                wx[half][3] + wy[half][3] - 2.0 * vert_diff * wet[half] for half in range(2)
            ]
            w_level = [vert_diff * wet[half] for half in range(2)]
            for half in range(2):
                for index, plane in enumerate((at(VE, half, 0), at(FE, half, 0), wet[half])):
                    if xt == 0:
                        weights_out[half, z, 3 + index] = plane
                    else:
                        weights_out[half, z, 3 + index] = jnp.where(
                            rows < 4, weights_out[half, z, 3 + index], plane
                        )
                for d in range(1, 4):
                    if xt == 0:
                        weights_out[half, z, d - 1] = jnp.where(rows < d, wx[half][3 - d], 0.0)
                    else:
                        weights_out[half, z, d - 1] += jnp.where(
                            rows >= 8 - d, wx[half][3 + d], 0.0
                        )
            for f in range(F):
                own_cells = [X[half, f, z, start : start + 8, :] for half in range(2)]
                total = [
                    centre[half] * own_cells[half]
                    + w_level[half]
                    * (
                        X[half, f, z_up, start : start + 8, :]
                        + X[half, f, z_down, start : start + 8, :]
                    )
                    for half in range(2)
                ]
                first, last = C[0, f], C[1, f]
                total[0] += jnp.where(lanes < 3, first, 0.0)
                total[1] += jnp.where(lanes >= LANES - 3, last, 0.0)
                C[0, f] = rolled(first, -4, 1)
                C[1, f] = rolled(last, -4, 1)
                for offset in (-3, -2, -1, 1, 2, 3):
                    moved = around_lanes(own_cells[0], own_cells[1], offset)
                    for half in range(2):
                        total[half] += wx[half][3 + offset] * X[
                            half, f, z, start + offset : start + offset + 8, :
                        ]
                        total[half] += wy[half][3 + offset] * moved[half]
                for half in range(2):
                    columns = slice(LANES * half, LANES * half + LANES)
                    low_rows = rows < 4
                    if xt == 1:
                        cells = X[half, f, z, 8:16, :]
                        edge_out[z, half, 8 + 8 * f : 16 + 8 * f, :] = jnp.where(
                            low_rows, cells, own_cells[half]
                        )
                    if f == M:
                        mean_out[z, 8 * xt : 8 * xt + 8, columns] = (
                            own_cells[half] + time_step * total[half]
                        )
                    elif xt == 0:
                        T[half, f] = total[half]
                    else:
                        near = T[half, f]
                        Z[8 * f : 8 * f + 8, columns] = jnp.where(
                            low_rows, own_cells[half], cells
                        )
                        Z[128 + 8 * f : 136 + 8 * f, columns] = jnp.where(
                            low_rows, total[half], near
                        )
                        place = slice(TAIL + 8 * f, TAIL + 8 * f + 8)
                        edge_out[z, half, place, :] = jnp.where(low_rows, near, total[half])
        high, low = split(Z[...])
        high_out[z] = high
        low_out[z] = low
        return carry

    lax.fori_loop(0, NZ, level, 0)
    add_products(acc, joined(high_out), joined(low_out))
    sums_out[...] = field_sums(acc)


def interior(cells, ve, vn, fe, fn, mask, west, east, own_last, own_first):
    parts = jax.ShapeDtypeStruct((NZ, 256, 256), bf16)
    return pl.pallas_call(
        interior_kernel,
        out_shape=(
            parts,
            parts,
            jax.ShapeDtypeStruct((NZ, 2, TAIL + 8 * M, LANES), f32),
            jax.ShapeDtypeStruct((2, NZ, 6, 8, LANES), f32),
            jax.ShapeDtypeStruct(ve.shape, f32),
            jax.ShapeDtypeStruct((64, 32), f32),
        ),
        in_specs=[VMEM] + [HBM] * 5 + [VMEM] * 4,
        out_specs=(VMEM,) * 6,
        scratch_shapes=[
            pltpu.VMEM((2, NZ, 32, LANES), f32),
            pltpu.VMEM((2, NZ, 32, LANES), f32),
            pltpu.VMEM((2, NZ, 32, LANES), jnp.int32),
            pltpu.VMEM((2, NZ, BX, LANES), f32),
            pltpu.VMEM((2, 2, NZ, BX, LANES), jnp.int32),
            pltpu.VMEM((3, 2 * NZ, 8, LANES), f32),
            pltpu.VMEM((2, F, 8, LANES), f32),
            pltpu.VMEM((6, 8, LANES), f32),
            pltpu.VMEM((2, M, 8, LANES), f32),
            pltpu.VMEM((256, 256), f32),
            pltpu.VMEM((512, 256), f32),
            pltpu.SemaphoreType.DMA((10,)),
        ],
        compiler_params=params(28),
        cost_estimate=cost(10**10, 4 * 10**7),
        name="interior",
    )(cells, ve, vn, fe, fn, mask, west, east, own_last, own_first)


def edge_kernel(
    below, above, edge_in, weights, mean_in, sums_in,
    high_out, low_out, mean_out, sums_out, Z, acc,
):
    acc[...] = jnp.zeros((512, 256), f32)
    rows = row_ids()
    low_rows = rows < 4
    first_row = rows == 0
    last_row = rows == 7

    def rows_from(ref, half, f, zh, first):
        start = min(max(first, 0), 16)
        return rolled(ref[half, f, zh, start : start + 8, :], start - first, 0)

    def gains_of(half, z, zh, zi):
        speed, flag, wet = (weights[half, z, 3 + i] for i in range(3))
        speed = jnp.where(first_row, rows_from(below, half, F, zh, 3 * zi), speed)
        flag = jnp.where(first_row, rows_from(below, half, F, zh, 3 * zi + 1), flag)
        beyond = jnp.where(first_row, rows_from(below, half, F, zh, 3 * zi + 2), 0.0)
        beyond = jnp.where(last_row, rows_from(above, half, F, zh, 3 * zi - 7), beyond)
        a, b, d = face_parts(beyond * wet, speed, flag)
        near, far = 47.0 * a + 27.0 * b + d, 27.0 * a + 47.0 * b - d
        left, right = -13.0 * a - 3.0 * b, -3.0 * a - 13.0 * b
        outside = (
            weights[half, z, 0] + jnp.where(first_row, near, -far),
            weights[half, z, 1] + jnp.where(first_row, left, -right),
            weights[half, z, 2] + jnp.where(first_row, 2.0 * a, -2.0 * b),
        )
        inside = (
            jnp.where(first_row, far, -near),
            jnp.where(first_row, right, -left),
            jnp.where(first_row, 2.0 * b, -2.0 * a),
        )
        return outside, inside

    def group(zh, carry):
        for zi in range(8):
            z = 8 * zh + zi
            for half in range(2):
                outside, inside = gains_of(half, z, zh, zi)
                for f in range(F):
                    base = 8 + 8 * f
                    change = inside[0] * edge_in[z, half, base : base + 8, :]
                    for d in range(1, 4):
                        cells = jnp.where(
                            low_rows,
                            rows_from(below, half, f, zh, 3 * zi + 3 - d),
                            rows_from(above, half, f, zh, 3 * zi + d - 8),
                        )
                        change = change + outside[d - 1] * cells
                    for d in range(1, 3):
                        cells = jnp.where(
                            low_rows,
                            edge_in[z, half, base + d : base + d + 8, :],
                            edge_in[z, half, base - d : base - d + 8, :],
                        )
                        change = change + inside[d] * cells
                    if f < M:
                        Z[half, 8 * f : 8 * f + 8, :] = (
                            edge_in[z, half, TAIL + 8 * f : TAIL + 8 * f + 8, :] + change
                        )
                    else:
                        columns = slice(LANES * half, LANES * half + LANES)
                        step = time_step * change
                        mean_out[z, 0:8, columns] = mean_in[z, 0:8, columns] + jnp.where(
                            low_rows, step, 0.0
                        )
                        mean_out[z, 8:16, columns] = mean_in[z, 8:16, columns] + jnp.where(
                            low_rows, 0.0, step
                        )
            halves = [
                jnp.concatenate([edge_in[z, half, 8 : 8 + 8 * M, :], Z[half]], axis=0)
                for half in range(2)
            ]
            high, low = split(jnp.concatenate(halves, axis=1))
            high_out[z] = high
            low_out[z] = low
            add_products(acc, high, low)
        return carry

    lax.fori_loop(0, 2, group, 0)
    sums = sums_in[...] + field_sums(acc)
    identity = (
        lax.broadcasted_iota(jnp.int32, (32, 32), 0) == lax.broadcasted_iota(jnp.int32, (32, 32), 1)
    ).astype(f32)
    turned = lax.dot_general(
        identity, sums[32:64], (((1,), (1,)), ((), ())), precision=HIGH, preferred_element_type=f32
    )
    sums_out[...] = sums[0:32] + sums[32:64] + turned


def edges(below, above, edge_in, weights, mean_in, sums_in):
    parts = jax.ShapeDtypeStruct((NZ, 256, 256), bf16)
    return pl.pallas_call(
        edge_kernel,
        out_shape=(
            parts,
            parts,
            jax.ShapeDtypeStruct(mean_in.shape, f32),
            jax.ShapeDtypeStruct((32, 32), f32),
        ),
        in_specs=[VMEM] * 6,
        out_specs=(VMEM,) * 4,
        scratch_shapes=[
            pltpu.VMEM((2, 8 * M, LANES), f32),
            pltpu.VMEM((512, 256), f32),
        ],
        compiler_params=params(16),
        cost_estimate=cost(10**9, 10**7),
        name="edges",
    )(below, above, edge_in, weights, mean_in, sums_in)


def factor_and_map(sums, cell_count):
    inner = sums * (1.0 / cell_count)
    row = lax.broadcasted_iota(jnp.int32, (M, 2 * M), 0)
    column = lax.broadcasted_iota(jnp.int32, (M, 2 * M), 1)
    update = jnp.where(
        column < M,
        jnp.where(column == row, 1.0, 0.0) - time_step * inner[M : 2 * M, :],
        jnp.where(column == row + M, time_step, 0.0),
    )
    half_way = jnp.dot(update, inner, precision=HIGH, preferred_element_type=f32)
    gram = lax.dot_general(
        half_way, update, (((1,), (1,)), ((), ())), precision=HIGH, preferred_element_type=f32
    )
    row_g = lax.broadcasted_iota(jnp.int32, (M, M), 0)
    column_g = lax.broadcasted_iota(jnp.int32, (M, M), 1)
    left, right = gram, update
    for j in range(M):
        pivot = jnp.sum(jnp.where(column_g == j, left, 0.0), axis=1, keepdims=True)
        scale = 1.0 / jnp.sqrt(pivot[j : j + 1, :])
        left_row = left[j : j + 1, :] * scale
        right_row = right[j : j + 1, :] * scale
        share = jnp.where(row_g[:, 0:1] > j, pivot * scale, 0.0)
        left = jnp.where(row_g == j, left_row, left - share * left_row)
        right = jnp.where(row == j, right_row, right - share * right_row)
    return jnp.where(column_g >= row_g, left, 0.0), right


def spread_map(mapping):
    parts = jnp.concatenate(split(mapping), axis=0)
    tall = (
        lax.broadcasted_iota(jnp.int32, (256, 2 * M), 0) // 8
        == lax.broadcasted_iota(jnp.int32, (256, 2 * M), 1)
    ).astype(bf16)
    wide = (
        lax.broadcasted_iota(jnp.int32, (2 * M, 256), 1) // 8
        == lax.broadcasted_iota(jnp.int32, (2 * M, 256), 0)
    ).astype(bf16)
    rows = jnp.dot(tall, parts, preferred_element_type=f32).astype(bf16)
    full = jnp.dot(rows, wide, preferred_element_type=f32)
    row = lax.broadcasted_iota(jnp.int32, (256, 256), 0)
    column = lax.broadcasted_iota(jnp.int32, (256, 256), 1)
    return jnp.where(row % 8 == column % 8, full, 0.0).astype(bf16)


def make_apply_kernel(cell_count):
    def apply_kernel(sums, high_i, low_i, high_e, low_e, out, factor_out, maps, new, sems):
        factor, mapping = factor_and_map(sums[...], cell_count)
        factor_out[...] = factor
        maps[...] = spread_map(mapping)
        low_rows = lax.broadcasted_iota(jnp.int32, (M, 8, 256), 1) < 4

        def put(z, slot):
            return pltpu.make_async_copy(new.at[slot], out.at[:, z], sems.at[slot])

        def level(z, carry):
            slot = lax.rem(z, SLOTS)

            @pl.when(z >= SLOTS)
            def _():
                put(z - SLOTS, slot).wait()

            results = []
            for high, low in ((high_i, low_i), (high_e, low_e)):
                first = jnp.dot(maps[...], high[z], preferred_element_type=f32)
                second = jnp.dot(maps[0:128, :], low[z], preferred_element_type=f32)
                results.append((first[0:128] + first[128:256] + second).reshape(M, 8, 256))
            inner, edge = results
            new[slot, :, 0:8, :] = jnp.where(low_rows, edge, inner)
            new[slot, :, 8:16, :] = jnp.where(low_rows, inner, edge)
            put(z, slot).start()
            return carry

        lax.fori_loop(0, NZ, level, 0)
        for z in range(NZ - SLOTS, NZ):
            put(z, z % SLOTS).wait()

    return apply_kernel


def apply_map(sums, high_i, low_i, high_e, low_e, cell_count):
    return pl.pallas_call(
        make_apply_kernel(cell_count),
        out_shape=(
            jax.ShapeDtypeStruct((M, NZ, BX, 256), f32),
            jax.ShapeDtypeStruct((M, M), f32),
        ),
        in_specs=[VMEM] * 5,
        out_specs=(ANY, VMEM),
        scratch_shapes=[
            pltpu.VMEM((256, 256), bf16),
            pltpu.VMEM((SLOTS, M, BX, 256), f32),
            pltpu.SemaphoreType.DMA((SLOTS,)),
        ],
        compiler_params=params(12),
        cost_estimate=cost(10**9, 13 * 10**6),
        name="apply",
    )(sums, high_i, low_i, high_e, low_e)


def onward(value, axis):
    size = lax.axis_size(axis)
    return lax.ppermute(value, axis, [(i, i + 1) for i in range(size - 1)])


def backward(value, axis):
    size = lax.axis_size(axis)
    return lax.ppermute(value, axis, [(i + 1, i) for i in range(size - 1)])


def exchanged(value, axes, distance):
    size = lax.axis_size(axes)
    return lax.ppermute(value, axes, [(i, i ^ distance) for i in range(size)])


def shards(
    mean_field, mode_fields, velocity_east, velocity_north, flag_east, flag_north, ocean_mask
):
    axes = ("gx", "gy")
    (
        mean_field, mode_fields, velocity_east, velocity_north, flag_east, flag_north, ocean_mask
    ) = (
        pltpu.with_memory_space_constraint(value, pltpu.HBM)
        for value in (
            mean_field, mode_fields, velocity_east, velocity_north, flag_east, flag_north,
            ocean_mask,
        )
    )
    up, down, east_send, west_send, cells = pack(
        mode_fields, mean_field, velocity_east, velocity_north, flag_east, flag_north, ocean_mask
    )
    west = onward(east_send, "gy")
    east = backward(west_send, "gy")
    below = onward(up, "gx")
    above = backward(down, "gx")
    high_i, low_i, edge, weights, mean_part, sums_i = interior(
        cells, velocity_east, velocity_north, flag_east, flag_north, ocean_mask,
        west, east, east_send, west_send,
    )
    high_e, low_e, mean_next, sums = edges(below, above, edge, weights, mean_part, sums_i)
    for distance in (1, 2, 6, 8, 24, 32, 96):
        sums = sums + exchanged(sums, axes, distance)
    cell_count = float(NZ * BX * 256 * lax.axis_size("gx") * lax.axis_size("gy"))
    modes_next, factor = apply_map(sums, high_i, low_i, high_e, low_e, cell_count)
    return (mean_next, modes_next, factor)


def solution(mesh):
    plane = P(None, "gx", "gy")
    return jax.shard_map(
        shards,
        mesh=mesh,
        in_specs=(plane, P(None, None, "gx", "gy"), plane, plane, plane, plane, plane),
        out_specs=(plane, P(None, None, "gx", "gy"), P()),
        check_vma=False,
    )
```

```python
import jax
import jax.numpy as jnp
from jax import lax
from jax.experimental import pallas as pl
from jax.experimental.pallas import tpu as pltpu
from jax.sharding import PartitionSpec as P

time_step = 0.1
horiz_diff = 0.05
vert_diff = 0.2

M = 16
F = 17
NZ = 16
BX = 16
LANES = 128
ROWS = 3 * NZ
SLOTS = 4
TAIL = 8 + 8 * F
HIGH = lax.Precision.HIGHEST
f32 = jnp.float32
bf16 = jnp.bfloat16

ANY = pl.BlockSpec(memory_space=pl.ANY)
HBM = pl.BlockSpec(memory_space=pltpu.HBM)
VMEM = pl.BlockSpec(memory_space=pltpu.VMEM)


def params(mib):
    return pltpu.CompilerParams(vmem_limit_bytes=mib * 1024 * 1024)


def cost(flops, nbytes):
    return pl.CostEstimate(flops=flops, bytes_accessed=nbytes, transcendentals=0)


def rolled(value, shift, axis):
    shift = shift % value.shape[axis]
    return value if shift == 0 else pltpu.roll(value, shift, axis)


def lane_ids():
    return lax.broadcasted_iota(jnp.int32, (8, LANES), 1)


def row_ids():
    return lax.broadcasted_iota(jnp.int32, (8, LANES), 0)


def lane_half(ref, half):
    where = (slice(None),) * (len(ref.shape) - 1) + (pl.ds(LANES * half, LANES),)
    return ref.at[where]


def pack_rows(get, first_row):
    rows = row_ids()
    tiles = []
    for out in range(3):
        tile = None
        for z in range(8):
            low, high = max(3 * z, 8 * out), min(3 * z + 3, 8 * out + 8)
            if low >= high:
                continue
            piece = rolled(get(z), 3 * z - 8 * out - first_row, 0)
            tile = piece if tile is None else jnp.where(rows >= low - 8 * out, piece, tile)
        tiles.append(tile)
    return tiles


def pack_columns(get, shift_of):
    slot = lane_ids() // 4
    parts = [jnp.zeros((8, LANES), f32) for _ in range(4)]
    for k in range(2 * NZ):
        moved = rolled(get(k), shift_of(k), 1)
        parts[k % 4] = jnp.where(slot == k, moved, parts[k % 4])
    out = parts[0]
    for k in range(1, 4):
        out = jnp.where(slot % 4 == k, parts[k], out)
    return out


def pack_kernel(
    modes, mean, ve, vn, fe, fn, mask, up, down, east, west, X, V, I, sems
):
    copies = []
    for chunk in range(4):
        for half in range(2):
            copies.append(
                pltpu.make_async_copy(
                    lane_half(modes, half).at[pl.ds(4 * chunk, 4)],
                    X.at[half, pl.ds(4 * chunk, 4), :, pl.ds(8, BX)],
                    sems.at[len(copies)],
                )
            )
    for source, target in (
        (mean, lambda half: X.at[half, M, :, pl.ds(8, BX)]),
        (vn, lambda half: V.at[0, half]),
        (ve, lambda half: V.at[1, half]),
        (fn, lambda half: I.at[0, half]),
        (mask, lambda half: I.at[1, half]),
        (fe, lambda half: I.at[2, half]),
    ):
        for half in range(2):
            copies.append(
                pltpu.make_async_copy(lane_half(source, half), target(half), sems.at[len(copies)])
            )
    for copy in copies:
        copy.start()
    zero_tile = jnp.zeros((8, LANES), f32)

    def clear(f, carry):
        for half in range(2):
            for z in range(NZ):
                X[half, f, z, 0:8, :] = zero_tile
                X[half, f, z, 24:32, :] = zero_tile
        return carry

    lax.fori_loop(0, F, clear, 0, unroll=True)

    def field(f, carry):
        for half in range(2):
            for zh in range(2):
                for target, tile, first in ((up, 1, 5), (down, 0, 0)):
                    tiles = pack_rows(
                        lambda z: X[half, f, 8 * zh + z, 8 + 8 * tile : 16 + 8 * tile, :], first
                    )
                    for t in range(3):
                        target[half, f, zh, 8 * t : 8 * t + 8, :] = tiles[t]
        def tile_of(half):
            return lambda k: X[half, f, k // 2, 8 + 8 * (k % 2) : 16 + 8 * (k % 2), :]
        east[f] = pack_columns(tile_of(1), lambda k: 4 * k - 125)
        west[f] = pack_columns(tile_of(0), lambda k: 4 * k)
        return carry

    for chunk in range(4):
        copies[2 * chunk].wait()
        copies[2 * chunk + 1].wait()
        lax.fori_loop(4 * chunk, 4 * chunk + 4, field, 0, unroll=4)
    for copy in copies[8:]:
        copy.wait()
    lax.fori_loop(M, F, field, 0)
    for index, plane in enumerate(
        (
            lambda half, k: V[0, half, k // 2, 8 * (k % 2) : 8 * (k % 2) + 8, :],
            lambda half, k: I[0, half, k // 2, 8 * (k % 2) : 8 * (k % 2) + 8, :].astype(f32),
            lambda half, k: I[1, half, k // 2, 8 * (k % 2) : 8 * (k % 2) + 8, :].astype(f32),
        )
    ):
        east[F + index] = pack_columns(lambda k: plane(1, k), lambda k: 4 * k - 125)
        west[F + index] = pack_columns(lambda k: plane(0, k), lambda k: 4 * k)
    rows = row_ids()
    for half in range(2):
        for zh in range(2):

            def last_row(z):
                level = 8 * zh + z
                speed = rolled(V[1, half, level, 8:16, :], -2, 0)
                flag = rolled(I[2, half, level, 8:16, :].astype(f32), -1, 0)
                wet = I[1, half, level, 8:16, :].astype(f32)
                return jnp.where(rows == 5, speed, jnp.where(rows == 6, flag, wet))

            for target, get, first in (
                (up, last_row, 5),
                (down, lambda z: I[1, half, 8 * zh + z, 0:8, :].astype(f32), 0),
            ):
                tiles = pack_rows(get, first)
                for t in range(3):
                    target[half, F, zh, 8 * t : 8 * t + 8, :] = tiles[t]


def pack(modes, mean, ve, vn, fe, fn, mask):
    rows = jax.ShapeDtypeStruct((2, F + 1, 2, ROWS // 2, LANES), f32)
    columns = jax.ShapeDtypeStruct((F + 3, 8, LANES), f32)
    return pl.pallas_call(
        pack_kernel,
        out_shape=(
            rows,
            rows,
            columns,
            columns,
            jax.ShapeDtypeStruct((2, F, NZ, 32, LANES), f32),
        ),
        in_specs=[HBM] * 7,
        out_specs=(VMEM,) * 5,
        scratch_shapes=[
            pltpu.VMEM((2, 2, NZ, BX, LANES), f32),
            pltpu.VMEM((3, 2, NZ, BX, LANES), jnp.int32),
            pltpu.SemaphoreType.DMA((20,)),
        ],
        compiler_params=params(24),
        cost_estimate=cost(10**7, 7 * 10**6),
        name="pack",
    )(modes, mean, ve, vn, fe, fn, mask)


def along_lanes(first, second, outer, offset):
    lanes = lane_ids()
    a, b, c = (rolled(v, -offset, 1) for v in (first, second, outer))
    if offset > 0:
        inside = lanes < LANES - offset
        return jnp.where(inside, a, b), jnp.where(inside, b, c)
    outside = lanes < -offset
    return jnp.where(outside, c, a), jnp.where(outside, a, b)


def around_lanes(first, second, offset):
    lanes = lane_ids()
    a, b = (rolled(v, -offset, 1) for v in (first, second))
    kept = lanes < LANES - offset if offset > 0 else lanes >= -offset
    return jnp.where(kept, a, b), jnp.where(kept, b, a)


def cell_weights(a_low, b_low, d_low, a_high, b_high, d_high):
    return (
        2.0 * a_low,
        -13.0 * a_low - 3.0 * b_low - 2.0 * a_high,
        47.0 * a_low + 27.0 * b_low + d_low + 13.0 * a_high + 3.0 * b_high,
        27.0 * a_low + 47.0 * b_low - d_low - 47.0 * a_high - 27.0 * b_high - d_high,
        -3.0 * a_low - 13.0 * b_low - 27.0 * a_high - 47.0 * b_high + d_high,
        2.0 * b_low + 3.0 * a_high + 13.0 * b_high,
        -2.0 * b_high,
    )


def face_parts(openness, speed, flag):
    scaled = openness * speed * (1.0 / 60.0)
    return scaled * flag, scaled * (1.0 - flag), horiz_diff * openness


def split(value):
    high = value.astype(bf16)
    return high, (value - high.astype(f32)).astype(bf16)


def add_products(acc, high, low):
    dims = (((1,), (1,)), ((), ()))
    acc[0:256, :] += lax.dot_general(high, high, dims, preferred_element_type=f32)
    acc[256:512, :] += lax.dot_general(low, high, dims, preferred_element_type=f32)


def joined(parts):
    return jnp.concatenate([parts[z] for z in range(NZ)], axis=1)


def field_sums(acc):
    rows = lax.broadcasted_iota(jnp.int32, (512, 256), 0)
    columns = lax.broadcasted_iota(jnp.int32, (512, 256), 1)
    kept = jnp.where(rows % 8 == columns % 8, acc[...], 0.0)
    by_row = jnp.sum(kept.reshape(64, 8, 256), axis=1)
    gather = (
        lax.broadcasted_iota(jnp.int32, (256, 32), 0) // 8
        == lax.broadcasted_iota(jnp.int32, (256, 32), 1)
    ).astype(f32)
    return jnp.dot(by_row, gather, precision=HIGH, preferred_element_type=f32)


def interior_kernel(
    X, ve, vn, fe, fn, mask, west, east, own_last, own_first,
    high_out, low_out, edge_out, weights_out, mean_out, sums_out,
    VE, FE, W, VN, FN, H, C, G, T, Z, acc, sems,
):
    zero_tile = jnp.zeros((8, LANES), f32)
    for half in range(2):
        for z in range(NZ):
            edge_out[z, half, 0:8, :] = zero_tile
    for half in range(2):
        for z in range(NZ):
            VE[half, z, 0:8, :] = zero_tile
            FE[half, z, 0:8, :] = zero_tile
            W[half, z, 0:8, :] = zero_tile.astype(jnp.int32)
            W[half, z, 24:32, :] = zero_tile.astype(jnp.int32)
    acc[...] = jnp.zeros((512, 256), f32)
    lanes = lane_ids()
    rows = row_ids()

    copies = []
    body = pl.ds(8, BX)
    for half in range(2):
        for source, target in (
            (ve, VE.at[half, :, body]),
            (mask, W.at[half, :, body]),
            (vn, VN.at[half]),
            (fn, FN.at[0, half]),
            (fe, FN.at[1, half]),
        ):
            copies.append(
                pltpu.make_async_copy(lane_half(source, half), target, sems.at[len(copies)])
            )
    for copy in copies:
        copy.start()

    for f in range(F, F + 3):
        after, before = east[f], west[f]
        for k in range(2 * NZ):
            H[f - F, k] = jnp.where(
                lanes < 64, rolled(after, -4 * k, 1), rolled(before, LANES - 3 - 4 * k, 1)
            )

    place = lanes % 4

    (v_in, f_in, w_in) = (west[F + i] for i in range(3))
    (v_own, f_own, w_own) = (own_first[F + i] for i in range(3))
    lower_of = lambda outer_plane, own: jnp.where(
        place == 0, rolled(outer_plane, -2, 1), rolled(own, 1, 1)
    )
    low_face = face_parts(
        lower_of(w_in, w_own) * w_own, lower_of(v_in, v_own), lower_of(f_in, f_own)
    )
    high_face = face_parts(w_own * rolled(w_own, -1, 1), v_own, f_own)
    first_gains = cell_weights(*low_face, *high_face)
    for d in range(1, 4):
        G[d - 1] = jnp.where(place < d, first_gains[3 - d], 0.0)
    w_next = east[F + 2]
    (v_own, f_own, w_own) = (own_last[F + i] for i in range(3))
    high_face = face_parts(
        w_own * jnp.where(place == 2, rolled(w_next, 2, 1), rolled(w_own, -1, 1)), v_own, f_own
    )
    low_face = tuple(rolled(part, 1, 1) for part in high_face)
    last_gains = cell_weights(*low_face, *high_face)
    for d in range(1, 4):
        G[2 + d] = jnp.where((place >= 3 - d) & (place < 3), last_gains[3 + d], 0.0)

    def beside(f):
        before, after = west[f], east[f]
        first = (
            G[0] * rolled(before, -2, 1) + G[1] * rolled(before, -1, 1) + G[2] * before
        )
        last = G[3] * rolled(after, 2, 1) + G[4] * rolled(after, 1, 1) + G[5] * after
        C[0, f] = first
        C[1, f] = rolled(last, LANES - 3, 1)

    for f in range(F):
        beside(f)
    for copy in copies:
        copy.wait()

    def level(z, carry):
        z_up = jnp.minimum(z + 1, NZ - 1)
        z_down = jnp.maximum(z - 1, 0)
        for half in range(2):
            for xt in range(2):
                FE[half, z, 8 + 8 * xt : 16 + 8 * xt, :] = FN[
                    1, half, z, 8 * xt : 8 * xt + 8, :
                ].astype(f32)
        for xt in range(2):
            start = 8 + 8 * xt

            def outer(index):
                return H[index - F, 2 * z + xt]

            def at(ref, half, offset):
                return ref[half, z, start + offset : start + offset + 8, :]

            wet = [at(W, half, 0).astype(f32) for half in range(2)]
            wx = []
            for half in range(2):
                before = wet[half] * at(W, half, -1).astype(f32)
                after = wet[half] * at(W, half, 1).astype(f32)
                wx.append(
                    cell_weights(
                        *face_parts(before, at(VE, half, -1), at(FE, half, -1)),
                        *face_parts(after, at(VE, half, 0), at(FE, half, 0)),
                    )
                )
            wet_out = outer(F + 2)
            following = along_lanes(wet[0], wet[1], wet_out, 1)
            own = [
                face_parts(
                    wet[half] * following[half],
                    VN[half, z, 8 * xt : 8 * xt + 8, :],
                    FN[0, half, z, 8 * xt : 8 * xt + 8, :].astype(f32),
                )
                for half in range(2)
            ]
            beyond = face_parts(wet_out * rolled(wet[0], -1, 1), outer(F), outer(F + 1))
            before = [along_lanes(own[0][i], own[1][i], beyond[i], -1) for i in range(3)]
            wy = [
                cell_weights(*(before[i][half] for i in range(3)), *own[half]) for half in range(2)
            ]
            wy = [
                [
                    jnp.where(
                        (lanes < 3 - j) if half == 0 else (lanes >= LANES + 3 - j), 0.0, wy[half][j]
                    )
                    if (half == 0) == (j < 3) and j != 3
                    else wy[half][j]
                    for j in range(7)
                ]
                for half in range(2)
            ]
            centre = [
                wx[half][3] + wy[half][3] - 2.0 * vert_diff * wet[half] for half in range(2)
            ]
            w_level = [vert_diff * wet[half] for half in range(2)]
            for half in range(2):
                for index, plane in enumerate((at(VE, half, 0), at(FE, half, 0), wet[half])):
                    if xt == 0:
                        weights_out[half, z, 3 + index] = plane
                    else:
                        weights_out[half, z, 3 + index] = jnp.where(
                            rows < 4, weights_out[half, z, 3 + index], plane
                        )
                for d in range(1, 4):
                    if xt == 0:
                        weights_out[half, z, d - 1] = jnp.where(rows < d, wx[half][3 - d], 0.0)
                    else:
                        weights_out[half, z, d - 1] += jnp.where(
                            rows >= 8 - d, wx[half][3 + d], 0.0
                        )
            for f in range(F):
                own_cells = [X[half, f, z, start : start + 8, :] for half in range(2)]
                total = [
                    centre[half] * own_cells[half]
                    + w_level[half]
                    * (
                        X[half, f, z_up, start : start + 8, :]
                        + X[half, f, z_down, start : start + 8, :]
                    )
                    for half in range(2)
                ]
                first, last = C[0, f], C[1, f]
                total[0] += jnp.where(lanes < 3, first, 0.0)
                total[1] += jnp.where(lanes >= LANES - 3, last, 0.0)
                C[0, f] = rolled(first, -4, 1)
                C[1, f] = rolled(last, -4, 1)
                for offset in (-3, -2, -1, 1, 2, 3):
                    moved = around_lanes(own_cells[0], own_cells[1], offset)
                    for half in range(2):
                        total[half] += wx[half][3 + offset] * X[
                            half, f, z, start + offset : start + offset + 8, :
                        ]
                        total[half] += wy[half][3 + offset] * moved[half]
                for half in range(2):
                    columns = slice(LANES * half, LANES * half + LANES)
                    low_rows = rows < 4
                    if xt == 1:
                        cells = X[half, f, z, 8:16, :]
                        edge_out[z, half, 8 + 8 * f : 16 + 8 * f, :] = jnp.where(
                            low_rows, cells, own_cells[half]
                        )
                    if f == M:
                        mean_out[z, 8 * xt : 8 * xt + 8, columns] = (
                            own_cells[half] + time_step * total[half]
                        )
                    elif xt == 0:
                        T[half, f] = total[half]
                    else:
                        near = T[half, f]
                        Z[8 * f : 8 * f + 8, columns] = jnp.where(
                            low_rows, own_cells[half], cells
                        )
                        Z[128 + 8 * f : 136 + 8 * f, columns] = jnp.where(
                            low_rows, total[half], near
                        )
                        place = slice(TAIL + 8 * f, TAIL + 8 * f + 8)
                        edge_out[z, half, place, :] = jnp.where(low_rows, near, total[half])
        high, low = split(Z[...])
        high_out[z] = high
        low_out[z] = low
        return carry

    lax.fori_loop(0, NZ, level, 0)
    add_products(acc, joined(high_out), joined(low_out))
    sums_out[...] = field_sums(acc)


def interior(cells, ve, vn, fe, fn, mask, west, east, own_last, own_first):
    parts = jax.ShapeDtypeStruct((NZ, 256, 256), bf16)
    return pl.pallas_call(
        interior_kernel,
        out_shape=(
            parts,
            parts,
            jax.ShapeDtypeStruct((NZ, 2, TAIL + 8 * M, LANES), f32),
            jax.ShapeDtypeStruct((2, NZ, 6, 8, LANES), f32),
            jax.ShapeDtypeStruct(ve.shape, f32),
            jax.ShapeDtypeStruct((64, 32), f32),
        ),
        in_specs=[VMEM] + [HBM] * 5 + [VMEM] * 4,
        out_specs=(VMEM,) * 6,
        scratch_shapes=[
            pltpu.VMEM((2, NZ, 32, LANES), f32),
            pltpu.VMEM((2, NZ, 32, LANES), f32),
            pltpu.VMEM((2, NZ, 32, LANES), jnp.int32),
            pltpu.VMEM((2, NZ, BX, LANES), f32),
            pltpu.VMEM((2, 2, NZ, BX, LANES), jnp.int32),
            pltpu.VMEM((3, 2 * NZ, 8, LANES), f32),
            pltpu.VMEM((2, F, 8, LANES), f32),
            pltpu.VMEM((6, 8, LANES), f32),
            pltpu.VMEM((2, M, 8, LANES), f32),
            pltpu.VMEM((256, 256), f32),
            pltpu.VMEM((512, 256), f32),
            pltpu.SemaphoreType.DMA((10,)),
        ],
        compiler_params=params(28),
        cost_estimate=cost(10**6, 10**6),
        name="interior",
    )(cells, ve, vn, fe, fn, mask, west, east, own_last, own_first)


def edge_kernel(
    below, above, edge_in, weights, mean_in, sums_in,
    high_out, low_out, mean_out, sums_out, Z, acc,
):
    acc[...] = jnp.zeros((512, 256), f32)
    rows = row_ids()
    low_rows = rows < 4
    first_row = rows == 0
    last_row = rows == 7

    def rows_from(ref, half, f, zh, first):
        start = min(max(first, 0), 16)
        return rolled(ref[half, f, zh, start : start + 8, :], start - first, 0)

    def gains_of(half, z, zh, zi):
        speed, flag, wet = (weights[half, z, 3 + i] for i in range(3))
        speed = jnp.where(first_row, rows_from(below, half, F, zh, 3 * zi), speed)
        flag = jnp.where(first_row, rows_from(below, half, F, zh, 3 * zi + 1), flag)
        beyond = jnp.where(first_row, rows_from(below, half, F, zh, 3 * zi + 2), 0.0)
        beyond = jnp.where(last_row, rows_from(above, half, F, zh, 3 * zi - 7), beyond)
        a, b, d = face_parts(beyond * wet, speed, flag)
        near, far = 47.0 * a + 27.0 * b + d, 27.0 * a + 47.0 * b - d
        left, right = -13.0 * a - 3.0 * b, -3.0 * a - 13.0 * b
        outside = (
            weights[half, z, 0] + jnp.where(first_row, near, -far),
            weights[half, z, 1] + jnp.where(first_row, left, -right),
            weights[half, z, 2] + jnp.where(first_row, 2.0 * a, -2.0 * b),
        )
        inside = (
            jnp.where(first_row, far, -near),
            jnp.where(first_row, right, -left),
            jnp.where(first_row, 2.0 * b, -2.0 * a),
        )
        return outside, inside

    def group(zh, carry):
        for zi in range(8):
            z = 8 * zh + zi
            for half in range(2):
                outside, inside = gains_of(half, z, zh, zi)
                for f in range(F):
                    base = 8 + 8 * f
                    change = inside[0] * edge_in[z, half, base : base + 8, :]
                    for d in range(1, 4):
                        cells = jnp.where(
                            low_rows,
                            rows_from(below, half, f, zh, 3 * zi + 3 - d),
                            rows_from(above, half, f, zh, 3 * zi + d - 8),
                        )
                        change = change + outside[d - 1] * cells
                    for d in range(1, 3):
                        cells = jnp.where(
                            low_rows,
                            edge_in[z, half, base + d : base + d + 8, :],
                            edge_in[z, half, base - d : base - d + 8, :],
                        )
                        change = change + inside[d] * cells
                    if f < M:
                        Z[half, 8 * f : 8 * f + 8, :] = (
                            edge_in[z, half, TAIL + 8 * f : TAIL + 8 * f + 8, :] + change
                        )
                    else:
                        columns = slice(LANES * half, LANES * half + LANES)
                        step = time_step * change
                        mean_out[z, 0:8, columns] = mean_in[z, 0:8, columns] + jnp.where(
                            low_rows, step, 0.0
                        )
                        mean_out[z, 8:16, columns] = mean_in[z, 8:16, columns] + jnp.where(
                            low_rows, 0.0, step
                        )
            halves = [
                jnp.concatenate([edge_in[z, half, 8 : 8 + 8 * M, :], Z[half]], axis=0)
                for half in range(2)
            ]
            high, low = split(jnp.concatenate(halves, axis=1))
            high_out[z] = high
            low_out[z] = low
            add_products(acc, high, low)
        return carry

    lax.fori_loop(0, 2, group, 0)
    sums = sums_in[...] + field_sums(acc)
    identity = (
        lax.broadcasted_iota(jnp.int32, (32, 32), 0) == lax.broadcasted_iota(jnp.int32, (32, 32), 1)
    ).astype(f32)
    turned = lax.dot_general(
        identity, sums[32:64], (((1,), (1,)), ((), ())), precision=HIGH, preferred_element_type=f32
    )
    sums_out[...] = sums[0:32] + sums[32:64] + turned


def edges(below, above, edge_in, weights, mean_in, sums_in):
    parts = jax.ShapeDtypeStruct((NZ, 256, 256), bf16)
    return pl.pallas_call(
        edge_kernel,
        out_shape=(
            parts,
            parts,
            jax.ShapeDtypeStruct(mean_in.shape, f32),
            jax.ShapeDtypeStruct((32, 32), f32),
        ),
        in_specs=[VMEM] * 6,
        out_specs=(VMEM,) * 4,
        scratch_shapes=[
            pltpu.VMEM((2, 8 * M, LANES), f32),
            pltpu.VMEM((512, 256), f32),
        ],
        compiler_params=params(16),
        cost_estimate=cost(10**9, 10**7),
        name="edges",
    )(below, above, edge_in, weights, mean_in, sums_in)


def factor_and_map(sums, cell_count):
    inner = sums * (1.0 / cell_count)
    row = lax.broadcasted_iota(jnp.int32, (M, 2 * M), 0)
    column = lax.broadcasted_iota(jnp.int32, (M, 2 * M), 1)
    update = jnp.where(
        column < M,
        jnp.where(column == row, 1.0, 0.0) - time_step * inner[M : 2 * M, :],
        jnp.where(column == row + M, time_step, 0.0),
    )
    half_way = jnp.dot(update, inner, precision=HIGH, preferred_element_type=f32)
    gram = lax.dot_general(
        half_way, update, (((1,), (1,)), ((), ())), precision=HIGH, preferred_element_type=f32
    )
    row_g = lax.broadcasted_iota(jnp.int32, (M, M), 0)
    column_g = lax.broadcasted_iota(jnp.int32, (M, M), 1)
    left, right = gram, update
    for j in range(M):
        pivot = jnp.sum(jnp.where(column_g == j, left, 0.0), axis=1, keepdims=True)
        scale = 1.0 / jnp.sqrt(pivot[j : j + 1, :])
        left_row = left[j : j + 1, :] * scale
        right_row = right[j : j + 1, :] * scale
        share = jnp.where(row_g[:, 0:1] > j, pivot * scale, 0.0)
        left = jnp.where(row_g == j, left_row, left - share * left_row)
        right = jnp.where(row == j, right_row, right - share * right_row)
    return jnp.where(column_g >= row_g, left, 0.0), right


def spread_map(mapping):
    parts = jnp.concatenate(split(mapping), axis=0)
    tall = (
        lax.broadcasted_iota(jnp.int32, (256, 2 * M), 0) // 8
        == lax.broadcasted_iota(jnp.int32, (256, 2 * M), 1)
    ).astype(bf16)
    wide = (
        lax.broadcasted_iota(jnp.int32, (2 * M, 256), 1) // 8
        == lax.broadcasted_iota(jnp.int32, (2 * M, 256), 0)
    ).astype(bf16)
    rows = jnp.dot(tall, parts, preferred_element_type=f32).astype(bf16)
    full = jnp.dot(rows, wide, preferred_element_type=f32)
    row = lax.broadcasted_iota(jnp.int32, (256, 256), 0)
    column = lax.broadcasted_iota(jnp.int32, (256, 256), 1)
    return jnp.where(row % 8 == column % 8, full, 0.0).astype(bf16)


def make_apply_kernel(cell_count):
    def apply_kernel(sums, high_i, low_i, high_e, low_e, out, factor_out, maps, new, sems):
        factor, mapping = factor_and_map(sums[...], cell_count)
        factor_out[...] = factor
        maps[...] = spread_map(mapping)
        low_rows = lax.broadcasted_iota(jnp.int32, (M, 8, 256), 1) < 4

        def put(z, slot):
            return pltpu.make_async_copy(new.at[slot], out.at[:, z], sems.at[slot])

        def level(z, carry):
            slot = lax.rem(z, SLOTS)

            @pl.when(z >= SLOTS)
            def _():
                put(z - SLOTS, slot).wait()

            results = []
            for high, low in ((high_i, low_i), (high_e, low_e)):
                first = jnp.dot(maps[...], high[z], preferred_element_type=f32)
                second = jnp.dot(maps[0:128, :], low[z], preferred_element_type=f32)
                results.append((first[0:128] + first[128:256] + second).reshape(M, 8, 256))
            inner, edge = results
            new[slot, :, 0:8, :] = jnp.where(low_rows, edge, inner)
            new[slot, :, 8:16, :] = jnp.where(low_rows, inner, edge)
            put(z, slot).start()
            return carry

        lax.fori_loop(0, NZ, level, 0)
        for z in range(NZ - SLOTS, NZ):
            put(z, z % SLOTS).wait()

    return apply_kernel


def apply_map(sums, high_i, low_i, high_e, low_e, cell_count):
    return pl.pallas_call(
        make_apply_kernel(cell_count),
        out_shape=(
            jax.ShapeDtypeStruct((M, NZ, BX, 256), f32),
            jax.ShapeDtypeStruct((M, M), f32),
        ),
        in_specs=[VMEM] * 5,
        out_specs=(ANY, VMEM),
        scratch_shapes=[
            pltpu.VMEM((256, 256), bf16),
            pltpu.VMEM((SLOTS, M, BX, 256), f32),
            pltpu.SemaphoreType.DMA((SLOTS,)),
        ],
        compiler_params=params(12),
        cost_estimate=cost(10**9, 13 * 10**6),
        name="apply",
    )(sums, high_i, low_i, high_e, low_e)


def onward(value, axis):
    size = lax.axis_size(axis)
    return lax.ppermute(value, axis, [(i, i + 1) for i in range(size - 1)])


def backward(value, axis):
    size = lax.axis_size(axis)
    return lax.ppermute(value, axis, [(i + 1, i) for i in range(size - 1)])


def exchanged(value, axes, distance):
    size = lax.axis_size(axes)
    return lax.ppermute(value, axes, [(i, i ^ distance) for i in range(size)])


def shards(
    mean_field, mode_fields, velocity_east, velocity_north, flag_east, flag_north, ocean_mask
):
    axes = ("gx", "gy")
    (
        mean_field, mode_fields, velocity_east, velocity_north, flag_east, flag_north, ocean_mask
    ) = (
        pltpu.with_memory_space_constraint(value, pltpu.HBM)
        for value in (
            mean_field, mode_fields, velocity_east, velocity_north, flag_east, flag_north,
            ocean_mask,
        )
    )
    up, down, east_send, west_send, cells = pack(
        mode_fields, mean_field, velocity_east, velocity_north, flag_east, flag_north, ocean_mask
    )
    west = onward(east_send, "gy")
    east = backward(west_send, "gy")
    below = onward(up, "gx")
    above = backward(down, "gx")
    high_i, low_i, edge, weights, mean_part, sums_i = interior(
        cells, velocity_east, velocity_north, flag_east, flag_north, ocean_mask,
        west, east, east_send, west_send,
    )
    high_e, low_e, mean_next, sums = edges(below, above, edge, weights, mean_part, sums_i)
    sums = sums + exchanged(sums, axes, 1)
    for first in (2, 8, 32):
        near, far, both = (exchanged(sums, axes, first * i) for i in (1, 2, 3))
        sums = (sums + near) + (far + both)
    cell_count = float(NZ * BX * 256 * lax.axis_size("gx") * lax.axis_size("gy"))
    modes_next, factor = apply_map(sums, high_i, low_i, high_e, low_e, cell_count)
    return (mean_next, modes_next, factor)


def solution(mesh):
    plane = P(None, "gx", "gy")
    return jax.shard_map(
        shards,
        mesh=mesh,
        in_specs=(plane, P(None, None, "gx", "gy"), plane, plane, plane, plane, plane),
        out_specs=(plane, P(None, None, "gx", "gy"), P()),
        check_vma=False,
    )
```

```python
import jax
import jax.numpy as jnp
from jax import lax
from jax.experimental import pallas as pl
from jax.experimental.pallas import tpu as pltpu
from jax.sharding import PartitionSpec as P

time_step = 0.1
horiz_diff = 0.05
vert_diff = 0.2

M = 16
F = 17
NZ = 16
BX = 16
LANES = 128
ROWS = 3 * NZ
SLOTS = 4
TAIL = 8 + 8 * F
HIGH = lax.Precision.HIGHEST
f32 = jnp.float32
bf16 = jnp.bfloat16

ANY = pl.BlockSpec(memory_space=pl.ANY)
HBM = pl.BlockSpec(memory_space=pltpu.HBM)
VMEM = pl.BlockSpec(memory_space=pltpu.VMEM)


def params(mib):
    return pltpu.CompilerParams(vmem_limit_bytes=mib * 1024 * 1024)


def cost(flops, nbytes):
    return pl.CostEstimate(flops=flops, bytes_accessed=nbytes, transcendentals=0)


def rolled(value, shift, axis):
    shift = shift % value.shape[axis]
    return value if shift == 0 else pltpu.roll(value, shift, axis)


def lane_ids():
    return lax.broadcasted_iota(jnp.int32, (8, LANES), 1)


def row_ids():
    return lax.broadcasted_iota(jnp.int32, (8, LANES), 0)


def lane_half(ref, half):
    where = (slice(None),) * (len(ref.shape) - 1) + (pl.ds(LANES * half, LANES),)
    return ref.at[where]


def pack_rows(get, first_row):
    rows = row_ids()
    tiles = []
    for out in range(3):
        tile = None
        for z in range(8):
            low, high = max(3 * z, 8 * out), min(3 * z + 3, 8 * out + 8)
            if low >= high:
                continue
            piece = rolled(get(z), 3 * z - 8 * out - first_row, 0)
            tile = piece if tile is None else jnp.where(rows >= low - 8 * out, piece, tile)
        tiles.append(tile)
    return tiles


def pack_columns(get, shift_of):
    slot = lane_ids() // 4
    parts = [jnp.zeros((8, LANES), f32) for _ in range(4)]
    for k in range(2 * NZ):
        moved = rolled(get(k), shift_of(k), 1)
        parts[k % 4] = jnp.where(slot == k, moved, parts[k % 4])
    out = parts[0]
    for k in range(1, 4):
        out = jnp.where(slot % 4 == k, parts[k], out)
    return out


def pack_kernel(
    modes, mean, ve, vn, fe, fn, mask, up, down, east, west, X, V, I, sems
):
    copies = []
    for chunk in range(4):
        for half in range(2):
            copies.append(
                pltpu.make_async_copy(
                    lane_half(modes, half).at[pl.ds(4 * chunk, 4)],
                    X.at[half, pl.ds(4 * chunk, 4), :, pl.ds(8, BX)],
                    sems.at[len(copies)],
                )
            )
    for source, target in (
        (mean, lambda half: X.at[half, M, :, pl.ds(8, BX)]),
        (vn, lambda half: V.at[0, half]),
        (ve, lambda half: V.at[1, half]),
        (fn, lambda half: I.at[0, half]),
        (mask, lambda half: I.at[1, half]),
        (fe, lambda half: I.at[2, half]),
    ):
        for half in range(2):
            copies.append(
                pltpu.make_async_copy(lane_half(source, half), target(half), sems.at[len(copies)])
            )
    for copy in copies:
        copy.start()
    zero_tile = jnp.zeros((8, LANES), f32)

    def clear(f, carry):
        for half in range(2):
            for z in range(NZ):
                X[half, f, z, 0:8, :] = zero_tile
                X[half, f, z, 24:32, :] = zero_tile
        return carry

    lax.fori_loop(0, F, clear, 0, unroll=True)

    def field(f, carry):
        for half in range(2):
            for zh in range(2):
                for target, tile, first in ((up, 1, 5), (down, 0, 0)):
                    tiles = pack_rows(
                        lambda z: X[half, f, 8 * zh + z, 8 + 8 * tile : 16 + 8 * tile, :], first
                    )
                    for t in range(3):
                        target[half, f, zh, 8 * t : 8 * t + 8, :] = tiles[t]
        def tile_of(half):
            return lambda k: X[half, f, k // 2, 8 + 8 * (k % 2) : 16 + 8 * (k % 2), :]
        east[f] = pack_columns(tile_of(1), lambda k: 4 * k - 125)
        west[f] = pack_columns(tile_of(0), lambda k: 4 * k)
        return carry

    for chunk in range(4):
        copies[2 * chunk].wait()
        copies[2 * chunk + 1].wait()
        lax.fori_loop(4 * chunk, 4 * chunk + 4, field, 0, unroll=4)
    for copy in copies[8:]:
        copy.wait()
    lax.fori_loop(M, F, field, 0)
    for index, plane in enumerate(
        (
            lambda half, k: V[0, half, k // 2, 8 * (k % 2) : 8 * (k % 2) + 8, :],
            lambda half, k: I[0, half, k // 2, 8 * (k % 2) : 8 * (k % 2) + 8, :].astype(f32),
            lambda half, k: I[1, half, k // 2, 8 * (k % 2) : 8 * (k % 2) + 8, :].astype(f32),
        )
    ):
        east[F + index] = pack_columns(lambda k: plane(1, k), lambda k: 4 * k - 125)
        west[F + index] = pack_columns(lambda k: plane(0, k), lambda k: 4 * k)
    rows = row_ids()
    for half in range(2):
        for zh in range(2):

            def last_row(z):
                level = 8 * zh + z
                speed = rolled(V[1, half, level, 8:16, :], -2, 0)
                flag = rolled(I[2, half, level, 8:16, :].astype(f32), -1, 0)
                wet = I[1, half, level, 8:16, :].astype(f32)
                return jnp.where(rows == 5, speed, jnp.where(rows == 6, flag, wet))

            for target, get, first in (
                (up, last_row, 5),
                (down, lambda z: I[1, half, 8 * zh + z, 0:8, :].astype(f32), 0),
            ):
                tiles = pack_rows(get, first)
                for t in range(3):
                    target[half, F, zh, 8 * t : 8 * t + 8, :] = tiles[t]


def pack(modes, mean, ve, vn, fe, fn, mask):
    rows = jax.ShapeDtypeStruct((2, F + 1, 2, ROWS // 2, LANES), f32)
    columns = jax.ShapeDtypeStruct((F + 3, 8, LANES), f32)
    return pl.pallas_call(
        pack_kernel,
        out_shape=(
            rows,
            rows,
            columns,
            columns,
            jax.ShapeDtypeStruct((2, F, NZ, 32, LANES), f32),
        ),
        in_specs=[HBM] * 7,
        out_specs=(VMEM,) * 5,
        scratch_shapes=[
            pltpu.VMEM((2, 2, NZ, BX, LANES), f32),
            pltpu.VMEM((3, 2, NZ, BX, LANES), jnp.int32),
            pltpu.SemaphoreType.DMA((20,)),
        ],
        compiler_params=params(24),
        cost_estimate=cost(10**7, 7 * 10**6),
        name="pack",
    )(modes, mean, ve, vn, fe, fn, mask)


def along_lanes(first, second, outer, offset):
    lanes = lane_ids()
    a, b, c = (rolled(v, -offset, 1) for v in (first, second, outer))
    if offset > 0:
        inside = lanes < LANES - offset
        return jnp.where(inside, a, b), jnp.where(inside, b, c)
    outside = lanes < -offset
    return jnp.where(outside, c, a), jnp.where(outside, a, b)


def around_lanes(first, second, offset):
    lanes = lane_ids()
    a, b = (rolled(v, -offset, 1) for v in (first, second))
    kept = lanes < LANES - offset if offset > 0 else lanes >= -offset
    return jnp.where(kept, a, b), jnp.where(kept, b, a)


def cell_weights(a_low, b_low, d_low, a_high, b_high, d_high):
    return (
        2.0 * a_low,
        -13.0 * a_low - 3.0 * b_low - 2.0 * a_high,
        47.0 * a_low + 27.0 * b_low + d_low + 13.0 * a_high + 3.0 * b_high,
        27.0 * a_low + 47.0 * b_low - d_low - 47.0 * a_high - 27.0 * b_high - d_high,
        -3.0 * a_low - 13.0 * b_low - 27.0 * a_high - 47.0 * b_high + d_high,
        2.0 * b_low + 3.0 * a_high + 13.0 * b_high,
        -2.0 * b_high,
    )


def face_parts(openness, speed, flag):
    scaled = openness * speed * (1.0 / 60.0)
    return scaled * flag, scaled * (1.0 - flag), horiz_diff * openness


def split(value):
    high = value.astype(bf16)
    return high, (value - high.astype(f32)).astype(bf16)


def add_products(acc, high, low):
    dims = (((1,), (1,)), ((), ()))
    acc[0:256, :] += lax.dot_general(high, high, dims, preferred_element_type=f32)
    acc[256:512, :] += lax.dot_general(low, high, dims, preferred_element_type=f32)


def joined(upper, lower):
    return jnp.concatenate([both(upper, lower, z) for z in range(NZ)], axis=1)


def both(upper, lower, z):
    return jnp.concatenate([upper[z], lower[z]], axis=0)


def field_sums(acc):
    rows = lax.broadcasted_iota(jnp.int32, (512, 256), 0)
    columns = lax.broadcasted_iota(jnp.int32, (512, 256), 1)
    kept = jnp.where(rows % 8 == columns % 8, acc[...], 0.0)
    by_row = jnp.sum(kept.reshape(64, 8, 256), axis=1)
    gather = (
        lax.broadcasted_iota(jnp.int32, (256, 32), 0) // 8
        == lax.broadcasted_iota(jnp.int32, (256, 32), 1)
    ).astype(f32)
    return jnp.dot(by_row, gather, precision=HIGH, preferred_element_type=f32)


def prepare_kernel(
    X, ve, vn, fe, fn, mask,
    high_in, low_in, high_edge, low_edge, edge_out, VE, FE, W, VN, FN, ints, Z, sems,
):
    zero_tile = jnp.zeros((8, LANES), f32)
    copies = []
    for half in range(2):
        for source, target in (
            (ve, VE.at[half, :, pl.ds(8, BX)]),
            (vn, VN.at[half]),
            (mask, ints.at[0, half]),
            (fn, ints.at[1, half]),
            (fe, ints.at[2, half]),
        ):
            copies.append(
                pltpu.make_async_copy(lane_half(source, half), target, sems.at[len(copies)])
            )
    for copy in copies:
        copy.start()
    low_rows = row_ids() < 4
    for half in range(2):
        for z in range(NZ):
            edge_out[z, half, 0:8, :] = zero_tile
            edge_out[z, half, TAIL : TAIL + 8, :] = zero_tile

    def level(z, carry):
        for half in range(2):
            columns = slice(LANES * half, LANES * half + LANES)
            for f in range(F):
                first, second = X[half, f, z, 8:16, :], X[half, f, z, 16:24, :]
                edge = jnp.where(low_rows, first, second)
                edge_out[z, half, 8 + 8 * f : 16 + 8 * f, :] = edge
                if f < M:
                    Z[0, 8 * f : 8 * f + 8, columns] = jnp.where(low_rows, second, first)
                    Z[1, 8 * f : 8 * f + 8, columns] = edge
        high_in[z], low_in[z] = split(Z[0])
        high_edge[z], low_edge[z] = split(Z[1])
        return carry

    lax.fori_loop(0, NZ, level, 0, unroll=2)
    for copy in copies:
        copy.wait()
    for half in range(2):
        for z in range(NZ):
            VE[half, z, 0:8, :] = zero_tile
            FE[half, z, 0:8, :] = zero_tile
            W[half, z, 0:8, :] = zero_tile
            W[half, z, 24:32, :] = zero_tile
            for xt in range(2):
                rows = slice(8 * xt, 8 * xt + 8)
                padded = slice(8 * xt + 8, 8 * xt + 16)
                W[half, z, padded, :] = ints[0, half, z, rows, :].astype(f32)
                FN[half, z, rows, :] = ints[1, half, z, rows, :].astype(f32)
                FE[half, z, padded, :] = ints[2, half, z, rows, :].astype(f32)


def prepare(cells, ve, vn, fe, fn, mask):
    parts = jax.ShapeDtypeStruct((NZ, 8 * M, 256), bf16)
    padded = jax.ShapeDtypeStruct((2, NZ, 32, LANES), f32)
    plain = jax.ShapeDtypeStruct((2, NZ, BX, LANES), f32)
    return pl.pallas_call(
        prepare_kernel,
        out_shape=(
            parts,
            parts,
            parts,
            parts,
            jax.ShapeDtypeStruct((NZ, 2, TAIL + 8, LANES), f32),
            padded,
            padded,
            padded,
            plain,
            plain,
        ),
        in_specs=[VMEM] + [HBM] * 5,
        out_specs=(VMEM,) * 10,
        scratch_shapes=[
            pltpu.VMEM((3, 2, NZ, BX, LANES), jnp.int32),
            pltpu.VMEM((2, 8 * M, 256), f32),
            pltpu.SemaphoreType.DMA((10,)),
        ],
        compiler_params=params(16),
        cost_estimate=cost(10**6, 10**6),
        name="prepare",
    )(cells, ve, vn, fe, fn, mask)


def interior_kernel(
    X, VE, FE, W, VN, FN, high_in, low_in, west, east, own_last, own_first,
    high_out, low_out, edge_out, weights_out, mean_out, sums_out,
    H, C, G, T, Z, acc,
):
    acc[...] = jnp.zeros((512, 256), f32)
    lanes = lane_ids()
    rows = row_ids()

    for f in range(F, F + 3):
        after, before = east[f], west[f]
        for k in range(2 * NZ):
            H[f - F, k] = jnp.where(
                lanes < 64, rolled(after, -4 * k, 1), rolled(before, LANES - 3 - 4 * k, 1)
            )

    place = lanes % 4

    (v_in, f_in, w_in) = (west[F + i] for i in range(3))
    (v_own, f_own, w_own) = (own_first[F + i] for i in range(3))
    lower_of = lambda outer_plane, own: jnp.where(
        place == 0, rolled(outer_plane, -2, 1), rolled(own, 1, 1)
    )
    low_face = face_parts(
        lower_of(w_in, w_own) * w_own, lower_of(v_in, v_own), lower_of(f_in, f_own)
    )
    high_face = face_parts(w_own * rolled(w_own, -1, 1), v_own, f_own)
    first_gains = cell_weights(*low_face, *high_face)
    for d in range(1, 4):
        G[d - 1] = jnp.where(place < d, first_gains[3 - d], 0.0)
    w_next = east[F + 2]
    (v_own, f_own, w_own) = (own_last[F + i] for i in range(3))
    high_face = face_parts(
        w_own * jnp.where(place == 2, rolled(w_next, 2, 1), rolled(w_own, -1, 1)), v_own, f_own
    )
    low_face = tuple(rolled(part, 1, 1) for part in high_face)
    last_gains = cell_weights(*low_face, *high_face)
    for d in range(1, 4):
        G[2 + d] = jnp.where((place >= 3 - d) & (place < 3), last_gains[3 + d], 0.0)

    def beside(f):
        before, after = west[f], east[f]
        first = (
            G[0] * rolled(before, -2, 1) + G[1] * rolled(before, -1, 1) + G[2] * before
        )
        last = G[3] * rolled(after, 2, 1) + G[4] * rolled(after, 1, 1) + G[5] * after
        C[0, f] = first
        C[1, f] = rolled(last, LANES - 3, 1)

    for f in range(F):
        beside(f)

    def level(z, carry):
        z_up = jnp.minimum(z + 1, NZ - 1)
        z_down = jnp.maximum(z - 1, 0)
        for xt in range(2):
            start = 8 + 8 * xt

            def outer(index):
                return H[index - F, 2 * z + xt]

            def at(ref, half, offset):
                return ref[half, z, start + offset : start + offset + 8, :]

            wet = [at(W, half, 0) for half in range(2)]
            wx = []
            for half in range(2):
                before = wet[half] * at(W, half, -1)
                after = wet[half] * at(W, half, 1)
                wx.append(
                    cell_weights(
                        *face_parts(before, at(VE, half, -1), at(FE, half, -1)),
                        *face_parts(after, at(VE, half, 0), at(FE, half, 0)),
                    )
                )
            wet_out = outer(F + 2)
            following = along_lanes(wet[0], wet[1], wet_out, 1)
            own = [
                face_parts(
                    wet[half] * following[half],
                    VN[half, z, 8 * xt : 8 * xt + 8, :],
                    FN[half, z, 8 * xt : 8 * xt + 8, :],
                )
                for half in range(2)
            ]
            beyond = face_parts(wet_out * rolled(wet[0], -1, 1), outer(F), outer(F + 1))
            before = [along_lanes(own[0][i], own[1][i], beyond[i], -1) for i in range(3)]
            wy = [
                cell_weights(*(before[i][half] for i in range(3)), *own[half]) for half in range(2)
            ]
            wy = [
                [
                    jnp.where(
                        (lanes < 3 - j) if half == 0 else (lanes >= LANES + 3 - j), 0.0, wy[half][j]
                    )
                    if (half == 0) == (j < 3) and j != 3
                    else wy[half][j]
                    for j in range(7)
                ]
                for half in range(2)
            ]
            centre = [
                wx[half][3] + wy[half][3] - 2.0 * vert_diff * wet[half] for half in range(2)
            ]
            w_level = [vert_diff * wet[half] for half in range(2)]
            for half in range(2):
                for index, plane in enumerate((at(VE, half, 0), at(FE, half, 0), wet[half])):
                    if xt == 0:
                        weights_out[half, z, 3 + index] = plane
                    else:
                        weights_out[half, z, 3 + index] = jnp.where(
                            rows < 4, weights_out[half, z, 3 + index], plane
                        )
                for d in range(1, 4):
                    if xt == 0:
                        weights_out[half, z, d - 1] = jnp.where(rows < d, wx[half][3 - d], 0.0)
                    else:
                        weights_out[half, z, d - 1] += jnp.where(
                            rows >= 8 - d, wx[half][3 + d], 0.0
                        )
            for f in range(F):
                own_cells = [X[half, f, z, start : start + 8, :] for half in range(2)]
                total = [
                    centre[half] * own_cells[half]
                    + w_level[half]
                    * (
                        X[half, f, z_up, start : start + 8, :]
                        + X[half, f, z_down, start : start + 8, :]
                    )
                    for half in range(2)
                ]
                first, last = C[0, f], C[1, f]
                total[0] += jnp.where(lanes < 3, first, 0.0)
                total[1] += jnp.where(lanes >= LANES - 3, last, 0.0)
                C[0, f] = rolled(first, -4, 1)
                C[1, f] = rolled(last, -4, 1)
                for offset in (-3, -2, -1, 1, 2, 3):
                    moved = around_lanes(own_cells[0], own_cells[1], offset)
                    for half in range(2):
                        total[half] += wx[half][3 + offset] * X[
                            half, f, z, start + offset : start + offset + 8, :
                        ]
                        total[half] += wy[half][3 + offset] * moved[half]
                for half in range(2):
                    columns = slice(LANES * half, LANES * half + LANES)
                    low_rows = rows < 4
                    if f == M:
                        mean_out[z, 8 * xt : 8 * xt + 8, columns] = (
                            own_cells[half] + time_step * total[half]
                        )
                    elif xt == 0:
                        T[half, f] = total[half]
                    else:
                        near = T[half, f]
                        place = slice(8 * f, 8 * f + 8)
                        Z[place, columns] = jnp.where(low_rows, total[half], near)
                        edge_out[z, half, place, :] = jnp.where(low_rows, near, total[half])
        high, low = split(Z[...])
        high_out[z] = high
        low_out[z] = low
        return carry

    lax.fori_loop(0, NZ, level, 0)
    add_products(acc, joined(high_in, high_out), joined(low_in, low_out))
    sums_out[...] = field_sums(acc)


def interior(cells, planes, high_in, low_in, west, east, own_last, own_first):
    parts = jax.ShapeDtypeStruct((NZ, 8 * M, 256), bf16)
    return pl.pallas_call(
        interior_kernel,
        out_shape=(
            parts,
            parts,
            jax.ShapeDtypeStruct((NZ, 2, 8 * M, LANES), f32),
            jax.ShapeDtypeStruct((2, NZ, 6, 8, LANES), f32),
            jax.ShapeDtypeStruct((NZ, BX, 2 * LANES), f32),
            jax.ShapeDtypeStruct((64, 32), f32),
        ),
        in_specs=[VMEM] * 12,
        out_specs=(VMEM,) * 6,
        scratch_shapes=[
            pltpu.VMEM((3, 2 * NZ, 8, LANES), f32),
            pltpu.VMEM((2, F, 8, LANES), f32),
            pltpu.VMEM((6, 8, LANES), f32),
            pltpu.VMEM((2, M, 8, LANES), f32),
            pltpu.VMEM((8 * M, 256), f32),
            pltpu.VMEM((512, 256), f32),
        ],
        compiler_params=params(20),
        cost_estimate=cost(10**6, 10**6),
        name="interior",
    )(cells, *planes, high_in, low_in, west, east, own_last, own_first)


def edge_kernel(
    below, above, edge_in, edge_tail, high_in, low_in, weights, mean_in, sums_in,
    high_out, low_out, mean_out, sums_out, Z, acc,
):
    acc[...] = jnp.zeros((512, 256), f32)
    rows = row_ids()
    low_rows = rows < 4
    first_row = rows == 0
    last_row = rows == 7

    def rows_from(ref, half, f, zh, first):
        start = min(max(first, 0), 16)
        return rolled(ref[half, f, zh, start : start + 8, :], start - first, 0)

    def gains_of(half, z, zh, zi):
        speed, flag, wet = (weights[half, z, 3 + i] for i in range(3))
        speed = jnp.where(first_row, rows_from(below, half, F, zh, 3 * zi), speed)
        flag = jnp.where(first_row, rows_from(below, half, F, zh, 3 * zi + 1), flag)
        beyond = jnp.where(first_row, rows_from(below, half, F, zh, 3 * zi + 2), 0.0)
        beyond = jnp.where(last_row, rows_from(above, half, F, zh, 3 * zi - 7), beyond)
        a, b, d = face_parts(beyond * wet, speed, flag)
        near, far = 47.0 * a + 27.0 * b + d, 27.0 * a + 47.0 * b - d
        left, right = -13.0 * a - 3.0 * b, -3.0 * a - 13.0 * b
        outside = (
            weights[half, z, 0] + jnp.where(first_row, near, -far),
            weights[half, z, 1] + jnp.where(first_row, left, -right),
            weights[half, z, 2] + jnp.where(first_row, 2.0 * a, -2.0 * b),
        )
        inside = (
            jnp.where(first_row, far, -near),
            jnp.where(first_row, right, -left),
            jnp.where(first_row, 2.0 * b, -2.0 * a),
        )
        return outside, inside

    def group(zh, carry):
        for zi in range(8):
            z = 8 * zh + zi
            for half in range(2):
                outside, inside = gains_of(half, z, zh, zi)
                for f in range(F):
                    base = 8 + 8 * f
                    change = inside[0] * edge_in[z, half, base : base + 8, :]
                    for d in range(1, 4):
                        cells = jnp.where(
                            low_rows,
                            rows_from(below, half, f, zh, 3 * zi + 3 - d),
                            rows_from(above, half, f, zh, 3 * zi + d - 8),
                        )
                        change = change + outside[d - 1] * cells
                    for d in range(1, 3):
                        cells = jnp.where(
                            low_rows,
                            edge_in[z, half, base + d : base + d + 8, :],
                            edge_in[z, half, base - d : base - d + 8, :],
                        )
                        change = change + inside[d] * cells
                    if f < M:
                        Z[half, 8 * f : 8 * f + 8, :] = (
                            edge_tail[z, half, 8 * f : 8 * f + 8, :] + change
                        )
                    else:
                        columns = slice(LANES * half, LANES * half + LANES)
                        step = time_step * change
                        mean_out[z, 0:8, columns] = mean_in[z, 0:8, columns] + jnp.where(
                            low_rows, step, 0.0
                        )
                        mean_out[z, 8:16, columns] = mean_in[z, 8:16, columns] + jnp.where(
                            low_rows, 0.0, step
                        )
            high, low = split(jnp.concatenate([Z[0], Z[1]], axis=1))
            high_out[z] = high
            low_out[z] = low
            add_products(
                acc,
                jnp.concatenate([high_in[z], high], axis=0),
                jnp.concatenate([low_in[z], low], axis=0),
            )
        return carry

    lax.fori_loop(0, 2, group, 0)
    sums = sums_in[...] + field_sums(acc)
    identity = (
        lax.broadcasted_iota(jnp.int32, (32, 32), 0) == lax.broadcasted_iota(jnp.int32, (32, 32), 1)
    ).astype(f32)
    turned = lax.dot_general(
        identity, sums[32:64], (((1,), (1,)), ((), ())), precision=HIGH, preferred_element_type=f32
    )
    sums_out[...] = sums[0:32] + sums[32:64] + turned


def edges(below, above, edge_in, edge_tail, high_in, low_in, weights, mean_in, sums_in):
    parts = jax.ShapeDtypeStruct((NZ, 8 * M, 256), bf16)
    return pl.pallas_call(
        edge_kernel,
        out_shape=(
            parts,
            parts,
            jax.ShapeDtypeStruct(mean_in.shape, f32),
            jax.ShapeDtypeStruct((32, 32), f32),
        ),
        in_specs=[VMEM] * 9,
        out_specs=(VMEM,) * 4,
        scratch_shapes=[
            pltpu.VMEM((2, 8 * M, LANES), f32),
            pltpu.VMEM((512, 256), f32),
        ],
        compiler_params=params(16),
        cost_estimate=cost(10**9, 10**7),
        name="edges",
    )(below, above, edge_in, edge_tail, high_in, low_in, weights, mean_in, sums_in)


def factor_and_map(sums, cell_count):
    inner = sums * (1.0 / cell_count)
    row = lax.broadcasted_iota(jnp.int32, (M, 2 * M), 0)
    column = lax.broadcasted_iota(jnp.int32, (M, 2 * M), 1)
    update = jnp.where(
        column < M,
        jnp.where(column == row, 1.0, 0.0) - time_step * inner[M : 2 * M, :],
        jnp.where(column == row + M, time_step, 0.0),
    )
    half_way = jnp.dot(update, inner, precision=HIGH, preferred_element_type=f32)
    gram = lax.dot_general(
        half_way, update, (((1,), (1,)), ((), ())), precision=HIGH, preferred_element_type=f32
    )
    row_g = lax.broadcasted_iota(jnp.int32, (M, M), 0)
    column_g = lax.broadcasted_iota(jnp.int32, (M, M), 1)
    left, right = gram, update
    for j in range(M):
        pivot = jnp.sum(jnp.where(column_g == j, left, 0.0), axis=1, keepdims=True)
        scale = 1.0 / jnp.sqrt(pivot[j : j + 1, :])
        left_row = left[j : j + 1, :] * scale
        right_row = right[j : j + 1, :] * scale
        share = jnp.where(row_g[:, 0:1] > j, pivot * scale, 0.0)
        left = jnp.where(row_g == j, left_row, left - share * left_row)
        right = jnp.where(row == j, right_row, right - share * right_row)
    return jnp.where(column_g >= row_g, left, 0.0), right


def spread_map(mapping):
    parts = jnp.concatenate(split(mapping), axis=0)
    tall = (
        lax.broadcasted_iota(jnp.int32, (256, 2 * M), 0) // 8
        == lax.broadcasted_iota(jnp.int32, (256, 2 * M), 1)
    ).astype(bf16)
    wide = (
        lax.broadcasted_iota(jnp.int32, (2 * M, 256), 1) // 8
        == lax.broadcasted_iota(jnp.int32, (2 * M, 256), 0)
    ).astype(bf16)
    rows = jnp.dot(tall, parts, preferred_element_type=f32).astype(bf16)
    full = jnp.dot(rows, wide, preferred_element_type=f32)
    row = lax.broadcasted_iota(jnp.int32, (256, 256), 0)
    column = lax.broadcasted_iota(jnp.int32, (256, 256), 1)
    return jnp.where(row % 8 == column % 8, full, 0.0).astype(bf16)


def make_apply_kernel(cell_count):
    def apply_kernel(sums, *refs):
        parts, (out, factor_out, maps, new, sems) = refs[:8], refs[8:]
        factor, mapping = factor_and_map(sums[...], cell_count)
        factor_out[...] = factor
        maps[...] = spread_map(mapping)
        low_rows = lax.broadcasted_iota(jnp.int32, (M, 8, 256), 1) < 4

        def put(z, slot):
            return pltpu.make_async_copy(new.at[slot], out.at[:, z], sems.at[slot])

        def level(z, carry):
            slot = lax.rem(z, SLOTS)

            @pl.when(z >= SLOTS)
            def _():
                put(z - SLOTS, slot).wait()

            results = []
            for i in (0, 4):
                high, low = both(parts[i], parts[i + 2], z), both(parts[i + 1], parts[i + 3], z)
                first = jnp.dot(maps[...], high, preferred_element_type=f32)
                second = jnp.dot(maps[0:128, :], low, preferred_element_type=f32)
                results.append((first[0:128] + first[128:256] + second).reshape(M, 8, 256))
            inner, edge = results
            new[slot, :, 0:8, :] = jnp.where(low_rows, edge, inner)
            new[slot, :, 8:16, :] = jnp.where(low_rows, inner, edge)
            put(z, slot).start()
            return carry

        lax.fori_loop(0, NZ, level, 0)
        for z in range(NZ - SLOTS, NZ):
            put(z, z % SLOTS).wait()

    return apply_kernel


def apply_map(sums, parts, cell_count):
    return pl.pallas_call(
        make_apply_kernel(cell_count),
        out_shape=(
            jax.ShapeDtypeStruct((M, NZ, BX, 256), f32),
            jax.ShapeDtypeStruct((M, M), f32),
        ),
        in_specs=[VMEM] * 9,
        out_specs=(ANY, VMEM),
        scratch_shapes=[
            pltpu.VMEM((256, 256), bf16),
            pltpu.VMEM((SLOTS, M, BX, 256), f32),
            pltpu.SemaphoreType.DMA((SLOTS,)),
        ],
        compiler_params=params(12),
        cost_estimate=cost(10**9, 13 * 10**6),
        name="apply",
    )(sums, *parts)


def onward(value, axis):
    size = lax.axis_size(axis)
    return lax.ppermute(value, axis, [(i, i + 1) for i in range(size - 1)])


def backward(value, axis):
    size = lax.axis_size(axis)
    return lax.ppermute(value, axis, [(i + 1, i) for i in range(size - 1)])


def exchanged(value, axes, distance):
    size = lax.axis_size(axes)
    return lax.ppermute(value, axes, [(i, i ^ distance) for i in range(size)])


def shards(
    mean_field, mode_fields, velocity_east, velocity_north, flag_east, flag_north, ocean_mask
):
    axes = ("gx", "gy")
    (
        mean_field, mode_fields, velocity_east, velocity_north, flag_east, flag_north, ocean_mask
    ) = (
        pltpu.with_memory_space_constraint(value, pltpu.HBM)
        for value in (
            mean_field, mode_fields, velocity_east, velocity_north, flag_east, flag_north,
            ocean_mask,
        )
    )
    up, down, east_send, west_send, cells = pack(
        mode_fields, mean_field, velocity_east, velocity_north, flag_east, flag_north, ocean_mask
    )
    west = onward(east_send, "gy")
    east = backward(west_send, "gy")
    below = onward(up, "gx")
    above = backward(down, "gx")
    high_x, low_x, high_xe, low_xe, edge, *planes = prepare(
        cells, velocity_east, velocity_north, flag_east, flag_north, ocean_mask
    )
    high_t, low_t, edge_tail, weights, mean_part, sums_i = interior(
        cells, planes, high_x, low_x, west, east, east_send, west_send
    )
    high_te, low_te, mean_next, sums = edges(
        below, above, edge, edge_tail, high_xe, low_xe, weights, mean_part, sums_i
    )
    sums = sums + exchanged(sums, axes, 1)
    for first in (2, 8, 32):
        near, far, both = (exchanged(sums, axes, first * i) for i in (1, 2, 3))
        sums = (sums + near) + (far + both)
    cell_count = float(NZ * BX * 256 * lax.axis_size("gx") * lax.axis_size("gy"))
    parts = high_x, low_x, high_t, low_t, high_xe, low_xe, high_te, low_te
    modes_next, factor = apply_map(sums, parts, cell_count)
    return (mean_next, modes_next, factor)


def solution(mesh):
    plane = P(None, "gx", "gy")
    return jax.shard_map(
        shards,
        mesh=mesh,
        in_specs=(plane, P(None, None, "gx", "gy"), plane, plane, plane, plane, plane),
        out_specs=(plane, P(None, None, "gx", "gy"), P()),
        check_vma=False,
    )
```

```python
import jax
import jax.numpy as jnp
from jax import lax
from jax.experimental import pallas as pl
from jax.experimental.pallas import tpu as pltpu
from jax.sharding import PartitionSpec as P

time_step = 0.1
horiz_diff = 0.05
vert_diff = 0.2

M = 16
F = 17
NZ = 16
BX = 16
LANES = 128
ROWS = 3 * NZ
SLOTS = 4
GROUP = 4
TAIL = 8 + 8 * F
HIGH = lax.Precision.HIGHEST
f32 = jnp.float32
bf16 = jnp.bfloat16

ANY = pl.BlockSpec(memory_space=pl.ANY)
HBM = pl.BlockSpec(memory_space=pltpu.HBM)
VMEM = pl.BlockSpec(memory_space=pltpu.VMEM)


def params(mib):
    return pltpu.CompilerParams(vmem_limit_bytes=mib * 1024 * 1024)


def cost(flops, nbytes):
    return pl.CostEstimate(flops=flops, bytes_accessed=nbytes, transcendentals=0)


def rolled(value, shift, axis):
    shift = shift % value.shape[axis]
    return value if shift == 0 else pltpu.roll(value, shift, axis)


def lane_ids():
    return lax.broadcasted_iota(jnp.int32, (8, LANES), 1)


def row_ids():
    return lax.broadcasted_iota(jnp.int32, (8, LANES), 0)


def lane_half(ref, half):
    where = (slice(None),) * (len(ref.shape) - 1) + (pl.ds(LANES * half, LANES),)
    return ref.at[where]


def pack_rows(get, first_row):
    rows = row_ids()
    tiles = []
    for out in range(3):
        tile = None
        for z in range(8):
            low, high = max(3 * z, 8 * out), min(3 * z + 3, 8 * out + 8)
            if low >= high:
                continue
            piece = rolled(get(z), 3 * z - 8 * out - first_row, 0)
            tile = piece if tile is None else jnp.where(rows >= low - 8 * out, piece, tile)
        tiles.append(tile)
    return tiles


def pack_columns(get, shift_of):
    slot = lane_ids() // 4
    parts = [jnp.zeros((8, LANES), f32) for _ in range(4)]
    for k in range(2 * NZ):
        moved = rolled(get(k), shift_of(k), 1)
        parts[k % 4] = jnp.where(slot == k, moved, parts[k % 4])
    out = parts[0]
    for k in range(1, 4):
        out = jnp.where(slot % 4 == k, parts[k], out)
    return out


def pack_kernel(
    modes, mean, ve, vn, fe, fn, mask, up, down, east, west, X, V, I, sems
):
    copies = []
    for chunk in range(4):
        for half in range(2):
            copies.append(
                pltpu.make_async_copy(
                    lane_half(modes, half).at[pl.ds(4 * chunk, 4)],
                    X.at[half, pl.ds(4 * chunk, 4), :, pl.ds(8, BX)],
                    sems.at[len(copies)],
                )
            )
    for source, target in (
        (mean, lambda half: X.at[half, M, :, pl.ds(8, BX)]),
        (vn, lambda half: V.at[0, half]),
        (ve, lambda half: V.at[1, half]),
        (fn, lambda half: I.at[0, half]),
        (mask, lambda half: I.at[1, half]),
        (fe, lambda half: I.at[2, half]),
    ):
        for half in range(2):
            copies.append(
                pltpu.make_async_copy(lane_half(source, half), target(half), sems.at[len(copies)])
            )
    for copy in copies:
        copy.start()
    zero_tile = jnp.zeros((8, LANES), f32)

    def clear(f, carry):
        for half in range(2):
            for z in range(NZ):
                X[half, f, z, 0:8, :] = zero_tile
                X[half, f, z, 24:32, :] = zero_tile
        return carry

    lax.fori_loop(0, F, clear, 0, unroll=True)

    def field(f, carry):
        for half in range(2):
            for zh in range(2):
                for target, tile, first in ((up, 1, 5), (down, 0, 0)):
                    tiles = pack_rows(
                        lambda z: X[half, f, 8 * zh + z, 8 + 8 * tile : 16 + 8 * tile, :], first
                    )
                    for t in range(3):
                        target[half, f, zh, 8 * t : 8 * t + 8, :] = tiles[t]
        def tile_of(half):
            return lambda k: X[half, f, k // 2, 8 + 8 * (k % 2) : 16 + 8 * (k % 2), :]
        east[f] = pack_columns(tile_of(1), lambda k: 4 * k - 125)
        west[f] = pack_columns(tile_of(0), lambda k: 4 * k)
        return carry

    for chunk in range(4):
        copies[2 * chunk].wait()
        copies[2 * chunk + 1].wait()
        lax.fori_loop(4 * chunk, 4 * chunk + 4, field, 0, unroll=4)
    for copy in copies[8:]:
        copy.wait()
    lax.fori_loop(M, F, field, 0)
    for index, plane in enumerate(
        (
            lambda half, k: V[0, half, k // 2, 8 * (k % 2) : 8 * (k % 2) + 8, :],
            lambda half, k: I[0, half, k // 2, 8 * (k % 2) : 8 * (k % 2) + 8, :].astype(f32),
            lambda half, k: I[1, half, k // 2, 8 * (k % 2) : 8 * (k % 2) + 8, :].astype(f32),
        )
    ):
        east[F + index] = pack_columns(lambda k: plane(1, k), lambda k: 4 * k - 125)
        west[F + index] = pack_columns(lambda k: plane(0, k), lambda k: 4 * k)
    rows = row_ids()
    for half in range(2):
        for zh in range(2):

            def last_row(z):
                level = 8 * zh + z
                speed = rolled(V[1, half, level, 8:16, :], -2, 0)
                flag = rolled(I[2, half, level, 8:16, :].astype(f32), -1, 0)
                wet = I[1, half, level, 8:16, :].astype(f32)
                return jnp.where(rows == 5, speed, jnp.where(rows == 6, flag, wet))

            for target, get, first in (
                (up, last_row, 5),
                (down, lambda z: I[1, half, 8 * zh + z, 0:8, :].astype(f32), 0),
            ):
                tiles = pack_rows(get, first)
                for t in range(3):
                    target[half, F, zh, 8 * t : 8 * t + 8, :] = tiles[t]


def pack(modes, mean, ve, vn, fe, fn, mask):
    rows = jax.ShapeDtypeStruct((2, F + 1, 2, ROWS // 2, LANES), f32)
    columns = jax.ShapeDtypeStruct((F + 3, 8, LANES), f32)
    return pl.pallas_call(
        pack_kernel,
        out_shape=(
            rows,
            rows,
            columns,
            columns,
            jax.ShapeDtypeStruct((2, F, NZ, 32, LANES), f32),
        ),
        in_specs=[HBM] * 7,
        out_specs=(VMEM,) * 5,
        scratch_shapes=[
            pltpu.VMEM((2, 2, NZ, BX, LANES), f32),
            pltpu.VMEM((3, 2, NZ, BX, LANES), jnp.int32),
            pltpu.SemaphoreType.DMA((20,)),
        ],
        compiler_params=params(24),
        cost_estimate=cost(10**7, 7 * 10**6),
        name="pack",
    )(modes, mean, ve, vn, fe, fn, mask)


def along_lanes(first, second, outer, offset):
    lanes = lane_ids()
    a, b, c = (rolled(v, -offset, 1) for v in (first, second, outer))
    if offset > 0:
        inside = lanes < LANES - offset
        return jnp.where(inside, a, b), jnp.where(inside, b, c)
    outside = lanes < -offset
    return jnp.where(outside, c, a), jnp.where(outside, a, b)


def around_lanes(first, second, offset):
    lanes = lane_ids()
    a, b = (rolled(v, -offset, 1) for v in (first, second))
    kept = lanes < LANES - offset if offset > 0 else lanes >= -offset
    return jnp.where(kept, a, b), jnp.where(kept, b, a)


def cell_weights(a_low, b_low, d_low, a_high, b_high, d_high):
    return (
        2.0 * a_low,
        -13.0 * a_low - 3.0 * b_low - 2.0 * a_high,
        47.0 * a_low + 27.0 * b_low + d_low + 13.0 * a_high + 3.0 * b_high,
        27.0 * a_low + 47.0 * b_low - d_low - 47.0 * a_high - 27.0 * b_high - d_high,
        -3.0 * a_low - 13.0 * b_low - 27.0 * a_high - 47.0 * b_high + d_high,
        2.0 * b_low + 3.0 * a_high + 13.0 * b_high,
        -2.0 * b_high,
    )


def face_parts(openness, speed, flag):
    scaled = openness * speed * (1.0 / 60.0)
    return scaled * flag, scaled * (1.0 - flag), horiz_diff * openness


def split(value):
    high = value.astype(bf16)
    return high, (value - high.astype(f32)).astype(bf16)


def add_products(acc, high, low):
    dims = (((1,), (1,)), ((), ()))
    acc[0:256, :] += lax.dot_general(high, high, dims, preferred_element_type=f32)
    acc[256:512, :] += lax.dot_general(low, high, dims, preferred_element_type=f32)


def joined(upper, lower):
    return jnp.concatenate([both(upper, lower, z) for z in range(NZ)], axis=1)


def both(upper, lower, z):
    return jnp.concatenate([upper[z], lower[z]], axis=0)


def field_sums(acc):
    rows = lax.broadcasted_iota(jnp.int32, (512, 256), 0)
    columns = lax.broadcasted_iota(jnp.int32, (512, 256), 1)
    kept = jnp.where(rows % 8 == columns % 8, acc[...], 0.0)
    by_row = jnp.sum(kept.reshape(64, 8, 256), axis=1)
    gather = (
        lax.broadcasted_iota(jnp.int32, (256, 32), 0) // 8
        == lax.broadcasted_iota(jnp.int32, (256, 32), 1)
    ).astype(f32)
    return jnp.dot(by_row, gather, precision=HIGH, preferred_element_type=f32)


def prepare_kernel(
    X, ve, vn, fe, fn, mask,
    high_in, low_in, high_edge, low_edge, edge_out, VE, FE, W, VN, FN, ints, Z, sems,
):
    zero_tile = jnp.zeros((8, LANES), f32)
    copies = []
    for half in range(2):
        for source, target in (
            (ve, VE.at[half, :, pl.ds(8, BX)]),
            (vn, VN.at[half]),
            (mask, ints.at[0, half]),
            (fn, ints.at[1, half]),
            (fe, ints.at[2, half]),
        ):
            copies.append(
                pltpu.make_async_copy(lane_half(source, half), target, sems.at[len(copies)])
            )
    for copy in copies:
        copy.start()
    low_rows = row_ids() < 4
    for half in range(2):
        for z in range(NZ):
            edge_out[z, half, 0:8, :] = zero_tile
            edge_out[z, half, TAIL : TAIL + 8, :] = zero_tile

    def level(z, carry):
        for half in range(2):
            columns = slice(LANES * half, LANES * half + LANES)
            for f in range(F):
                first, second = X[half, f, z, 8:16, :], X[half, f, z, 16:24, :]
                edge = jnp.where(low_rows, first, second)
                edge_out[z, half, 8 + 8 * f : 16 + 8 * f, :] = edge
                if f < M:
                    Z[0, 8 * f : 8 * f + 8, columns] = jnp.where(low_rows, second, first)
                    Z[1, 8 * f : 8 * f + 8, columns] = edge
        high_in[z], low_in[z] = split(Z[0])
        high_edge[z], low_edge[z] = split(Z[1])
        return carry

    lax.fori_loop(0, NZ, level, 0, unroll=2)
    for copy in copies:
        copy.wait()
    for half in range(2):
        for z in range(NZ):
            VE[half, z, 0:8, :] = zero_tile
            FE[half, z, 0:8, :] = zero_tile
            W[half, z, 0:8, :] = zero_tile
            W[half, z, 24:32, :] = zero_tile
            for xt in range(2):
                rows = slice(8 * xt, 8 * xt + 8)
                padded = slice(8 * xt + 8, 8 * xt + 16)
                W[half, z, padded, :] = ints[0, half, z, rows, :].astype(f32)
                FN[half, z, rows, :] = ints[1, half, z, rows, :].astype(f32)
                FE[half, z, padded, :] = ints[2, half, z, rows, :].astype(f32)


def prepare(cells, ve, vn, fe, fn, mask):
    parts = jax.ShapeDtypeStruct((NZ, 8 * M, 256), bf16)
    padded = jax.ShapeDtypeStruct((2, NZ, 32, LANES), f32)
    plain = jax.ShapeDtypeStruct((2, NZ, BX, LANES), f32)
    return pl.pallas_call(
        prepare_kernel,
        out_shape=(
            parts,
            parts,
            parts,
            parts,
            jax.ShapeDtypeStruct((NZ, 2, TAIL + 8, LANES), f32),
            padded,
            padded,
            padded,
            plain,
            plain,
        ),
        in_specs=[VMEM] + [HBM] * 5,
        out_specs=(VMEM,) * 10,
        scratch_shapes=[
            pltpu.VMEM((3, 2, NZ, BX, LANES), jnp.int32),
            pltpu.VMEM((2, 8 * M, 256), f32),
            pltpu.SemaphoreType.DMA((10,)),
        ],
        compiler_params=params(16),
        cost_estimate=cost(10**6, 10**6),
        name="prepare",
    )(cells, ve, vn, fe, fn, mask)


def interior_kernel(
    X, VE, FE, W, VN, FN, high_in, low_in, west, east, own_last, own_first,
    high_out, low_out, edge_out, weights_out, mean_out, sums_out,
    H, C, G, T, Z, acc,
):
    acc[...] = jnp.zeros((512, 256), f32)
    lanes = lane_ids()
    rows = row_ids()

    for f in range(F, F + 3):
        after, before = east[f], west[f]
        for k in range(2 * NZ):
            H[f - F, k] = jnp.where(
                lanes < 64, rolled(after, -4 * k, 1), rolled(before, LANES - 3 - 4 * k, 1)
            )

    place = lanes % 4

    (v_in, f_in, w_in) = (west[F + i] for i in range(3))
    (v_own, f_own, w_own) = (own_first[F + i] for i in range(3))
    lower_of = lambda outer_plane, own: jnp.where(
        place == 0, rolled(outer_plane, -2, 1), rolled(own, 1, 1)
    )
    low_face = face_parts(
        lower_of(w_in, w_own) * w_own, lower_of(v_in, v_own), lower_of(f_in, f_own)
    )
    high_face = face_parts(w_own * rolled(w_own, -1, 1), v_own, f_own)
    first_gains = cell_weights(*low_face, *high_face)
    for d in range(1, 4):
        G[d - 1] = jnp.where(place < d, first_gains[3 - d], 0.0)
    w_next = east[F + 2]
    (v_own, f_own, w_own) = (own_last[F + i] for i in range(3))
    high_face = face_parts(
        w_own * jnp.where(place == 2, rolled(w_next, 2, 1), rolled(w_own, -1, 1)), v_own, f_own
    )
    low_face = tuple(rolled(part, 1, 1) for part in high_face)
    last_gains = cell_weights(*low_face, *high_face)
    for d in range(1, 4):
        G[2 + d] = jnp.where((place >= 3 - d) & (place < 3), last_gains[3 + d], 0.0)

    def beside(f):
        before, after = west[f], east[f]
        first = (
            G[0] * rolled(before, -2, 1) + G[1] * rolled(before, -1, 1) + G[2] * before
        )
        last = G[3] * rolled(after, 2, 1) + G[4] * rolled(after, 1, 1) + G[5] * after
        C[0, f] = first
        C[1, f] = rolled(last, LANES - 3, 1)

    for f in range(F):
        beside(f)

    def level(z, carry):
        z_up = jnp.minimum(z + 1, NZ - 1)
        z_down = jnp.maximum(z - 1, 0)
        for xt in range(2):
            start = 8 + 8 * xt

            def outer(index):
                return H[index - F, 2 * z + xt]

            def at(ref, half, offset):
                return ref[half, z, start + offset : start + offset + 8, :]

            wet = [at(W, half, 0) for half in range(2)]
            wx = []
            for half in range(2):
                before = wet[half] * at(W, half, -1)
                after = wet[half] * at(W, half, 1)
                wx.append(
                    cell_weights(
                        *face_parts(before, at(VE, half, -1), at(FE, half, -1)),
                        *face_parts(after, at(VE, half, 0), at(FE, half, 0)),
                    )
                )
            wet_out = outer(F + 2)
            following = along_lanes(wet[0], wet[1], wet_out, 1)
            own = [
                face_parts(
                    wet[half] * following[half],
                    VN[half, z, 8 * xt : 8 * xt + 8, :],
                    FN[half, z, 8 * xt : 8 * xt + 8, :],
                )
                for half in range(2)
            ]
            beyond = face_parts(wet_out * rolled(wet[0], -1, 1), outer(F), outer(F + 1))
            before = [along_lanes(own[0][i], own[1][i], beyond[i], -1) for i in range(3)]
            wy = [
                cell_weights(*(before[i][half] for i in range(3)), *own[half]) for half in range(2)
            ]
            wy = [
                [
                    jnp.where(
                        (lanes < 3 - j) if half == 0 else (lanes >= LANES + 3 - j), 0.0, wy[half][j]
                    )
                    if (half == 0) == (j < 3) and j != 3
                    else wy[half][j]
                    for j in range(7)
                ]
                for half in range(2)
            ]
            centre = [
                wx[half][3] + wy[half][3] - 2.0 * vert_diff * wet[half] for half in range(2)
            ]
            w_level = [vert_diff * wet[half] for half in range(2)]
            for half in range(2):
                for index, plane in enumerate((at(VE, half, 0), at(FE, half, 0), wet[half])):
                    if xt == 0:
                        weights_out[half, z, 3 + index] = plane
                    else:
                        weights_out[half, z, 3 + index] = jnp.where(
                            rows < 4, weights_out[half, z, 3 + index], plane
                        )
                for d in range(1, 4):
                    if xt == 0:
                        weights_out[half, z, d - 1] = jnp.where(rows < d, wx[half][3 - d], 0.0)
                    else:
                        weights_out[half, z, d - 1] += jnp.where(
                            rows >= 8 - d, wx[half][3 + d], 0.0
                        )
            for f in range(F):
                own_cells = [X[half, f, z, start : start + 8, :] for half in range(2)]
                total = [
                    centre[half] * own_cells[half]
                    + w_level[half]
                    * (
                        X[half, f, z_up, start : start + 8, :]
                        + X[half, f, z_down, start : start + 8, :]
                    )
                    for half in range(2)
                ]
                first, last = C[0, f], C[1, f]
                total[0] += jnp.where(lanes < 3, first, 0.0)
                total[1] += jnp.where(lanes >= LANES - 3, last, 0.0)
                C[0, f] = rolled(first, -4, 1)
                C[1, f] = rolled(last, -4, 1)
                for offset in (-3, -2, -1, 1, 2, 3):
                    moved = around_lanes(own_cells[0], own_cells[1], offset)
                    for half in range(2):
                        total[half] += wx[half][3 + offset] * X[
                            half, f, z, start + offset : start + offset + 8, :
                        ]
                        total[half] += wy[half][3 + offset] * moved[half]
                for half in range(2):
                    columns = slice(LANES * half, LANES * half + LANES)
                    low_rows = rows < 4
                    if f == M:
                        mean_out[z, 8 * xt : 8 * xt + 8, columns] = (
                            own_cells[half] + time_step * total[half]
                        )
                    elif xt == 0:
                        T[half, f] = total[half]
                    else:
                        near = T[half, f]
                        place = slice(8 * f, 8 * f + 8)
                        Z[place, columns] = jnp.where(low_rows, total[half], near)
                        edge_out[z, half, place, :] = jnp.where(low_rows, near, total[half])
        high, low = split(Z[...])
        high_out[z] = high
        low_out[z] = low
        return carry

    lax.fori_loop(0, NZ, level, 0)
    add_products(acc, joined(high_in, high_out), joined(low_in, low_out))
    sums_out[...] = field_sums(acc)


def interior(cells, planes, high_in, low_in, west, east, own_last, own_first):
    parts = jax.ShapeDtypeStruct((NZ, 8 * M, 256), bf16)
    return pl.pallas_call(
        interior_kernel,
        out_shape=(
            parts,
            parts,
            jax.ShapeDtypeStruct((NZ, 2, 8 * M, LANES), f32),
            jax.ShapeDtypeStruct((2, NZ, 6, 8, LANES), f32),
            jax.ShapeDtypeStruct((NZ, BX, 2 * LANES), f32),
            jax.ShapeDtypeStruct((64, 32), f32),
        ),
        in_specs=[VMEM] * 12,
        out_specs=(VMEM,) * 6,
        scratch_shapes=[
            pltpu.VMEM((3, 2 * NZ, 8, LANES), f32),
            pltpu.VMEM((2, F, 8, LANES), f32),
            pltpu.VMEM((6, 8, LANES), f32),
            pltpu.VMEM((2, M, 8, LANES), f32),
            pltpu.VMEM((8 * M, 256), f32),
            pltpu.VMEM((512, 256), f32),
        ],
        compiler_params=params(20),
        cost_estimate=cost(10**6, 10**6),
        name="interior",
    )(cells, *planes, high_in, low_in, west, east, own_last, own_first)


def edge_kernel(
    below, above, edge_in, edge_tail, high_in, low_in, weights, mean_in, sums_in,
    high_out, low_out, mean_out, sums_out, Z, acc,
):
    acc[...] = jnp.zeros((512, 256), f32)
    rows = row_ids()
    low_rows = rows < 4
    first_row = rows == 0
    last_row = rows == 7

    def rows_from(ref, half, f, zh, first):
        start = min(max(first, 0), 16)
        return rolled(ref[half, f, zh, start : start + 8, :], start - first, 0)

    def gains_of(half, z, zh, zi):
        speed, flag, wet = (weights[half, z, 3 + i] for i in range(3))
        speed = jnp.where(first_row, rows_from(below, half, F, zh, 3 * zi), speed)
        flag = jnp.where(first_row, rows_from(below, half, F, zh, 3 * zi + 1), flag)
        beyond = jnp.where(first_row, rows_from(below, half, F, zh, 3 * zi + 2), 0.0)
        beyond = jnp.where(last_row, rows_from(above, half, F, zh, 3 * zi - 7), beyond)
        a, b, d = face_parts(beyond * wet, speed, flag)
        near, far = 47.0 * a + 27.0 * b + d, 27.0 * a + 47.0 * b - d
        left, right = -13.0 * a - 3.0 * b, -3.0 * a - 13.0 * b
        outside = (
            weights[half, z, 0] + jnp.where(first_row, near, -far),
            weights[half, z, 1] + jnp.where(first_row, left, -right),
            weights[half, z, 2] + jnp.where(first_row, 2.0 * a, -2.0 * b),
        )
        inside = (
            jnp.where(first_row, far, -near),
            jnp.where(first_row, right, -left),
            jnp.where(first_row, 2.0 * b, -2.0 * a),
        )
        return outside, inside

    def group(zh, carry):
        for zi in range(8):
            z = 8 * zh + zi
            for half in range(2):
                outside, inside = gains_of(half, z, zh, zi)
                for f in range(F):
                    base = 8 + 8 * f
                    change = inside[0] * edge_in[z, half, base : base + 8, :]
                    for d in range(1, 4):
                        cells = jnp.where(
                            low_rows,
                            rows_from(below, half, f, zh, 3 * zi + 3 - d),
                            rows_from(above, half, f, zh, 3 * zi + d - 8),
                        )
                        change = change + outside[d - 1] * cells
                    for d in range(1, 3):
                        cells = jnp.where(
                            low_rows,
                            edge_in[z, half, base + d : base + d + 8, :],
                            edge_in[z, half, base - d : base - d + 8, :],
                        )
                        change = change + inside[d] * cells
                    if f < M:
                        Z[half, 8 * f : 8 * f + 8, :] = (
                            edge_tail[z, half, 8 * f : 8 * f + 8, :] + change
                        )
                    else:
                        columns = slice(LANES * half, LANES * half + LANES)
                        step = time_step * change
                        mean_out[z, 0:8, columns] = mean_in[z, 0:8, columns] + jnp.where(
                            low_rows, step, 0.0
                        )
                        mean_out[z, 8:16, columns] = mean_in[z, 8:16, columns] + jnp.where(
                            low_rows, 0.0, step
                        )
            high, low = split(jnp.concatenate([Z[0], Z[1]], axis=1))
            high_out[z] = high
            low_out[z] = low
            add_products(
                acc,
                jnp.concatenate([high_in[z], high], axis=0),
                jnp.concatenate([low_in[z], low], axis=0),
            )
        return carry

    lax.fori_loop(0, 2, group, 0)
    sums = sums_in[...] + field_sums(acc)
    identity = (
        lax.broadcasted_iota(jnp.int32, (32, 32), 0) == lax.broadcasted_iota(jnp.int32, (32, 32), 1)
    ).astype(f32)
    turned = lax.dot_general(
        identity, sums[32:64], (((1,), (1,)), ((), ())), precision=HIGH, preferred_element_type=f32
    )
    whole = sums[0:32] + sums[32:64] + turned
    sums_out[...] = jnp.concatenate([whole[8 * i : 8 * i + 8] for i in range(4)], axis=1)


def edges(below, above, edge_in, edge_tail, high_in, low_in, weights, mean_in, sums_in):
    parts = jax.ShapeDtypeStruct((NZ, 8 * M, 256), bf16)
    return pl.pallas_call(
        edge_kernel,
        out_shape=(
            parts,
            parts,
            jax.ShapeDtypeStruct(mean_in.shape, f32),
            jax.ShapeDtypeStruct((8, LANES), f32),
        ),
        in_specs=[VMEM] * 9,
        out_specs=(VMEM,) * 4,
        scratch_shapes=[
            pltpu.VMEM((2, 8 * M, LANES), f32),
            pltpu.VMEM((512, 256), f32),
        ],
        compiler_params=params(16),
        cost_estimate=cost(10**9, 10**7),
        name="edges",
    )(below, above, edge_in, edge_tail, high_in, low_in, weights, mean_in, sums_in)


def factor_and_map(sums, cell_count):
    whole = jnp.concatenate([sums[:, 32 * i : 32 * i + 32] for i in range(4)], axis=0)
    inner = whole * (1.0 / cell_count)
    row = lax.broadcasted_iota(jnp.int32, (M, 2 * M), 0)
    column = lax.broadcasted_iota(jnp.int32, (M, 2 * M), 1)
    update = jnp.where(
        column < M,
        jnp.where(column == row, 1.0, 0.0) - time_step * inner[M : 2 * M, :],
        jnp.where(column == row + M, time_step, 0.0),
    )
    half_way = jnp.dot(update, inner, precision=HIGH, preferred_element_type=f32)
    gram = lax.dot_general(
        half_way, update, (((1,), (1,)), ((), ())), precision=HIGH, preferred_element_type=f32
    )
    row_g = lax.broadcasted_iota(jnp.int32, (M, M), 0)
    column_g = lax.broadcasted_iota(jnp.int32, (M, M), 1)
    left, right = gram, update
    for j in range(M):
        pivot = jnp.sum(jnp.where(column_g == j, left, 0.0), axis=1, keepdims=True)
        scale = 1.0 / jnp.sqrt(pivot[j : j + 1, :])
        left_row = left[j : j + 1, :] * scale
        right_row = right[j : j + 1, :] * scale
        share = jnp.where(row_g[:, 0:1] > j, pivot * scale, 0.0)
        left = jnp.where(row_g == j, left_row, left - share * left_row)
        right = jnp.where(row == j, right_row, right - share * right_row)
    return jnp.where(column_g >= row_g, left, 0.0), right


def spread_map(mapping):
    parts = jnp.concatenate(split(mapping), axis=0)
    tall = (
        lax.broadcasted_iota(jnp.int32, (256, 2 * M), 0) // 8
        == lax.broadcasted_iota(jnp.int32, (256, 2 * M), 1)
    ).astype(bf16)
    wide = (
        lax.broadcasted_iota(jnp.int32, (2 * M, 256), 1) // 8
        == lax.broadcasted_iota(jnp.int32, (2 * M, 256), 0)
    ).astype(bf16)
    rows = jnp.dot(tall, parts, preferred_element_type=f32).astype(bf16)
    full = jnp.dot(rows, wide, preferred_element_type=f32)
    row = lax.broadcasted_iota(jnp.int32, (256, 256), 0)
    column = lax.broadcasted_iota(jnp.int32, (256, 256), 1)
    return jnp.where(row % 8 == column % 8, full, 0.0).astype(bf16)


def make_apply_kernel(cell_count):
    def apply_kernel(sums, *refs):
        parts, (out, factor_out, maps, new, sems) = refs[:8], refs[8:]
        factor, mapping = factor_and_map(sums[...], cell_count)
        factor_out[...] = factor
        maps[...] = spread_map(mapping)
        low_rows = lax.broadcasted_iota(jnp.int32, (M, 8, 256), 1) < 4

        def put(group, slot):
            return pltpu.make_async_copy(
                new.at[slot], out.at[:, pl.ds(GROUP * group, GROUP)], sems.at[slot]
            )

        for group in range(NZ // GROUP):
            slot = group % SLOTS
            if group >= SLOTS:
                put(group - SLOTS, slot).wait()
            for k in range(GROUP):
                z = GROUP * group + k
                results = []
                for i in (0, 4):
                    high = both(parts[i], parts[i + 2], z)
                    low = both(parts[i + 1], parts[i + 3], z)
                    first = jnp.dot(maps[...], high, preferred_element_type=f32)
                    second = jnp.dot(maps[0:128, :], low, preferred_element_type=f32)
                    results.append((first[0:128] + first[128:256] + second).reshape(M, 8, 256))
                inner, edge = results
                new[slot, :, k, 0:8, :] = jnp.where(low_rows, edge, inner)
                new[slot, :, k, 8:16, :] = jnp.where(low_rows, inner, edge)
            put(group, slot).start()
        for group in range(NZ // GROUP - SLOTS, NZ // GROUP):
            put(group, group % SLOTS).wait()

    return apply_kernel


def apply_map(sums, parts, cell_count):
    return pl.pallas_call(
        make_apply_kernel(cell_count),
        out_shape=(
            jax.ShapeDtypeStruct((M, NZ, BX, 256), f32),
            jax.ShapeDtypeStruct((M, M), f32),
        ),
        in_specs=[VMEM] * 9,
        out_specs=(ANY, VMEM),
        scratch_shapes=[
            pltpu.VMEM((256, 256), bf16),
            pltpu.VMEM((SLOTS, M, GROUP, BX, 256), f32),
            pltpu.SemaphoreType.DMA((SLOTS,)),
        ],
        compiler_params=params(16),
        cost_estimate=cost(10**9, 13 * 10**6),
        name="apply",
    )(sums, *parts)


def onward(value, axis):
    size = lax.axis_size(axis)
    return lax.ppermute(value, axis, [(i, i + 1) for i in range(size - 1)])


def backward(value, axis):
    size = lax.axis_size(axis)
    return lax.ppermute(value, axis, [(i + 1, i) for i in range(size - 1)])


def exchanged(value, axes, distance):
    size = lax.axis_size(axes)
    return lax.ppermute(value, axes, [(i, i ^ distance) for i in range(size)])


def shards(
    mean_field, mode_fields, velocity_east, velocity_north, flag_east, flag_north, ocean_mask
):
    axes = ("gx", "gy")
    (
        mean_field, mode_fields, velocity_east, velocity_north, flag_east, flag_north, ocean_mask
    ) = (
        pltpu.with_memory_space_constraint(value, pltpu.HBM)
        for value in (
            mean_field, mode_fields, velocity_east, velocity_north, flag_east, flag_north,
            ocean_mask,
        )
    )
    up, down, east_send, west_send, cells = pack(
        mode_fields, mean_field, velocity_east, velocity_north, flag_east, flag_north, ocean_mask
    )
    west = onward(east_send, "gy")
    east = backward(west_send, "gy")
    below = onward(up, "gx")
    above = backward(down, "gx")
    high_x, low_x, high_xe, low_xe, edge, *planes = prepare(
        cells, velocity_east, velocity_north, flag_east, flag_north, ocean_mask
    )
    high_t, low_t, edge_tail, weights, mean_part, sums_i = interior(
        cells, planes, high_x, low_x, west, east, east_send, west_send
    )
    high_te, low_te, mean_next, sums = edges(
        below, above, edge, edge_tail, high_xe, low_xe, weights, mean_part, sums_i
    )
    sums = sums + exchanged(sums, axes, 1)
    for first in (2, 8, 32):
        near, far, both = (exchanged(sums, axes, first * i) for i in (1, 2, 3))
        sums = (sums + near) + (far + both)
    cell_count = float(NZ * BX * 256 * lax.axis_size("gx") * lax.axis_size("gy"))
    parts = high_x, low_x, high_t, low_t, high_xe, low_xe, high_te, low_te
    modes_next, factor = apply_map(sums, parts, cell_count)
    return (mean_next, modes_next, factor)


def solution(mesh):
    plane = P(None, "gx", "gy")
    return jax.shard_map(
        shards,
        mesh=mesh,
        in_specs=(plane, P(None, None, "gx", "gy"), plane, plane, plane, plane, plane),
        out_specs=(plane, P(None, None, "gx", "gy"), P()),
        check_vma=False,
    )
```

```python
import jax
import jax.numpy as jnp
from jax import lax
from jax.experimental import pallas as pl
from jax.experimental.pallas import tpu as pltpu
from jax.sharding import PartitionSpec as P

time_step = 0.1
horiz_diff = 0.05
vert_diff = 0.2

M = 16
F = 17
NZ = 16
BX = 16
LANES = 128
ROWS = 3 * NZ
SLOTS = 16
GROUP = 1
TAIL = 8 + 8 * F
HIGH = lax.Precision.HIGHEST
f32 = jnp.float32
bf16 = jnp.bfloat16

ANY = pl.BlockSpec(memory_space=pl.ANY)
HBM = pl.BlockSpec(memory_space=pltpu.HBM)
VMEM = pl.BlockSpec(memory_space=pltpu.VMEM)


def params(mib):
    return pltpu.CompilerParams(vmem_limit_bytes=mib * 1024 * 1024)


def cost(flops, nbytes):
    return pl.CostEstimate(flops=flops, bytes_accessed=nbytes, transcendentals=0)


def rolled(value, shift, axis):
    shift = shift % value.shape[axis]
    return value if shift == 0 else pltpu.roll(value, shift, axis)


def lane_ids():
    return lax.broadcasted_iota(jnp.int32, (8, LANES), 1)


def row_ids():
    return lax.broadcasted_iota(jnp.int32, (8, LANES), 0)


def lane_half(ref, half):
    where = (slice(None),) * (len(ref.shape) - 1) + (pl.ds(LANES * half, LANES),)
    return ref.at[where]


def pack_rows(get, first_row):
    rows = row_ids()
    tiles = []
    for out in range(3):
        tile = None
        for z in range(8):
            low, high = max(3 * z, 8 * out), min(3 * z + 3, 8 * out + 8)
            if low >= high:
                continue
            piece = rolled(get(z), 3 * z - 8 * out - first_row, 0)
            tile = piece if tile is None else jnp.where(rows >= low - 8 * out, piece, tile)
        tiles.append(tile)
    return tiles


def pack_columns(get, shift_of):
    slot = lane_ids() // 4
    parts = [jnp.zeros((8, LANES), f32) for _ in range(4)]
    for k in range(2 * NZ):
        moved = rolled(get(k), shift_of(k), 1)
        parts[k % 4] = jnp.where(slot == k, moved, parts[k % 4])
    out = parts[0]
    for k in range(1, 4):
        out = jnp.where(slot % 4 == k, parts[k], out)
    return out


def pack_kernel(
    modes, mean, ve, vn, fe, fn, mask, up, down, east, west, X, V, I, sems
):
    copies = []
    for chunk in range(4):
        for half in range(2):
            copies.append(
                pltpu.make_async_copy(
                    lane_half(modes, half).at[pl.ds(4 * chunk, 4)],
                    X.at[half, pl.ds(4 * chunk, 4), :, pl.ds(8, BX)],
                    sems.at[len(copies)],
                )
            )
    for source, target in (
        (mean, lambda half: X.at[half, M, :, pl.ds(8, BX)]),
        (vn, lambda half: V.at[0, half]),
        (ve, lambda half: V.at[1, half]),
        (fn, lambda half: I.at[0, half]),
        (mask, lambda half: I.at[1, half]),
        (fe, lambda half: I.at[2, half]),
    ):
        for half in range(2):
            copies.append(
                pltpu.make_async_copy(lane_half(source, half), target(half), sems.at[len(copies)])
            )
    for copy in copies:
        copy.start()
    zero_tile = jnp.zeros((8, LANES), f32)

    def clear(f, carry):
        for half in range(2):
            for z in range(NZ):
                X[half, f, z, 0:8, :] = zero_tile
                X[half, f, z, 24:32, :] = zero_tile
        return carry

    lax.fori_loop(0, F, clear, 0, unroll=True)

    def field(f, carry):
        for half in range(2):
            for zh in range(2):
                for target, tile, first in ((up, 1, 5), (down, 0, 0)):
                    tiles = pack_rows(
                        lambda z: X[half, f, 8 * zh + z, 8 + 8 * tile : 16 + 8 * tile, :], first
                    )
                    for t in range(3):
                        target[half, f, zh, 8 * t : 8 * t + 8, :] = tiles[t]
        def tile_of(half):
            return lambda k: X[half, f, k // 2, 8 + 8 * (k % 2) : 16 + 8 * (k % 2), :]
        east[f] = pack_columns(tile_of(1), lambda k: 4 * k - 125)
        west[f] = pack_columns(tile_of(0), lambda k: 4 * k)
        return carry

    for chunk in range(4):
        copies[2 * chunk].wait()
        copies[2 * chunk + 1].wait()
        lax.fori_loop(4 * chunk, 4 * chunk + 4, field, 0, unroll=4)
    for copy in copies[8:]:
        copy.wait()
    lax.fori_loop(M, F, field, 0)
    for index, plane in enumerate(
        (
            lambda half, k: V[0, half, k // 2, 8 * (k % 2) : 8 * (k % 2) + 8, :],
            lambda half, k: I[0, half, k // 2, 8 * (k % 2) : 8 * (k % 2) + 8, :].astype(f32),
            lambda half, k: I[1, half, k // 2, 8 * (k % 2) : 8 * (k % 2) + 8, :].astype(f32),
        )
    ):
        east[F + index] = pack_columns(lambda k: plane(1, k), lambda k: 4 * k - 125)
        west[F + index] = pack_columns(lambda k: plane(0, k), lambda k: 4 * k)
    rows = row_ids()
    for half in range(2):
        for zh in range(2):

            def last_row(z):
                level = 8 * zh + z
                speed = rolled(V[1, half, level, 8:16, :], -2, 0)
                flag = rolled(I[2, half, level, 8:16, :].astype(f32), -1, 0)
                wet = I[1, half, level, 8:16, :].astype(f32)
                return jnp.where(rows == 5, speed, jnp.where(rows == 6, flag, wet))

            for target, get, first in (
                (up, last_row, 5),
                (down, lambda z: I[1, half, 8 * zh + z, 0:8, :].astype(f32), 0),
            ):
                tiles = pack_rows(get, first)
                for t in range(3):
                    target[half, F, zh, 8 * t : 8 * t + 8, :] = tiles[t]


def pack(modes, mean, ve, vn, fe, fn, mask):
    rows = jax.ShapeDtypeStruct((2, F + 1, 2, ROWS // 2, LANES), f32)
    columns = jax.ShapeDtypeStruct((F + 3, 8, LANES), f32)
    return pl.pallas_call(
        pack_kernel,
        out_shape=(
            rows,
            rows,
            columns,
            columns,
            jax.ShapeDtypeStruct((2, F, NZ, 32, LANES), f32),
        ),
        in_specs=[HBM] * 7,
        out_specs=(VMEM,) * 5,
        scratch_shapes=[
            pltpu.VMEM((2, 2, NZ, BX, LANES), f32),
            pltpu.VMEM((3, 2, NZ, BX, LANES), jnp.int32),
            pltpu.SemaphoreType.DMA((20,)),
        ],
        compiler_params=params(24),
        cost_estimate=cost(10**7, 7 * 10**6),
        name="pack",
    )(modes, mean, ve, vn, fe, fn, mask)


def along_lanes(first, second, outer, offset):
    lanes = lane_ids()
    a, b, c = (rolled(v, -offset, 1) for v in (first, second, outer))
    if offset > 0:
        inside = lanes < LANES - offset
        return jnp.where(inside, a, b), jnp.where(inside, b, c)
    outside = lanes < -offset
    return jnp.where(outside, c, a), jnp.where(outside, a, b)


def around_lanes(first, second, offset):
    lanes = lane_ids()
    a, b = (rolled(v, -offset, 1) for v in (first, second))
    kept = lanes < LANES - offset if offset > 0 else lanes >= -offset
    return jnp.where(kept, a, b), jnp.where(kept, b, a)


def cell_weights(a_low, b_low, d_low, a_high, b_high, d_high):
    return (
        2.0 * a_low,
        -13.0 * a_low - 3.0 * b_low - 2.0 * a_high,
        47.0 * a_low + 27.0 * b_low + d_low + 13.0 * a_high + 3.0 * b_high,
        27.0 * a_low + 47.0 * b_low - d_low - 47.0 * a_high - 27.0 * b_high - d_high,
        -3.0 * a_low - 13.0 * b_low - 27.0 * a_high - 47.0 * b_high + d_high,
        2.0 * b_low + 3.0 * a_high + 13.0 * b_high,
        -2.0 * b_high,
    )


def face_parts(openness, speed, flag):
    scaled = openness * speed * (1.0 / 60.0)
    return scaled * flag, scaled * (1.0 - flag), horiz_diff * openness


def split(value):
    high = value.astype(bf16)
    return high, (value - high.astype(f32)).astype(bf16)


def add_products(acc, high, low):
    dims = (((1,), (1,)), ((), ()))
    acc[0:256, :] += lax.dot_general(high, high, dims, preferred_element_type=f32)
    acc[256:512, :] += lax.dot_general(low, high, dims, preferred_element_type=f32)


def joined(upper, lower):
    return jnp.concatenate([both(upper, lower, z) for z in range(NZ)], axis=1)


def both(upper, lower, z):
    return jnp.concatenate([upper[z], lower[z]], axis=0)


def field_sums(acc):
    rows = lax.broadcasted_iota(jnp.int32, (512, 256), 0)
    columns = lax.broadcasted_iota(jnp.int32, (512, 256), 1)
    kept = jnp.where(rows % 8 == columns % 8, acc[...], 0.0)
    by_row = jnp.sum(kept.reshape(64, 8, 256), axis=1)
    gather = (
        lax.broadcasted_iota(jnp.int32, (256, 32), 0) // 8
        == lax.broadcasted_iota(jnp.int32, (256, 32), 1)
    ).astype(f32)
    return jnp.dot(by_row, gather, precision=HIGH, preferred_element_type=f32)


def prepare_kernel(
    X, ve, vn, fe, fn, mask,
    high_in, low_in, high_edge, low_edge, edge_out, VE, FE, W, VN, FN, ints, Z, sems,
):
    zero_tile = jnp.zeros((8, LANES), f32)
    copies = []
    for half in range(2):
        for source, target in (
            (ve, VE.at[half, :, pl.ds(8, BX)]),
            (vn, VN.at[half]),
            (mask, ints.at[0, half]),
            (fn, ints.at[1, half]),
            (fe, ints.at[2, half]),
        ):
            copies.append(
                pltpu.make_async_copy(lane_half(source, half), target, sems.at[len(copies)])
            )
    for copy in copies:
        copy.start()
    low_rows = row_ids() < 4
    for half in range(2):
        for z in range(NZ):
            edge_out[z, half, 0:8, :] = zero_tile
            edge_out[z, half, TAIL : TAIL + 8, :] = zero_tile

    def level(z, carry):
        for half in range(2):
            columns = slice(LANES * half, LANES * half + LANES)
            for f in range(F):
                first, second = X[half, f, z, 8:16, :], X[half, f, z, 16:24, :]
                edge = jnp.where(low_rows, first, second)
                edge_out[z, half, 8 + 8 * f : 16 + 8 * f, :] = edge
                if f < M:
                    Z[0, 8 * f : 8 * f + 8, columns] = jnp.where(low_rows, second, first)
                    Z[1, 8 * f : 8 * f + 8, columns] = edge
        high_in[z], low_in[z] = split(Z[0])
        high_edge[z], low_edge[z] = split(Z[1])
        return carry

    lax.fori_loop(0, NZ, level, 0, unroll=2)
    for copy in copies:
        copy.wait()
    for half in range(2):
        for z in range(NZ):
            VE[half, z, 0:8, :] = zero_tile
            FE[half, z, 0:8, :] = zero_tile
            W[half, z, 0:8, :] = zero_tile
            W[half, z, 24:32, :] = zero_tile
            for xt in range(2):
                rows = slice(8 * xt, 8 * xt + 8)
                padded = slice(8 * xt + 8, 8 * xt + 16)
                W[half, z, padded, :] = ints[0, half, z, rows, :].astype(f32)
                FN[half, z, rows, :] = ints[1, half, z, rows, :].astype(f32)
                FE[half, z, padded, :] = ints[2, half, z, rows, :].astype(f32)


def prepare(cells, ve, vn, fe, fn, mask):
    parts = jax.ShapeDtypeStruct((NZ, 8 * M, 256), bf16)
    padded = jax.ShapeDtypeStruct((2, NZ, 32, LANES), f32)
    plain = jax.ShapeDtypeStruct((2, NZ, BX, LANES), f32)
    return pl.pallas_call(
        prepare_kernel,
        out_shape=(
            parts,
            parts,
            parts,
            parts,
            jax.ShapeDtypeStruct((NZ, 2, TAIL + 8, LANES), f32),
            padded,
            padded,
            padded,
            plain,
            plain,
        ),
        in_specs=[VMEM] + [HBM] * 5,
        out_specs=(VMEM,) * 10,
        scratch_shapes=[
            pltpu.VMEM((3, 2, NZ, BX, LANES), jnp.int32),
            pltpu.VMEM((2, 8 * M, 256), f32),
            pltpu.SemaphoreType.DMA((10,)),
        ],
        compiler_params=params(16),
        cost_estimate=cost(10**6, 10**6),
        name="prepare",
    )(cells, ve, vn, fe, fn, mask)


def interior_kernel(
    X, VE, FE, W, VN, FN, high_in, low_in, west, east, own_last, own_first,
    high_out, low_out, edge_out, weights_out, mean_out, sums_out,
    H, C, G, T, Z, acc,
):
    acc[...] = jnp.zeros((512, 256), f32)
    lanes = lane_ids()
    rows = row_ids()

    for f in range(F, F + 3):
        after, before = east[f], west[f]
        for k in range(2 * NZ):
            H[f - F, k] = jnp.where(
                lanes < 64, rolled(after, -4 * k, 1), rolled(before, LANES - 3 - 4 * k, 1)
            )

    place = lanes % 4

    (v_in, f_in, w_in) = (west[F + i] for i in range(3))
    (v_own, f_own, w_own) = (own_first[F + i] for i in range(3))
    lower_of = lambda outer_plane, own: jnp.where(
        place == 0, rolled(outer_plane, -2, 1), rolled(own, 1, 1)
    )
    low_face = face_parts(
        lower_of(w_in, w_own) * w_own, lower_of(v_in, v_own), lower_of(f_in, f_own)
    )
    high_face = face_parts(w_own * rolled(w_own, -1, 1), v_own, f_own)
    first_gains = cell_weights(*low_face, *high_face)
    for d in range(1, 4):
        G[d - 1] = jnp.where(place < d, first_gains[3 - d], 0.0)
    w_next = east[F + 2]
    (v_own, f_own, w_own) = (own_last[F + i] for i in range(3))
    high_face = face_parts(
        w_own * jnp.where(place == 2, rolled(w_next, 2, 1), rolled(w_own, -1, 1)), v_own, f_own
    )
    low_face = tuple(rolled(part, 1, 1) for part in high_face)
    last_gains = cell_weights(*low_face, *high_face)
    for d in range(1, 4):
        G[2 + d] = jnp.where((place >= 3 - d) & (place < 3), last_gains[3 + d], 0.0)

    def beside(f):
        before, after = west[f], east[f]
        first = (
            G[0] * rolled(before, -2, 1) + G[1] * rolled(before, -1, 1) + G[2] * before
        )
        last = G[3] * rolled(after, 2, 1) + G[4] * rolled(after, 1, 1) + G[5] * after
        C[0, f] = first
        C[1, f] = rolled(last, LANES - 3, 1)

    for f in range(F):
        beside(f)

    def level(z, carry):
        z_up = jnp.minimum(z + 1, NZ - 1)
        z_down = jnp.maximum(z - 1, 0)
        for xt in range(2):
            start = 8 + 8 * xt

            def outer(index):
                return H[index - F, 2 * z + xt]

            def at(ref, half, offset):
                return ref[half, z, start + offset : start + offset + 8, :]

            wet = [at(W, half, 0) for half in range(2)]
            wx = []
            for half in range(2):
                before = wet[half] * at(W, half, -1)
                after = wet[half] * at(W, half, 1)
                wx.append(
                    cell_weights(
                        *face_parts(before, at(VE, half, -1), at(FE, half, -1)),
                        *face_parts(after, at(VE, half, 0), at(FE, half, 0)),
                    )
                )
            wet_out = outer(F + 2)
            following = along_lanes(wet[0], wet[1], wet_out, 1)
            own = [
                face_parts(
                    wet[half] * following[half],
                    VN[half, z, 8 * xt : 8 * xt + 8, :],
                    FN[half, z, 8 * xt : 8 * xt + 8, :],
                )
                for half in range(2)
            ]
            beyond = face_parts(wet_out * rolled(wet[0], -1, 1), outer(F), outer(F + 1))
            before = [along_lanes(own[0][i], own[1][i], beyond[i], -1) for i in range(3)]
            wy = [
                cell_weights(*(before[i][half] for i in range(3)), *own[half]) for half in range(2)
            ]
            wy = [
                [
                    jnp.where(
                        (lanes < 3 - j) if half == 0 else (lanes >= LANES + 3 - j), 0.0, wy[half][j]
                    )
                    if (half == 0) == (j < 3) and j != 3
                    else wy[half][j]
                    for j in range(7)
                ]
                for half in range(2)
            ]
            centre = [
                wx[half][3] + wy[half][3] - 2.0 * vert_diff * wet[half] for half in range(2)
            ]
            w_level = [vert_diff * wet[half] for half in range(2)]
            for half in range(2):
                for index, plane in enumerate((at(VE, half, 0), at(FE, half, 0), wet[half])):
                    if xt == 0:
                        weights_out[half, z, 3 + index] = plane
                    else:
                        weights_out[half, z, 3 + index] = jnp.where(
                            rows < 4, weights_out[half, z, 3 + index], plane
                        )
                for d in range(1, 4):
                    if xt == 0:
                        weights_out[half, z, d - 1] = jnp.where(rows < d, wx[half][3 - d], 0.0)
                    else:
                        weights_out[half, z, d - 1] += jnp.where(
                            rows >= 8 - d, wx[half][3 + d], 0.0
                        )
            for f in range(F):
                own_cells = [X[half, f, z, start : start + 8, :] for half in range(2)]
                total = [
                    centre[half] * own_cells[half]
                    + w_level[half]
                    * (
                        X[half, f, z_up, start : start + 8, :]
                        + X[half, f, z_down, start : start + 8, :]
                    )
                    for half in range(2)
                ]
                first, last = C[0, f], C[1, f]
                total[0] += jnp.where(lanes < 3, first, 0.0)
                total[1] += jnp.where(lanes >= LANES - 3, last, 0.0)
                C[0, f] = rolled(first, -4, 1)
                C[1, f] = rolled(last, -4, 1)
                for offset in (-3, -2, -1, 1, 2, 3):
                    moved = around_lanes(own_cells[0], own_cells[1], offset)
                    for half in range(2):
                        total[half] += wx[half][3 + offset] * X[
                            half, f, z, start + offset : start + offset + 8, :
                        ]
                        total[half] += wy[half][3 + offset] * moved[half]
                for half in range(2):
                    columns = slice(LANES * half, LANES * half + LANES)
                    low_rows = rows < 4
                    if f == M:
                        mean_out[z, 8 * xt : 8 * xt + 8, columns] = (
                            own_cells[half] + time_step * total[half]
                        )
                    elif xt == 0:
                        T[half, f] = total[half]
                    else:
                        near = T[half, f]
                        place = slice(8 * f, 8 * f + 8)
                        Z[place, columns] = jnp.where(low_rows, total[half], near)
                        edge_out[z, half, place, :] = jnp.where(low_rows, near, total[half])
        high, low = split(Z[...])
        high_out[z] = high
        low_out[z] = low
        return carry

    lax.fori_loop(0, NZ, level, 0, unroll=2)
    add_products(acc, joined(high_in, high_out), joined(low_in, low_out))
    sums_out[...] = field_sums(acc)


def interior(cells, planes, high_in, low_in, west, east, own_last, own_first):
    parts = jax.ShapeDtypeStruct((NZ, 8 * M, 256), bf16)
    return pl.pallas_call(
        interior_kernel,
        out_shape=(
            parts,
            parts,
            jax.ShapeDtypeStruct((NZ, 2, 8 * M, LANES), f32),
            jax.ShapeDtypeStruct((2, NZ, 6, 8, LANES), f32),
            jax.ShapeDtypeStruct((NZ, BX, 2 * LANES), f32),
            jax.ShapeDtypeStruct((64, 32), f32),
        ),
        in_specs=[VMEM] * 12,
        out_specs=(VMEM,) * 6,
        scratch_shapes=[
            pltpu.VMEM((3, 2 * NZ, 8, LANES), f32),
            pltpu.VMEM((2, F, 8, LANES), f32),
            pltpu.VMEM((6, 8, LANES), f32),
            pltpu.VMEM((2, M, 8, LANES), f32),
            pltpu.VMEM((8 * M, 256), f32),
            pltpu.VMEM((512, 256), f32),
        ],
        compiler_params=params(20),
        cost_estimate=cost(10**6, 10**6),
        name="interior",
    )(cells, *planes, high_in, low_in, west, east, own_last, own_first)


def edge_kernel(
    below, above, edge_in, edge_tail, high_in, low_in, weights, mean_in, sums_in,
    high_out, low_out, mean_out, sums_out, Z, acc,
):
    acc[...] = jnp.zeros((512, 256), f32)
    rows = row_ids()
    low_rows = rows < 4
    first_row = rows == 0
    last_row = rows == 7

    def rows_from(ref, half, f, zh, first):
        start = min(max(first, 0), 16)
        return rolled(ref[half, f, zh, start : start + 8, :], start - first, 0)

    def gains_of(half, z, zh, zi):
        speed, flag, wet = (weights[half, z, 3 + i] for i in range(3))
        speed = jnp.where(first_row, rows_from(below, half, F, zh, 3 * zi), speed)
        flag = jnp.where(first_row, rows_from(below, half, F, zh, 3 * zi + 1), flag)
        beyond = jnp.where(first_row, rows_from(below, half, F, zh, 3 * zi + 2), 0.0)
        beyond = jnp.where(last_row, rows_from(above, half, F, zh, 3 * zi - 7), beyond)
        a, b, d = face_parts(beyond * wet, speed, flag)
        near, far = 47.0 * a + 27.0 * b + d, 27.0 * a + 47.0 * b - d
        left, right = -13.0 * a - 3.0 * b, -3.0 * a - 13.0 * b
        outside = (
            weights[half, z, 0] + jnp.where(first_row, near, -far),
            weights[half, z, 1] + jnp.where(first_row, left, -right),
            weights[half, z, 2] + jnp.where(first_row, 2.0 * a, -2.0 * b),
        )
        inside = (
            jnp.where(first_row, far, -near),
            jnp.where(first_row, right, -left),
            jnp.where(first_row, 2.0 * b, -2.0 * a),
        )
        return outside, inside

    def group(zh, carry):
        for zi in range(8):
            z = 8 * zh + zi
            for half in range(2):
                outside, inside = gains_of(half, z, zh, zi)
                for f in range(F):
                    base = 8 + 8 * f
                    change = inside[0] * edge_in[z, half, base : base + 8, :]
                    for d in range(1, 4):
                        cells = jnp.where(
                            low_rows,
                            rows_from(below, half, f, zh, 3 * zi + 3 - d),
                            rows_from(above, half, f, zh, 3 * zi + d - 8),
                        )
                        change = change + outside[d - 1] * cells
                    for d in range(1, 3):
                        cells = jnp.where(
                            low_rows,
                            edge_in[z, half, base + d : base + d + 8, :],
                            edge_in[z, half, base - d : base - d + 8, :],
                        )
                        change = change + inside[d] * cells
                    if f < M:
                        Z[half, 8 * f : 8 * f + 8, :] = (
                            edge_tail[z, half, 8 * f : 8 * f + 8, :] + change
                        )
                    else:
                        columns = slice(LANES * half, LANES * half + LANES)
                        step = time_step * change
                        mean_out[z, 0:8, columns] = mean_in[z, 0:8, columns] + jnp.where(
                            low_rows, step, 0.0
                        )
                        mean_out[z, 8:16, columns] = mean_in[z, 8:16, columns] + jnp.where(
                            low_rows, 0.0, step
                        )
            high, low = split(jnp.concatenate([Z[0], Z[1]], axis=1))
            high_out[z] = high
            low_out[z] = low
            add_products(
                acc,
                jnp.concatenate([high_in[z], high], axis=0),
                jnp.concatenate([low_in[z], low], axis=0),
            )
        return carry

    lax.fori_loop(0, 2, group, 0)
    sums = sums_in[...] + field_sums(acc)
    identity = (
        lax.broadcasted_iota(jnp.int32, (32, 32), 0) == lax.broadcasted_iota(jnp.int32, (32, 32), 1)
    ).astype(f32)
    turned = lax.dot_general(
        identity, sums[32:64], (((1,), (1,)), ((), ())), precision=HIGH, preferred_element_type=f32
    )
    whole = sums[0:32] + sums[32:64] + turned
    sums_out[...] = jnp.concatenate([whole[8 * i : 8 * i + 8] for i in range(4)], axis=1)


def edges(below, above, edge_in, edge_tail, high_in, low_in, weights, mean_in, sums_in):
    parts = jax.ShapeDtypeStruct((NZ, 8 * M, 256), bf16)
    return pl.pallas_call(
        edge_kernel,
        out_shape=(
            parts,
            parts,
            jax.ShapeDtypeStruct(mean_in.shape, f32),
            jax.ShapeDtypeStruct((8, LANES), f32),
        ),
        in_specs=[VMEM] * 9,
        out_specs=(VMEM,) * 4,
        scratch_shapes=[
            pltpu.VMEM((2, 8 * M, LANES), f32),
            pltpu.VMEM((512, 256), f32),
        ],
        compiler_params=params(16),
        cost_estimate=cost(10**9, 10**7),
        name="edges",
    )(below, above, edge_in, edge_tail, high_in, low_in, weights, mean_in, sums_in)


def factor_and_map(sums, cell_count):
    whole = jnp.concatenate([sums[:, 32 * i : 32 * i + 32] for i in range(4)], axis=0)
    inner = whole * (1.0 / cell_count)
    row = lax.broadcasted_iota(jnp.int32, (M, 2 * M), 0)
    column = lax.broadcasted_iota(jnp.int32, (M, 2 * M), 1)
    update = jnp.where(
        column < M,
        jnp.where(column == row, 1.0, 0.0) - time_step * inner[M : 2 * M, :],
        jnp.where(column == row + M, time_step, 0.0),
    )
    half_way = jnp.dot(update, inner, precision=HIGH, preferred_element_type=f32)
    gram = lax.dot_general(
        half_way, update, (((1,), (1,)), ((), ())), precision=HIGH, preferred_element_type=f32
    )
    row_g = lax.broadcasted_iota(jnp.int32, (M, M), 0)
    column_g = lax.broadcasted_iota(jnp.int32, (M, M), 1)
    left, right = gram, update
    for j in range(M):
        share = jnp.where(row_g[:, 0:1] > j, left[:, j : j + 1] / left[j : j + 1, j : j + 1], 0.0)
        left = left - share * left[j : j + 1, :]
        right = right - share * right[j : j + 1, :]
    diagonal = jnp.sum(jnp.where(column_g == row_g, left, 0.0), axis=1, keepdims=True)
    scale = 1.0 / jnp.sqrt(diagonal)
    return jnp.where(column_g >= row_g, left * scale, 0.0), right * scale


def spread_map(mapping):
    parts = jnp.concatenate(split(mapping), axis=0)
    tall = (
        lax.broadcasted_iota(jnp.int32, (256, 2 * M), 0) // 8
        == lax.broadcasted_iota(jnp.int32, (256, 2 * M), 1)
    ).astype(bf16)
    wide = (
        lax.broadcasted_iota(jnp.int32, (2 * M, 256), 1) // 8
        == lax.broadcasted_iota(jnp.int32, (2 * M, 256), 0)
    ).astype(bf16)
    rows = jnp.dot(tall, parts, preferred_element_type=f32).astype(bf16)
    full = jnp.dot(rows, wide, preferred_element_type=f32)
    row = lax.broadcasted_iota(jnp.int32, (256, 256), 0)
    column = lax.broadcasted_iota(jnp.int32, (256, 256), 1)
    return jnp.where(row % 8 == column % 8, full, 0.0).astype(bf16)


def make_apply_kernel(cell_count):
    def apply_kernel(sums, *refs):
        parts, (out, factor_out, maps, new, sems) = refs[:8], refs[8:]
        factor, mapping = factor_and_map(sums[...], cell_count)
        factor_out[...] = factor
        maps[...] = spread_map(mapping)
        low_rows = lax.broadcasted_iota(jnp.int32, (M, 8, 256), 1) < 4

        def put(group, slot):
            return pltpu.make_async_copy(
                new.at[slot], out.at[:, pl.ds(GROUP * group, GROUP)], sems.at[slot]
            )

        for group in range(NZ // GROUP):
            slot = group % SLOTS
            if group >= SLOTS:
                put(group - SLOTS, slot).wait()
            for k in range(GROUP):
                z = GROUP * group + k
                results = []
                for i in (0, 4):
                    high = both(parts[i], parts[i + 2], z)
                    low = both(parts[i + 1], parts[i + 3], z)
                    first = jnp.dot(maps[...], high, preferred_element_type=f32)
                    second = jnp.dot(maps[0:128, :], low, preferred_element_type=f32)
                    results.append((first[0:128] + first[128:256] + second).reshape(M, 8, 256))
                inner, edge = results
                new[slot, :, k, 0:8, :] = jnp.where(low_rows, edge, inner)
                new[slot, :, k, 8:16, :] = jnp.where(low_rows, inner, edge)
            put(group, slot).start()
        for group in range(NZ // GROUP - SLOTS, NZ // GROUP):
            put(group, group % SLOTS).wait()

    return apply_kernel


def apply_map(sums, parts, cell_count):
    return pl.pallas_call(
        make_apply_kernel(cell_count),
        out_shape=(
            jax.ShapeDtypeStruct((M, NZ, BX, 256), f32),
            jax.ShapeDtypeStruct((M, M), f32),
        ),
        in_specs=[VMEM] * 9,
        out_specs=(ANY, VMEM),
        scratch_shapes=[
            pltpu.VMEM((256, 256), bf16),
            pltpu.VMEM((SLOTS, M, GROUP, BX, 256), f32),
            pltpu.SemaphoreType.DMA((SLOTS,)),
        ],
        compiler_params=params(16),
        cost_estimate=cost(10**9, 13 * 10**6),
        name="apply",
    )(sums, *parts)


def onward(value, axis):
    size = lax.axis_size(axis)
    return lax.ppermute(value, axis, [(i, i + 1) for i in range(size - 1)])


def backward(value, axis):
    size = lax.axis_size(axis)
    return lax.ppermute(value, axis, [(i + 1, i) for i in range(size - 1)])


def exchanged(value, axes, distance):
    size = lax.axis_size(axes)
    return lax.ppermute(value, axes, [(i, i ^ distance) for i in range(size)])


def shards(
    mean_field, mode_fields, velocity_east, velocity_north, flag_east, flag_north, ocean_mask
):
    axes = ("gx", "gy")
    (
        mean_field, mode_fields, velocity_east, velocity_north, flag_east, flag_north, ocean_mask
    ) = (
        pltpu.with_memory_space_constraint(value, pltpu.HBM)
        for value in (
            mean_field, mode_fields, velocity_east, velocity_north, flag_east, flag_north,
            ocean_mask,
        )
    )
    up, down, east_send, west_send, cells = pack(
        mode_fields, mean_field, velocity_east, velocity_north, flag_east, flag_north, ocean_mask
    )
    west = onward(east_send, "gy")
    east = backward(west_send, "gy")
    below = onward(up, "gx")
    above = backward(down, "gx")
    high_x, low_x, high_xe, low_xe, edge, *planes = prepare(
        cells, velocity_east, velocity_north, flag_east, flag_north, ocean_mask
    )
    high_t, low_t, edge_tail, weights, mean_part, sums_i = interior(
        cells, planes, high_x, low_x, west, east, east_send, west_send
    )
    high_te, low_te, mean_next, sums = edges(
        below, above, edge, edge_tail, high_xe, low_xe, weights, mean_part, sums_i
    )
    sums = sums + exchanged(sums, axes, 1)
    for first in (2, 8, 32):
        near, far, both = (exchanged(sums, axes, first * i) for i in (1, 2, 3))
        sums = (sums + near) + (far + both)
    cell_count = float(NZ * BX * 256 * lax.axis_size("gx") * lax.axis_size("gy"))
    parts = high_x, low_x, high_t, low_t, high_xe, low_xe, high_te, low_te
    modes_next, factor = apply_map(sums, parts, cell_count)
    return (mean_next, modes_next, factor)


def solution(mesh):
    plane = P(None, "gx", "gy")
    return jax.shard_map(
        shards,
        mesh=mesh,
        in_specs=(plane, P(None, None, "gx", "gy"), plane, plane, plane, plane, plane),
        out_specs=(plane, P(None, None, "gx", "gy"), P()),
        check_vma=False,
    )
```

```python
import jax
import jax.numpy as jnp
from jax import lax
from jax.experimental import pallas as pl
from jax.experimental.pallas import tpu as pltpu
from jax.sharding import PartitionSpec as P

time_step = 0.1
horiz_diff = 0.05
vert_diff = 0.2

M = 16
F = 17
NZ = 16
BX = 16
LANES = 128
ROWS = 3 * NZ
SLOTS = 16
GROUP = 1
TAIL = 8 + 8 * F
HIGH = lax.Precision.HIGHEST
f32 = jnp.float32
bf16 = jnp.bfloat16

ANY = pl.BlockSpec(memory_space=pl.ANY)
HBM = pl.BlockSpec(memory_space=pltpu.HBM)
VMEM = pl.BlockSpec(memory_space=pltpu.VMEM)


def params(mib):
    return pltpu.CompilerParams(vmem_limit_bytes=mib * 1024 * 1024)


def cost(flops, nbytes):
    return pl.CostEstimate(flops=flops, bytes_accessed=nbytes, transcendentals=0)


def rolled(value, shift, axis):
    shift = shift % value.shape[axis]
    return value if shift == 0 else pltpu.roll(value, shift, axis)


def lane_ids():
    return lax.broadcasted_iota(jnp.int32, (8, LANES), 1)


def row_ids():
    return lax.broadcasted_iota(jnp.int32, (8, LANES), 0)


def lane_half(ref, half):
    where = (slice(None),) * (len(ref.shape) - 1) + (pl.ds(LANES * half, LANES),)
    return ref.at[where]


def pack_rows(get, first_row):
    rows = row_ids()
    tiles = []
    for out in range(3):
        tile = None
        for z in range(8):
            low, high = max(3 * z, 8 * out), min(3 * z + 3, 8 * out + 8)
            if low >= high:
                continue
            piece = rolled(get(z), 3 * z - 8 * out - first_row, 0)
            tile = piece if tile is None else jnp.where(rows >= low - 8 * out, piece, tile)
        tiles.append(tile)
    return tiles


def pack_columns(get, shift_of):
    slot = lane_ids() // 4
    parts = [jnp.zeros((8, LANES), f32) for _ in range(4)]
    for k in range(2 * NZ):
        moved = rolled(get(k), shift_of(k), 1)
        parts[k % 4] = jnp.where(slot == k, moved, parts[k % 4])
    out = parts[0]
    for k in range(1, 4):
        out = jnp.where(slot % 4 == k, parts[k], out)
    return out


def pack_kernel(
    modes, mean, ve, vn, fe, fn, mask, up, down, east, west, X, V, I, sems
):
    copies = []
    for chunk in range(4):
        for half in range(2):
            copies.append(
                pltpu.make_async_copy(
                    lane_half(modes, half).at[pl.ds(4 * chunk, 4)],
                    X.at[half, pl.ds(4 * chunk, 4), :, pl.ds(8, BX)],
                    sems.at[len(copies)],
                )
            )
    for source, target in (
        (mean, lambda half: X.at[half, M, :, pl.ds(8, BX)]),
        (vn, lambda half: V.at[0, half]),
        (ve, lambda half: V.at[1, half]),
        (fn, lambda half: I.at[0, half]),
        (mask, lambda half: I.at[1, half]),
        (fe, lambda half: I.at[2, half]),
    ):
        for half in range(2):
            copies.append(
                pltpu.make_async_copy(lane_half(source, half), target(half), sems.at[len(copies)])
            )
    for copy in copies:
        copy.start()
    zero_tile = jnp.zeros((8, LANES), f32)

    def clear(f, carry):
        for half in range(2):
            for z in range(NZ):
                X[half, f, z, 0:8, :] = zero_tile
                X[half, f, z, 24:32, :] = zero_tile
        return carry

    lax.fori_loop(0, F, clear, 0, unroll=True)

    def field(f, carry):
        for half in range(2):
            for zh in range(2):
                for target, tile, first in ((up, 1, 5), (down, 0, 0)):
                    tiles = pack_rows(
                        lambda z: X[half, f, 8 * zh + z, 8 + 8 * tile : 16 + 8 * tile, :], first
                    )
                    for t in range(3):
                        target[half, f, zh, 8 * t : 8 * t + 8, :] = tiles[t]
        def tile_of(half):
            return lambda k: X[half, f, k // 2, 8 + 8 * (k % 2) : 16 + 8 * (k % 2), :]
        east[f] = pack_columns(tile_of(1), lambda k: 4 * k - 125)
        west[f] = pack_columns(tile_of(0), lambda k: 4 * k)
        return carry

    for chunk in range(4):
        copies[2 * chunk].wait()
        copies[2 * chunk + 1].wait()
        lax.fori_loop(4 * chunk, 4 * chunk + 4, field, 0, unroll=4)
    for copy in copies[8:]:
        copy.wait()
    lax.fori_loop(M, F, field, 0)
    for index, plane in enumerate(
        (
            lambda half, k: V[0, half, k // 2, 8 * (k % 2) : 8 * (k % 2) + 8, :],
            lambda half, k: I[0, half, k // 2, 8 * (k % 2) : 8 * (k % 2) + 8, :].astype(f32),
            lambda half, k: I[1, half, k // 2, 8 * (k % 2) : 8 * (k % 2) + 8, :].astype(f32),
        )
    ):
        east[F + index] = pack_columns(lambda k: plane(1, k), lambda k: 4 * k - 125)
        west[F + index] = pack_columns(lambda k: plane(0, k), lambda k: 4 * k)
    rows = row_ids()
    for half in range(2):
        for zh in range(2):

            def last_row(z):
                level = 8 * zh + z
                speed = rolled(V[1, half, level, 8:16, :], -2, 0)
                flag = rolled(I[2, half, level, 8:16, :].astype(f32), -1, 0)
                wet = I[1, half, level, 8:16, :].astype(f32)
                return jnp.where(rows == 5, speed, jnp.where(rows == 6, flag, wet))

            for target, get, first in (
                (up, last_row, 5),
                (down, lambda z: I[1, half, 8 * zh + z, 0:8, :].astype(f32), 0),
            ):
                tiles = pack_rows(get, first)
                for t in range(3):
                    target[half, F, zh, 8 * t : 8 * t + 8, :] = tiles[t]


def pack(modes, mean, ve, vn, fe, fn, mask):
    rows = jax.ShapeDtypeStruct((2, F + 1, 2, ROWS // 2, LANES), f32)
    columns = jax.ShapeDtypeStruct((F + 3, 8, LANES), f32)
    return pl.pallas_call(
        pack_kernel,
        out_shape=(
            rows,
            rows,
            columns,
            columns,
            jax.ShapeDtypeStruct((2, F, NZ, 32, LANES), f32),
        ),
        in_specs=[HBM] * 7,
        out_specs=(VMEM,) * 5,
        scratch_shapes=[
            pltpu.VMEM((2, 2, NZ, BX, LANES), f32),
            pltpu.VMEM((3, 2, NZ, BX, LANES), jnp.int32),
            pltpu.SemaphoreType.DMA((20,)),
        ],
        compiler_params=params(24),
        cost_estimate=cost(10**7, 7 * 10**6),
        name="pack",
    )(modes, mean, ve, vn, fe, fn, mask)


def along_lanes(first, second, outer, offset):
    lanes = lane_ids()
    a, b, c = (rolled(v, -offset, 1) for v in (first, second, outer))
    if offset > 0:
        inside = lanes < LANES - offset
        return jnp.where(inside, a, b), jnp.where(inside, b, c)
    outside = lanes < -offset
    return jnp.where(outside, c, a), jnp.where(outside, a, b)


def around_lanes(first, second, offset):
    lanes = lane_ids()
    a, b = (rolled(v, -offset, 1) for v in (first, second))
    kept = lanes < LANES - offset if offset > 0 else lanes >= -offset
    return jnp.where(kept, a, b), jnp.where(kept, b, a)


def cell_weights(a_low, b_low, d_low, a_high, b_high, d_high):
    return (
        2.0 * a_low,
        -13.0 * a_low - 3.0 * b_low - 2.0 * a_high,
        47.0 * a_low + 27.0 * b_low + d_low + 13.0 * a_high + 3.0 * b_high,
        27.0 * a_low + 47.0 * b_low - d_low - 47.0 * a_high - 27.0 * b_high - d_high,
        -3.0 * a_low - 13.0 * b_low - 27.0 * a_high - 47.0 * b_high + d_high,
        2.0 * b_low + 3.0 * a_high + 13.0 * b_high,
        -2.0 * b_high,
    )


def face_parts(openness, speed, flag):
    scaled = openness * speed * (1.0 / 60.0)
    return scaled * flag, scaled * (1.0 - flag), horiz_diff * openness


def split(value):
    high = value.astype(bf16)
    return high, (value - high.astype(f32)).astype(bf16)


def add_products(acc, high, low):
    dims = (((1,), (1,)), ((), ()))
    acc[0:256, :] += lax.dot_general(high, high, dims, preferred_element_type=f32)
    acc[256:512, :] += lax.dot_general(low, high, dims, preferred_element_type=f32)


def joined(upper, lower):
    return jnp.concatenate([both(upper, lower, z) for z in range(NZ)], axis=1)


def both(upper, lower, z):
    return jnp.concatenate([upper[z], lower[z]], axis=0)


def field_sums(acc):
    rows = lax.broadcasted_iota(jnp.int32, (512, 256), 0)
    columns = lax.broadcasted_iota(jnp.int32, (512, 256), 1)
    kept = jnp.where(rows % 8 == columns % 8, acc[...], 0.0)
    by_row = jnp.sum(kept.reshape(64, 8, 256), axis=1)
    gather = (
        lax.broadcasted_iota(jnp.int32, (256, 32), 0) // 8
        == lax.broadcasted_iota(jnp.int32, (256, 32), 1)
    ).astype(f32)
    return jnp.dot(by_row, gather, precision=HIGH, preferred_element_type=f32)


def prepare_kernel(
    X, ve, vn, fe, fn, mask,
    high_in, low_in, high_edge, low_edge, edge_out, VE, FE, W, VN, FN, ints, Z, sems,
):
    zero_tile = jnp.zeros((8, LANES), f32)
    copies = []
    for half in range(2):
        for source, target in (
            (ve, VE.at[half, :, pl.ds(8, BX)]),
            (vn, VN.at[half]),
            (mask, ints.at[0, half]),
            (fn, ints.at[1, half]),
            (fe, ints.at[2, half]),
        ):
            copies.append(
                pltpu.make_async_copy(lane_half(source, half), target, sems.at[len(copies)])
            )
    for copy in copies:
        copy.start()
    low_rows = row_ids() < 4
    for half in range(2):
        for z in range(NZ):
            edge_out[z, half, 0:8, :] = zero_tile
            edge_out[z, half, TAIL : TAIL + 8, :] = zero_tile

    def level(z, carry):
        for half in range(2):
            columns = slice(LANES * half, LANES * half + LANES)
            for f in range(F):
                first, second = X[half, f, z, 8:16, :], X[half, f, z, 16:24, :]
                edge = jnp.where(low_rows, first, second)
                edge_out[z, half, 8 + 8 * f : 16 + 8 * f, :] = edge
                if f < M:
                    Z[0, 8 * f : 8 * f + 8, columns] = jnp.where(low_rows, second, first)
                    Z[1, 8 * f : 8 * f + 8, columns] = edge
        high_in[z], low_in[z] = split(Z[0])
        high_edge[z], low_edge[z] = split(Z[1])
        return carry

    lax.fori_loop(0, NZ, level, 0, unroll=2)
    for copy in copies:
        copy.wait()
    for half in range(2):
        for z in range(NZ):
            VE[half, z, 0:8, :] = zero_tile
            FE[half, z, 0:8, :] = zero_tile
            W[half, z, 0:8, :] = zero_tile
            W[half, z, 24:32, :] = zero_tile
            for xt in range(2):
                rows = slice(8 * xt, 8 * xt + 8)
                padded = slice(8 * xt + 8, 8 * xt + 16)
                W[half, z, padded, :] = ints[0, half, z, rows, :].astype(f32)
                FN[half, z, rows, :] = ints[1, half, z, rows, :].astype(f32)
                FE[half, z, padded, :] = ints[2, half, z, rows, :].astype(f32)


def prepare(cells, ve, vn, fe, fn, mask):
    parts = jax.ShapeDtypeStruct((NZ, 8 * M, 256), bf16)
    padded = jax.ShapeDtypeStruct((2, NZ, 32, LANES), f32)
    plain = jax.ShapeDtypeStruct((2, NZ, BX, LANES), f32)
    return pl.pallas_call(
        prepare_kernel,
        out_shape=(
            parts,
            parts,
            parts,
            parts,
            jax.ShapeDtypeStruct((NZ, 2, TAIL + 8, LANES), f32),
            padded,
            padded,
            padded,
            plain,
            plain,
        ),
        in_specs=[VMEM] + [HBM] * 5,
        out_specs=(VMEM,) * 10,
        scratch_shapes=[
            pltpu.VMEM((3, 2, NZ, BX, LANES), jnp.int32),
            pltpu.VMEM((2, 8 * M, 256), f32),
            pltpu.SemaphoreType.DMA((10,)),
        ],
        compiler_params=params(16),
        cost_estimate=cost(10**6, 10**6),
        name="prepare",
    )(cells, ve, vn, fe, fn, mask)


def interior_kernel(
    X, VE, FE, W, VN, FN, high_in, low_in, west, east, own_last, own_first,
    high_out, low_out, edge_out, weights_out, mean_out, sums_out,
    H, C, G, T, Z, acc,
):
    acc[...] = jnp.zeros((512, 256), f32)
    lanes = lane_ids()
    rows = row_ids()

    for f in range(F, F + 3):
        after, before = east[f], west[f]
        for k in range(2 * NZ):
            H[f - F, k] = jnp.where(
                lanes < 64, rolled(after, -4 * k, 1), rolled(before, LANES - 3 - 4 * k, 1)
            )

    place = lanes % 4

    (v_in, f_in, w_in) = (west[F + i] for i in range(3))
    (v_own, f_own, w_own) = (own_first[F + i] for i in range(3))
    lower_of = lambda outer_plane, own: jnp.where(
        place == 0, rolled(outer_plane, -2, 1), rolled(own, 1, 1)
    )
    low_face = face_parts(
        lower_of(w_in, w_own) * w_own, lower_of(v_in, v_own), lower_of(f_in, f_own)
    )
    high_face = face_parts(w_own * rolled(w_own, -1, 1), v_own, f_own)
    first_gains = cell_weights(*low_face, *high_face)
    for d in range(1, 4):
        G[d - 1] = jnp.where(place < d, first_gains[3 - d], 0.0)
    w_next = east[F + 2]
    (v_own, f_own, w_own) = (own_last[F + i] for i in range(3))
    high_face = face_parts(
        w_own * jnp.where(place == 2, rolled(w_next, 2, 1), rolled(w_own, -1, 1)), v_own, f_own
    )
    low_face = tuple(rolled(part, 1, 1) for part in high_face)
    last_gains = cell_weights(*low_face, *high_face)
    for d in range(1, 4):
        G[2 + d] = jnp.where((place >= 3 - d) & (place < 3), last_gains[3 + d], 0.0)

    def beside(f):
        before, after = west[f], east[f]
        first = (
            G[0] * rolled(before, -2, 1) + G[1] * rolled(before, -1, 1) + G[2] * before
        )
        last = G[3] * rolled(after, 2, 1) + G[4] * rolled(after, 1, 1) + G[5] * after
        C[0, f] = first
        C[1, f] = rolled(last, LANES - 3, 1)

    for f in range(F):
        beside(f)

    def level(z, carry):
        z_up = jnp.minimum(z + 1, NZ - 1)
        z_down = jnp.maximum(z - 1, 0)
        for xt in range(2):
            start = 8 + 8 * xt

            def outer(index):
                return H[index - F, 2 * z + xt]

            def at(ref, half, offset):
                return ref[half, z, start + offset : start + offset + 8, :]

            wet = [at(W, half, 0) for half in range(2)]
            wx = []
            for half in range(2):
                before = wet[half] * at(W, half, -1)
                after = wet[half] * at(W, half, 1)
                wx.append(
                    cell_weights(
                        *face_parts(before, at(VE, half, -1), at(FE, half, -1)),
                        *face_parts(after, at(VE, half, 0), at(FE, half, 0)),
                    )
                )
            wet_out = outer(F + 2)
            following = along_lanes(wet[0], wet[1], wet_out, 1)
            own = [
                face_parts(
                    wet[half] * following[half],
                    VN[half, z, 8 * xt : 8 * xt + 8, :],
                    FN[half, z, 8 * xt : 8 * xt + 8, :],
                )
                for half in range(2)
            ]
            beyond = face_parts(wet_out * rolled(wet[0], -1, 1), outer(F), outer(F + 1))
            before = [along_lanes(own[0][i], own[1][i], beyond[i], -1) for i in range(3)]
            wy = [
                cell_weights(*(before[i][half] for i in range(3)), *own[half]) for half in range(2)
            ]
            wy = [
                [
                    jnp.where(
                        (lanes < 3 - j) if half == 0 else (lanes >= LANES + 3 - j), 0.0, wy[half][j]
                    )
                    if (half == 0) == (j < 3) and j != 3
                    else wy[half][j]
                    for j in range(7)
                ]
                for half in range(2)
            ]
            centre = [
                wx[half][3] + wy[half][3] - 2.0 * vert_diff * wet[half] for half in range(2)
            ]
            w_level = [vert_diff * wet[half] for half in range(2)]
            for half in range(2):
                for index, plane in enumerate((at(VE, half, 0), at(FE, half, 0), wet[half])):
                    if xt == 0:
                        weights_out[half, z, 3 + index] = plane
                    else:
                        weights_out[half, z, 3 + index] = jnp.where(
                            rows < 4, weights_out[half, z, 3 + index], plane
                        )
                for d in range(1, 4):
                    if xt == 0:
                        weights_out[half, z, d - 1] = jnp.where(rows < d, wx[half][3 - d], 0.0)
                    else:
                        weights_out[half, z, d - 1] += jnp.where(
                            rows >= 8 - d, wx[half][3 + d], 0.0
                        )
            for f in range(F):
                own_cells = [X[half, f, z, start : start + 8, :] for half in range(2)]
                total = [
                    centre[half] * own_cells[half]
                    + w_level[half]
                    * (
                        X[half, f, z_up, start : start + 8, :]
                        + X[half, f, z_down, start : start + 8, :]
                    )
                    for half in range(2)
                ]
                first, last = C[0, f], C[1, f]
                total[0] += jnp.where(lanes < 3, first, 0.0)
                total[1] += jnp.where(lanes >= LANES - 3, last, 0.0)
                C[0, f] = rolled(first, -4, 1)
                C[1, f] = rolled(last, -4, 1)
                for offset in (-3, -2, -1, 1, 2, 3):
                    moved = around_lanes(own_cells[0], own_cells[1], offset)
                    for half in range(2):
                        total[half] += wx[half][3 + offset] * X[
                            half, f, z, start + offset : start + offset + 8, :
                        ]
                        total[half] += wy[half][3 + offset] * moved[half]
                for half in range(2):
                    columns = slice(LANES * half, LANES * half + LANES)
                    low_rows = rows < 4
                    if f == M:
                        mean_out[z, 8 * xt : 8 * xt + 8, columns] = (
                            own_cells[half] + time_step * total[half]
                        )
                    elif xt == 0:
                        T[half, f] = total[half]
                    else:
                        near = T[half, f]
                        place = slice(8 * f, 8 * f + 8)
                        Z[place, columns] = jnp.where(low_rows, total[half], near)
                        edge_out[z, half, place, :] = jnp.where(low_rows, near, total[half])
        high, low = split(Z[...])
        high_out[z] = high
        low_out[z] = low
        return carry

    lax.fori_loop(0, NZ, level, 0, unroll=2)
    add_products(acc, joined(high_in, high_out), joined(low_in, low_out))
    sums_out[...] = field_sums(acc)


def interior(cells, planes, high_in, low_in, west, east, own_last, own_first):
    parts = jax.ShapeDtypeStruct((NZ, 8 * M, 256), bf16)
    return pl.pallas_call(
        interior_kernel,
        out_shape=(
            parts,
            parts,
            jax.ShapeDtypeStruct((NZ, 2, 8 * M, LANES), f32),
            jax.ShapeDtypeStruct((2, NZ, 6, 8, LANES), f32),
            jax.ShapeDtypeStruct((NZ, BX, 2 * LANES), f32),
            jax.ShapeDtypeStruct((64, 32), f32),
        ),
        in_specs=[VMEM] * 12,
        out_specs=(VMEM,) * 6,
        scratch_shapes=[
            pltpu.VMEM((3, 2 * NZ, 8, LANES), f32),
            pltpu.VMEM((2, F, 8, LANES), f32),
            pltpu.VMEM((6, 8, LANES), f32),
            pltpu.VMEM((2, M, 8, LANES), f32),
            pltpu.VMEM((8 * M, 256), f32),
            pltpu.VMEM((512, 256), f32),
        ],
        compiler_params=params(20),
        cost_estimate=cost(10**6, 10**6),
        name="interior",
    )(cells, *planes, high_in, low_in, west, east, own_last, own_first)


def edge_kernel(
    below, above, edge_in, edge_tail, high_in, low_in, weights, mean_in, sums_in,
    high_out, low_out, mean_out, sums_out, Z, acc,
):
    acc[...] = jnp.zeros((512, 256), f32)
    rows = row_ids()
    low_rows = rows < 4
    first_row = rows == 0
    last_row = rows == 7

    def rows_from(ref, half, f, zh, first):
        start = min(max(first, 0), 16)
        return rolled(ref[half, f, zh, start : start + 8, :], start - first, 0)

    def gains_of(half, z, zh, zi):
        speed, flag, wet = (weights[half, z, 3 + i] for i in range(3))
        speed = jnp.where(first_row, rows_from(below, half, F, zh, 3 * zi), speed)
        flag = jnp.where(first_row, rows_from(below, half, F, zh, 3 * zi + 1), flag)
        beyond = jnp.where(first_row, rows_from(below, half, F, zh, 3 * zi + 2), 0.0)
        beyond = jnp.where(last_row, rows_from(above, half, F, zh, 3 * zi - 7), beyond)
        a, b, d = face_parts(beyond * wet, speed, flag)
        near, far = 47.0 * a + 27.0 * b + d, 27.0 * a + 47.0 * b - d
        left, right = -13.0 * a - 3.0 * b, -3.0 * a - 13.0 * b
        outside = (
            weights[half, z, 0] + jnp.where(first_row, near, -far),
            weights[half, z, 1] + jnp.where(first_row, left, -right),
            weights[half, z, 2] + jnp.where(first_row, 2.0 * a, -2.0 * b),
        )
        inside = (
            jnp.where(first_row, far, -near),
            jnp.where(first_row, right, -left),
            jnp.where(first_row, 2.0 * b, -2.0 * a),
        )
        return outside, inside

    def group(zh, carry):
        for zi in range(8):
            z = 8 * zh + zi
            for half in range(2):
                outside, inside = gains_of(half, z, zh, zi)
                for f in range(F):
                    base = 8 + 8 * f
                    change = inside[0] * edge_in[z, half, base : base + 8, :]
                    for d in range(1, 4):
                        cells = jnp.where(
                            low_rows,
                            rows_from(below, half, f, zh, 3 * zi + 3 - d),
                            rows_from(above, half, f, zh, 3 * zi + d - 8),
                        )
                        change = change + outside[d - 1] * cells
                    for d in range(1, 3):
                        cells = jnp.where(
                            low_rows,
                            edge_in[z, half, base + d : base + d + 8, :],
                            edge_in[z, half, base - d : base - d + 8, :],
                        )
                        change = change + inside[d] * cells
                    if f < M:
                        Z[half, 8 * f : 8 * f + 8, :] = (
                            edge_tail[z, half, 8 * f : 8 * f + 8, :] + change
                        )
                    else:
                        columns = slice(LANES * half, LANES * half + LANES)
                        step = time_step * change
                        mean_out[z, 0:8, columns] = mean_in[z, 0:8, columns] + jnp.where(
                            low_rows, step, 0.0
                        )
                        mean_out[z, 8:16, columns] = mean_in[z, 8:16, columns] + jnp.where(
                            low_rows, 0.0, step
                        )
            high, low = split(jnp.concatenate([Z[0], Z[1]], axis=1))
            high_out[z] = high
            low_out[z] = low
            add_products(
                acc,
                jnp.concatenate([high_in[z], high], axis=0),
                jnp.concatenate([low_in[z], low], axis=0),
            )
        return carry

    lax.fori_loop(0, 2, group, 0, unroll=True)
    sums = sums_in[...] + field_sums(acc)
    identity = (
        lax.broadcasted_iota(jnp.int32, (32, 32), 0) == lax.broadcasted_iota(jnp.int32, (32, 32), 1)
    ).astype(f32)
    turned = lax.dot_general(
        identity, sums[32:64], (((1,), (1,)), ((), ())), precision=HIGH, preferred_element_type=f32
    )
    whole = sums[0:32] + sums[32:64] + turned
    sums_out[...] = jnp.concatenate([whole[8 * i : 8 * i + 8] for i in range(4)], axis=1)


def edges(below, above, edge_in, edge_tail, high_in, low_in, weights, mean_in, sums_in):
    parts = jax.ShapeDtypeStruct((NZ, 8 * M, 256), bf16)
    return pl.pallas_call(
        edge_kernel,
        out_shape=(
            parts,
            parts,
            jax.ShapeDtypeStruct(mean_in.shape, f32),
            jax.ShapeDtypeStruct((8, LANES), f32),
        ),
        in_specs=[VMEM] * 9,
        out_specs=(VMEM,) * 4,
        scratch_shapes=[
            pltpu.VMEM((2, 8 * M, LANES), f32),
            pltpu.VMEM((512, 256), f32),
        ],
        compiler_params=params(16),
        cost_estimate=cost(10**9, 10**7),
        name="edges",
    )(below, above, edge_in, edge_tail, high_in, low_in, weights, mean_in, sums_in)


def factor_and_map(sums, cell_count):
    whole = jnp.concatenate([sums[:, 32 * i : 32 * i + 32] for i in range(4)], axis=0)
    inner = whole * (1.0 / cell_count)
    row = lax.broadcasted_iota(jnp.int32, (M, 2 * M), 0)
    column = lax.broadcasted_iota(jnp.int32, (M, 2 * M), 1)
    update = jnp.where(
        column < M,
        jnp.where(column == row, 1.0, 0.0) - time_step * inner[M : 2 * M, :],
        jnp.where(column == row + M, time_step, 0.0),
    )
    half_way = jnp.dot(update, inner, precision=HIGH, preferred_element_type=f32)
    gram = lax.dot_general(
        half_way, update, (((1,), (1,)), ((), ())), precision=HIGH, preferred_element_type=f32
    )
    row_g = lax.broadcasted_iota(jnp.int32, (M, M), 0)
    column_g = lax.broadcasted_iota(jnp.int32, (M, M), 1)
    left, right = gram, update
    for j in range(M):
        share = jnp.where(row_g[:, 0:1] > j, left[:, j : j + 1] / left[j : j + 1, j : j + 1], 0.0)
        left = left - share * left[j : j + 1, :]
        right = right - share * right[j : j + 1, :]
    diagonal = jnp.sum(jnp.where(column_g == row_g, left, 0.0), axis=1, keepdims=True)
    scale = 1.0 / jnp.sqrt(diagonal)
    return jnp.where(column_g >= row_g, left * scale, 0.0), right * scale


def spread_map(mapping):
    parts = jnp.concatenate(split(mapping), axis=0)
    tall = (
        lax.broadcasted_iota(jnp.int32, (256, 2 * M), 0) // 8
        == lax.broadcasted_iota(jnp.int32, (256, 2 * M), 1)
    ).astype(bf16)
    wide = (
        lax.broadcasted_iota(jnp.int32, (2 * M, 256), 1) // 8
        == lax.broadcasted_iota(jnp.int32, (2 * M, 256), 0)
    ).astype(bf16)
    rows = jnp.dot(tall, parts, preferred_element_type=f32).astype(bf16)
    full = jnp.dot(rows, wide, preferred_element_type=f32)
    row = lax.broadcasted_iota(jnp.int32, (256, 256), 0)
    column = lax.broadcasted_iota(jnp.int32, (256, 256), 1)
    return jnp.where(row % 8 == column % 8, full, 0.0).astype(bf16)


def make_apply_kernel(cell_count):
    def apply_kernel(sums, *refs):
        parts, (out, factor_out, maps, new, sems) = refs[:8], refs[8:]
        factor, mapping = factor_and_map(sums[...], cell_count)
        factor_out[...] = factor
        maps[...] = spread_map(mapping)
        low_rows = lax.broadcasted_iota(jnp.int32, (M, 8, 256), 1) < 4

        def put(group, slot):
            return pltpu.make_async_copy(
                new.at[slot], out.at[:, pl.ds(GROUP * group, GROUP)], sems.at[slot]
            )

        for group in range(NZ // GROUP):
            slot = group % SLOTS
            if group >= SLOTS:
                put(group - SLOTS, slot).wait()
            for k in range(GROUP):
                z = GROUP * group + k
                results = []
                for i in (0, 4):
                    high = both(parts[i], parts[i + 2], z)
                    low = both(parts[i + 1], parts[i + 3], z)
                    first = jnp.dot(maps[...], high, preferred_element_type=f32)
                    second = jnp.dot(maps[0:128, :], low, preferred_element_type=f32)
                    results.append((first[0:128] + first[128:256] + second).reshape(M, 8, 256))
                inner, edge = results
                new[slot, :, k, 0:8, :] = jnp.where(low_rows, edge, inner)
                new[slot, :, k, 8:16, :] = jnp.where(low_rows, inner, edge)
            put(group, slot).start()
        for group in range(NZ // GROUP - SLOTS, NZ // GROUP):
            put(group, group % SLOTS).wait()

    return apply_kernel


def apply_map(sums, parts, cell_count):
    return pl.pallas_call(
        make_apply_kernel(cell_count),
        out_shape=(
            jax.ShapeDtypeStruct((M, NZ, BX, 256), f32),
            jax.ShapeDtypeStruct((M, M), f32),
        ),
        in_specs=[VMEM] * 9,
        out_specs=(ANY, VMEM),
        scratch_shapes=[
            pltpu.VMEM((256, 256), bf16),
            pltpu.VMEM((SLOTS, M, GROUP, BX, 256), f32),
            pltpu.SemaphoreType.DMA((SLOTS,)),
        ],
        compiler_params=params(16),
        cost_estimate=cost(10**9, 13 * 10**6),
        name="apply",
    )(sums, *parts)


def onward(value, axis):
    size = lax.axis_size(axis)
    return lax.ppermute(value, axis, [(i, i + 1) for i in range(size - 1)])


def backward(value, axis):
    size = lax.axis_size(axis)
    return lax.ppermute(value, axis, [(i + 1, i) for i in range(size - 1)])


def exchanged(value, axes, distance):
    size = lax.axis_size(axes)
    return lax.ppermute(value, axes, [(i, i ^ distance) for i in range(size)])


def shards(
    mean_field, mode_fields, velocity_east, velocity_north, flag_east, flag_north, ocean_mask
):
    axes = ("gx", "gy")
    (
        mean_field, mode_fields, velocity_east, velocity_north, flag_east, flag_north, ocean_mask
    ) = (
        pltpu.with_memory_space_constraint(value, pltpu.HBM)
        for value in (
            mean_field, mode_fields, velocity_east, velocity_north, flag_east, flag_north,
            ocean_mask,
        )
    )
    up, down, east_send, west_send, cells = pack(
        mode_fields, mean_field, velocity_east, velocity_north, flag_east, flag_north, ocean_mask
    )
    west = onward(east_send, "gy")
    east = backward(west_send, "gy")
    below = onward(up, "gx")
    above = backward(down, "gx")
    high_x, low_x, high_xe, low_xe, edge, *planes = prepare(
        cells, velocity_east, velocity_north, flag_east, flag_north, ocean_mask
    )
    high_t, low_t, edge_tail, weights, mean_part, sums_i = interior(
        cells, planes, high_x, low_x, west, east, east_send, west_send
    )
    high_te, low_te, mean_next, sums = edges(
        below, above, edge, edge_tail, high_xe, low_xe, weights, mean_part, sums_i
    )
    sums = sums + exchanged(sums, axes, 1)
    for first in (2, 8, 32):
        near, far, both = (exchanged(sums, axes, first * i) for i in (1, 2, 3))
        sums = (sums + near) + (far + both)
    cell_count = float(NZ * BX * 256 * lax.axis_size("gx") * lax.axis_size("gy"))
    parts = high_x, low_x, high_t, low_t, high_xe, low_xe, high_te, low_te
    modes_next, factor = apply_map(sums, parts, cell_count)
    return (mean_next, modes_next, factor)


def solution(mesh):
    plane = P(None, "gx", "gy")
    return jax.shard_map(
        shards,
        mesh=mesh,
        in_specs=(plane, P(None, None, "gx", "gy"), plane, plane, plane, plane, plane),
        out_specs=(plane, P(None, None, "gx", "gy"), P()),
        check_vma=False,
    )
```

```python
import jax
import jax.numpy as jnp
from jax import lax
from jax.experimental import pallas as pl
from jax.experimental.pallas import tpu as pltpu
from jax.sharding import PartitionSpec as P

time_step = 0.1
horiz_diff = 0.05
vert_diff = 0.2

M = 16
F = 17
NZ = 16
BX = 16
LANES = 128
ROWS = 3 * NZ
SLOTS = 16
GROUP = 1
TAIL = 8 + 8 * F
HIGH = lax.Precision.HIGHEST
f32 = jnp.float32
bf16 = jnp.bfloat16

ANY = pl.BlockSpec(memory_space=pl.ANY)
HBM = pl.BlockSpec(memory_space=pltpu.HBM)
VMEM = pl.BlockSpec(memory_space=pltpu.VMEM)


def params(mib):
    return pltpu.CompilerParams(vmem_limit_bytes=mib * 1024 * 1024)


def cost(flops, nbytes):
    return pl.CostEstimate(flops=flops, bytes_accessed=nbytes, transcendentals=0)


def rolled(value, shift, axis):
    shift = shift % value.shape[axis]
    return value if shift == 0 else pltpu.roll(value, shift, axis)


def lane_ids():
    return lax.broadcasted_iota(jnp.int32, (8, LANES), 1)


def row_ids():
    return lax.broadcasted_iota(jnp.int32, (8, LANES), 0)


def lane_half(ref, half):
    where = (slice(None),) * (len(ref.shape) - 1) + (pl.ds(LANES * half, LANES),)
    return ref.at[where]


def pack_rows(get, first_row):
    rows = row_ids()
    tiles = []
    for out in range(3):
        tile = None
        for z in range(8):
            low, high = max(3 * z, 8 * out), min(3 * z + 3, 8 * out + 8)
            if low >= high:
                continue
            piece = rolled(get(z), 3 * z - 8 * out - first_row, 0)
            tile = piece if tile is None else jnp.where(rows >= low - 8 * out, piece, tile)
        tiles.append(tile)
    return tiles


def pack_columns(get, shift_of):
    slot = lane_ids() // 4
    parts = [jnp.zeros((8, LANES), f32) for _ in range(4)]
    for k in range(2 * NZ):
        moved = rolled(get(k), shift_of(k), 1)
        parts[k % 4] = jnp.where(slot == k, moved, parts[k % 4])
    out = parts[0]
    for k in range(1, 4):
        out = jnp.where(slot % 4 == k, parts[k], out)
    return out


def pack_kernel(
    modes, mean, ve, vn, fe, fn, mask, up, down, east, west, X, V, I, sems
):
    copies = []
    for chunk in range(4):
        for half in range(2):
            copies.append(
                pltpu.make_async_copy(
                    lane_half(modes, half).at[pl.ds(4 * chunk, 4)],
                    X.at[half, pl.ds(4 * chunk, 4), :, pl.ds(8, BX)],
                    sems.at[len(copies)],
                )
            )
    for source, target in (
        (mean, lambda half: X.at[half, M, :, pl.ds(8, BX)]),
        (vn, lambda half: V.at[0, half]),
        (ve, lambda half: V.at[1, half]),
        (fn, lambda half: I.at[0, half]),
        (mask, lambda half: I.at[1, half]),
        (fe, lambda half: I.at[2, half]),
    ):
        for half in range(2):
            copies.append(
                pltpu.make_async_copy(lane_half(source, half), target(half), sems.at[len(copies)])
            )
    for copy in copies:
        copy.start()
    zero_tile = jnp.zeros((8, LANES), f32)

    def clear(f, carry):
        for half in range(2):
            for z in range(NZ):
                X[half, f, z, 0:8, :] = zero_tile
                X[half, f, z, 24:32, :] = zero_tile
        return carry

    lax.fori_loop(0, F, clear, 0, unroll=True)

    def field(f, carry):
        for half in range(2):
            for zh in range(2):
                for target, tile, first in ((up, 1, 5), (down, 0, 0)):
                    tiles = pack_rows(
                        lambda z: X[half, f, 8 * zh + z, 8 + 8 * tile : 16 + 8 * tile, :], first
                    )
                    for t in range(3):
                        target[half, f, zh, 8 * t : 8 * t + 8, :] = tiles[t]
        def tile_of(half):
            return lambda k: X[half, f, k // 2, 8 + 8 * (k % 2) : 16 + 8 * (k % 2), :]
        east[f] = pack_columns(tile_of(1), lambda k: 4 * k - 125)
        west[f] = pack_columns(tile_of(0), lambda k: 4 * k)
        return carry

    for chunk in range(4):
        copies[2 * chunk].wait()
        copies[2 * chunk + 1].wait()
        lax.fori_loop(4 * chunk, 4 * chunk + 4, field, 0, unroll=4)
    for copy in copies[8:]:
        copy.wait()
    lax.fori_loop(M, F, field, 0)
    for index, plane in enumerate(
        (
            lambda half, k: V[0, half, k // 2, 8 * (k % 2) : 8 * (k % 2) + 8, :],
            lambda half, k: I[0, half, k // 2, 8 * (k % 2) : 8 * (k % 2) + 8, :].astype(f32),
            lambda half, k: I[1, half, k // 2, 8 * (k % 2) : 8 * (k % 2) + 8, :].astype(f32),
        )
    ):
        east[F + index] = pack_columns(lambda k: plane(1, k), lambda k: 4 * k - 125)
        west[F + index] = pack_columns(lambda k: plane(0, k), lambda k: 4 * k)
    rows = row_ids()
    for half in range(2):
        for zh in range(2):

            def last_row(z):
                level = 8 * zh + z
                speed = rolled(V[1, half, level, 8:16, :], -2, 0)
                flag = rolled(I[2, half, level, 8:16, :].astype(f32), -1, 0)
                wet = I[1, half, level, 8:16, :].astype(f32)
                return jnp.where(rows == 5, speed, jnp.where(rows == 6, flag, wet))

            for target, get, first in (
                (up, last_row, 5),
                (down, lambda z: I[1, half, 8 * zh + z, 0:8, :].astype(f32), 0),
            ):
                tiles = pack_rows(get, first)
                for t in range(3):
                    target[half, F, zh, 8 * t : 8 * t + 8, :] = tiles[t]


def pack(modes, mean, ve, vn, fe, fn, mask):
    rows = jax.ShapeDtypeStruct((2, F + 1, 2, ROWS // 2, LANES), f32)
    columns = jax.ShapeDtypeStruct((F + 3, 8, LANES), f32)
    return pl.pallas_call(
        pack_kernel,
        out_shape=(
            rows,
            rows,
            columns,
            columns,
            jax.ShapeDtypeStruct((2, F, NZ, 32, LANES), f32),
        ),
        in_specs=[HBM] * 7,
        out_specs=(VMEM,) * 5,
        scratch_shapes=[
            pltpu.VMEM((2, 2, NZ, BX, LANES), f32),
            pltpu.VMEM((3, 2, NZ, BX, LANES), jnp.int32),
            pltpu.SemaphoreType.DMA((20,)),
        ],
        compiler_params=params(24),
        cost_estimate=cost(10**7, 7 * 10**6),
        name="pack",
    )(modes, mean, ve, vn, fe, fn, mask)


def along_lanes(first, second, outer, offset):
    lanes = lane_ids()
    a, b, c = (rolled(v, -offset, 1) for v in (first, second, outer))
    if offset > 0:
        inside = lanes < LANES - offset
        return jnp.where(inside, a, b), jnp.where(inside, b, c)
    outside = lanes < -offset
    return jnp.where(outside, c, a), jnp.where(outside, a, b)


def around_lanes(first, second, offset):
    lanes = lane_ids()
    a, b = (rolled(v, -offset, 1) for v in (first, second))
    kept = lanes < LANES - offset if offset > 0 else lanes >= -offset
    return jnp.where(kept, a, b), jnp.where(kept, b, a)


def cell_weights(a_low, b_low, d_low, a_high, b_high, d_high):
    return (
        2.0 * a_low,
        -13.0 * a_low - 3.0 * b_low - 2.0 * a_high,
        47.0 * a_low + 27.0 * b_low + d_low + 13.0 * a_high + 3.0 * b_high,
        27.0 * a_low + 47.0 * b_low - d_low - 47.0 * a_high - 27.0 * b_high - d_high,
        -3.0 * a_low - 13.0 * b_low - 27.0 * a_high - 47.0 * b_high + d_high,
        2.0 * b_low + 3.0 * a_high + 13.0 * b_high,
        -2.0 * b_high,
    )


def face_parts(openness, speed, flag):
    scaled = openness * speed * (1.0 / 60.0)
    return scaled * flag, scaled * (1.0 - flag), horiz_diff * openness


def split(value):
    high = value.astype(bf16)
    return high, (value - high.astype(f32)).astype(bf16)


def add_products(acc, high, low):
    dims = (((1,), (1,)), ((), ()))
    acc[0:256, :] += lax.dot_general(high, high, dims, preferred_element_type=f32)
    acc[256:512, :] += lax.dot_general(low, high, dims, preferred_element_type=f32)


def joined(upper, lower):
    return jnp.concatenate([both(upper, lower, z) for z in range(NZ)], axis=1)


def both(upper, lower, z):
    return jnp.concatenate([upper[z], lower[z]], axis=0)


def field_sums(acc):
    rows = lax.broadcasted_iota(jnp.int32, (512, 256), 0)
    columns = lax.broadcasted_iota(jnp.int32, (512, 256), 1)
    kept = jnp.where(rows % 8 == columns % 8, acc[...], 0.0)
    by_row = jnp.sum(kept.reshape(64, 8, 256), axis=1)
    gather = (
        lax.broadcasted_iota(jnp.int32, (256, 32), 0) // 8
        == lax.broadcasted_iota(jnp.int32, (256, 32), 1)
    ).astype(f32)
    return jnp.dot(by_row, gather, precision=HIGH, preferred_element_type=f32)


def prepare_kernel(
    X, ve, vn, fe, fn, mask,
    high_in, low_in, high_edge, low_edge, edge_out, VE, FE, W, VN, FN, ints, Z, sems,
):
    zero_tile = jnp.zeros((8, LANES), f32)
    copies = []
    for half in range(2):
        for source, target in (
            (ve, VE.at[half, :, pl.ds(8, BX)]),
            (vn, VN.at[half]),
            (mask, ints.at[0, half]),
            (fn, ints.at[1, half]),
            (fe, ints.at[2, half]),
        ):
            copies.append(
                pltpu.make_async_copy(lane_half(source, half), target, sems.at[len(copies)])
            )
    for copy in copies:
        copy.start()
    low_rows = row_ids() < 4
    for half in range(2):
        for z in range(NZ):
            edge_out[z, half, 0:8, :] = zero_tile
            edge_out[z, half, TAIL : TAIL + 8, :] = zero_tile

    def level(z, carry):
        for half in range(2):
            columns = slice(LANES * half, LANES * half + LANES)
            for f in range(F):
                first, second = X[half, f, z, 8:16, :], X[half, f, z, 16:24, :]
                edge = jnp.where(low_rows, first, second)
                edge_out[z, half, 8 + 8 * f : 16 + 8 * f, :] = edge
                if f < M:
                    Z[0, 8 * f : 8 * f + 8, columns] = jnp.where(low_rows, second, first)
                    Z[1, 8 * f : 8 * f + 8, columns] = edge
        high_in[z], low_in[z] = split(Z[0])
        high_edge[z], low_edge[z] = split(Z[1])
        return carry

    lax.fori_loop(0, NZ, level, 0, unroll=4)
    for copy in copies:
        copy.wait()
    for half in range(2):
        for z in range(NZ):
            VE[half, z, 0:8, :] = zero_tile
            FE[half, z, 0:8, :] = zero_tile
            W[half, z, 0:8, :] = zero_tile
            W[half, z, 24:32, :] = zero_tile
            for xt in range(2):
                rows = slice(8 * xt, 8 * xt + 8)
                padded = slice(8 * xt + 8, 8 * xt + 16)
                W[half, z, padded, :] = ints[0, half, z, rows, :].astype(f32)
                FN[half, z, rows, :] = ints[1, half, z, rows, :].astype(f32)
                FE[half, z, padded, :] = ints[2, half, z, rows, :].astype(f32)


def prepare(cells, ve, vn, fe, fn, mask):
    parts = jax.ShapeDtypeStruct((NZ, 8 * M, 256), bf16)
    padded = jax.ShapeDtypeStruct((2, NZ, 32, LANES), f32)
    plain = jax.ShapeDtypeStruct((2, NZ, BX, LANES), f32)
    return pl.pallas_call(
        prepare_kernel,
        out_shape=(
            parts,
            parts,
            parts,
            parts,
            jax.ShapeDtypeStruct((NZ, 2, TAIL + 8, LANES), f32),
            padded,
            padded,
            padded,
            plain,
            plain,
        ),
        in_specs=[VMEM] + [HBM] * 5,
        out_specs=(VMEM,) * 10,
        scratch_shapes=[
            pltpu.VMEM((3, 2, NZ, BX, LANES), jnp.int32),
            pltpu.VMEM((2, 8 * M, 256), f32),
            pltpu.SemaphoreType.DMA((10,)),
        ],
        compiler_params=params(16),
        cost_estimate=cost(10**6, 10**6),
        name="prepare",
    )(cells, ve, vn, fe, fn, mask)


def interior_kernel(
    X, VE, FE, W, VN, FN, high_in, low_in, west, east, own_last, own_first,
    high_out, low_out, edge_out, weights_out, mean_out, sums_out,
    H, C, G, T, Z, acc,
):
    acc[...] = jnp.zeros((512, 256), f32)
    lanes = lane_ids()
    rows = row_ids()

    for f in range(F, F + 3):
        after, before = east[f], west[f]
        for k in range(2 * NZ):
            H[f - F, k] = jnp.where(
                lanes < 64, rolled(after, -4 * k, 1), rolled(before, LANES - 3 - 4 * k, 1)
            )

    place = lanes % 4

    (v_in, f_in, w_in) = (west[F + i] for i in range(3))
    (v_own, f_own, w_own) = (own_first[F + i] for i in range(3))
    lower_of = lambda outer_plane, own: jnp.where(
        place == 0, rolled(outer_plane, -2, 1), rolled(own, 1, 1)
    )
    low_face = face_parts(
        lower_of(w_in, w_own) * w_own, lower_of(v_in, v_own), lower_of(f_in, f_own)
    )
    high_face = face_parts(w_own * rolled(w_own, -1, 1), v_own, f_own)
    first_gains = cell_weights(*low_face, *high_face)
    for d in range(1, 4):
        G[d - 1] = jnp.where(place < d, first_gains[3 - d], 0.0)
    w_next = east[F + 2]
    (v_own, f_own, w_own) = (own_last[F + i] for i in range(3))
    high_face = face_parts(
        w_own * jnp.where(place == 2, rolled(w_next, 2, 1), rolled(w_own, -1, 1)), v_own, f_own
    )
    low_face = tuple(rolled(part, 1, 1) for part in high_face)
    last_gains = cell_weights(*low_face, *high_face)
    for d in range(1, 4):
        G[2 + d] = jnp.where((place >= 3 - d) & (place < 3), last_gains[3 + d], 0.0)

    def beside(f):
        before, after = west[f], east[f]
        first = (
            G[0] * rolled(before, -2, 1) + G[1] * rolled(before, -1, 1) + G[2] * before
        )
        last = G[3] * rolled(after, 2, 1) + G[4] * rolled(after, 1, 1) + G[5] * after
        C[0, f] = first
        C[1, f] = rolled(last, LANES - 3, 1)

    for f in range(F):
        beside(f)

    def level(z, carry):
        z_up = jnp.minimum(z + 1, NZ - 1)
        z_down = jnp.maximum(z - 1, 0)
        for xt in range(2):
            start = 8 + 8 * xt

            def outer(index):
                return H[index - F, 2 * z + xt]

            def at(ref, half, offset):
                return ref[half, z, start + offset : start + offset + 8, :]

            wet = [at(W, half, 0) for half in range(2)]
            wx = []
            for half in range(2):
                before = wet[half] * at(W, half, -1)
                after = wet[half] * at(W, half, 1)
                wx.append(
                    cell_weights(
                        *face_parts(before, at(VE, half, -1), at(FE, half, -1)),
                        *face_parts(after, at(VE, half, 0), at(FE, half, 0)),
                    )
                )
            wet_out = outer(F + 2)
            following = along_lanes(wet[0], wet[1], wet_out, 1)
            own = [
                face_parts(
                    wet[half] * following[half],
                    VN[half, z, 8 * xt : 8 * xt + 8, :],
                    FN[half, z, 8 * xt : 8 * xt + 8, :],
                )
                for half in range(2)
            ]
            beyond = face_parts(wet_out * rolled(wet[0], -1, 1), outer(F), outer(F + 1))
            before = [along_lanes(own[0][i], own[1][i], beyond[i], -1) for i in range(3)]
            wy = [
                cell_weights(*(before[i][half] for i in range(3)), *own[half]) for half in range(2)
            ]
            wy = [
                [
                    jnp.where(
                        (lanes < 3 - j) if half == 0 else (lanes >= LANES + 3 - j), 0.0, wy[half][j]
                    )
                    if (half == 0) == (j < 3) and j != 3
                    else wy[half][j]
                    for j in range(7)
                ]
                for half in range(2)
            ]
            centre = [
                wx[half][3] + wy[half][3] - 2.0 * vert_diff * wet[half] for half in range(2)
            ]
            w_level = [vert_diff * wet[half] for half in range(2)]
            for half in range(2):
                for index, plane in enumerate((at(VE, half, 0), at(FE, half, 0), wet[half])):
                    if xt == 0:
                        weights_out[half, z, 3 + index] = plane
                    else:
                        weights_out[half, z, 3 + index] = jnp.where(
                            rows < 4, weights_out[half, z, 3 + index], plane
                        )
                for d in range(1, 4):
                    if xt == 0:
                        weights_out[half, z, d - 1] = jnp.where(rows < d, wx[half][3 - d], 0.0)
                    else:
                        weights_out[half, z, d - 1] += jnp.where(
                            rows >= 8 - d, wx[half][3 + d], 0.0
                        )
            for f in range(F):
                own_cells = [X[half, f, z, start : start + 8, :] for half in range(2)]
                total = [
                    centre[half] * own_cells[half]
                    + w_level[half]
                    * (
                        X[half, f, z_up, start : start + 8, :]
                        + X[half, f, z_down, start : start + 8, :]
                    )
                    for half in range(2)
                ]
                first, last = C[0, f], C[1, f]
                total[0] += jnp.where(lanes < 3, first, 0.0)
                total[1] += jnp.where(lanes >= LANES - 3, last, 0.0)
                C[0, f] = rolled(first, -4, 1)
                C[1, f] = rolled(last, -4, 1)
                for offset in (-3, -2, -1, 1, 2, 3):
                    moved = around_lanes(own_cells[0], own_cells[1], offset)
                    for half in range(2):
                        total[half] += wx[half][3 + offset] * X[
                            half, f, z, start + offset : start + offset + 8, :
                        ]
                        total[half] += wy[half][3 + offset] * moved[half]
                for half in range(2):
                    columns = slice(LANES * half, LANES * half + LANES)
                    low_rows = rows < 4
                    if f == M:
                        mean_out[z, 8 * xt : 8 * xt + 8, columns] = (
                            own_cells[half] + time_step * total[half]
                        )
                    elif xt == 0:
                        T[half, f] = total[half]
                    else:
                        near = T[half, f]
                        place = slice(8 * f, 8 * f + 8)
                        Z[place, columns] = jnp.where(low_rows, total[half], near)
                        edge_out[z, half, place, :] = jnp.where(low_rows, near, total[half])
        high, low = split(Z[...])
        high_out[z] = high
        low_out[z] = low
        return carry

    lax.fori_loop(0, NZ, level, 0, unroll=4)
    add_products(acc, joined(high_in, high_out), joined(low_in, low_out))
    sums_out[...] = field_sums(acc)


def interior(cells, planes, high_in, low_in, west, east, own_last, own_first):
    parts = jax.ShapeDtypeStruct((NZ, 8 * M, 256), bf16)
    return pl.pallas_call(
        interior_kernel,
        out_shape=(
            parts,
            parts,
            jax.ShapeDtypeStruct((NZ, 2, 8 * M, LANES), f32),
            jax.ShapeDtypeStruct((2, NZ, 6, 8, LANES), f32),
            jax.ShapeDtypeStruct((NZ, BX, 2 * LANES), f32),
            jax.ShapeDtypeStruct((64, 32), f32),
        ),
        in_specs=[VMEM] * 12,
        out_specs=(VMEM,) * 6,
        scratch_shapes=[
            pltpu.VMEM((3, 2 * NZ, 8, LANES), f32),
            pltpu.VMEM((2, F, 8, LANES), f32),
            pltpu.VMEM((6, 8, LANES), f32),
            pltpu.VMEM((2, M, 8, LANES), f32),
            pltpu.VMEM((8 * M, 256), f32),
            pltpu.VMEM((512, 256), f32),
        ],
        compiler_params=params(20),
        cost_estimate=cost(10**6, 10**6),
        name="interior",
    )(cells, *planes, high_in, low_in, west, east, own_last, own_first)


def edge_kernel(
    below, above, edge_in, edge_tail, high_in, low_in, weights, mean_in, sums_in,
    high_out, low_out, mean_out, sums_out, Z, acc,
):
    acc[...] = jnp.zeros((512, 256), f32)
    rows = row_ids()
    low_rows = rows < 4
    first_row = rows == 0
    last_row = rows == 7

    def rows_from(ref, half, f, zh, first):
        start = min(max(first, 0), 16)
        return rolled(ref[half, f, zh, start : start + 8, :], start - first, 0)

    def gains_of(half, z, zh, zi):
        speed, flag, wet = (weights[half, z, 3 + i] for i in range(3))
        speed = jnp.where(first_row, rows_from(below, half, F, zh, 3 * zi), speed)
        flag = jnp.where(first_row, rows_from(below, half, F, zh, 3 * zi + 1), flag)
        beyond = jnp.where(first_row, rows_from(below, half, F, zh, 3 * zi + 2), 0.0)
        beyond = jnp.where(last_row, rows_from(above, half, F, zh, 3 * zi - 7), beyond)
        a, b, d = face_parts(beyond * wet, speed, flag)
        near, far = 47.0 * a + 27.0 * b + d, 27.0 * a + 47.0 * b - d
        left, right = -13.0 * a - 3.0 * b, -3.0 * a - 13.0 * b
        outside = (
            weights[half, z, 0] + jnp.where(first_row, near, -far),
            weights[half, z, 1] + jnp.where(first_row, left, -right),
            weights[half, z, 2] + jnp.where(first_row, 2.0 * a, -2.0 * b),
        )
        inside = (
            jnp.where(first_row, far, -near),
            jnp.where(first_row, right, -left),
            jnp.where(first_row, 2.0 * b, -2.0 * a),
        )
        return outside, inside

    def group(zh, carry):
        for zi in range(8):
            z = 8 * zh + zi
            for half in range(2):
                outside, inside = gains_of(half, z, zh, zi)
                for f in range(F):
                    base = 8 + 8 * f
                    change = inside[0] * edge_in[z, half, base : base + 8, :]
                    for d in range(1, 4):
                        cells = jnp.where(
                            low_rows,
                            rows_from(below, half, f, zh, 3 * zi + 3 - d),
                            rows_from(above, half, f, zh, 3 * zi + d - 8),
                        )
                        change = change + outside[d - 1] * cells
                    for d in range(1, 3):
                        cells = jnp.where(
                            low_rows,
                            edge_in[z, half, base + d : base + d + 8, :],
                            edge_in[z, half, base - d : base - d + 8, :],
                        )
                        change = change + inside[d] * cells
                    if f < M:
                        Z[half, 8 * f : 8 * f + 8, :] = (
                            edge_tail[z, half, 8 * f : 8 * f + 8, :] + change
                        )
                    else:
                        columns = slice(LANES * half, LANES * half + LANES)
                        step = time_step * change
                        mean_out[z, 0:8, columns] = mean_in[z, 0:8, columns] + jnp.where(
                            low_rows, step, 0.0
                        )
                        mean_out[z, 8:16, columns] = mean_in[z, 8:16, columns] + jnp.where(
                            low_rows, 0.0, step
                        )
            high, low = split(jnp.concatenate([Z[0], Z[1]], axis=1))
            high_out[z] = high
            low_out[z] = low
            add_products(
                acc,
                jnp.concatenate([high_in[z], high], axis=0),
                jnp.concatenate([low_in[z], low], axis=0),
            )
        return carry

    lax.fori_loop(0, 2, group, 0, unroll=True)
    sums = sums_in[...] + field_sums(acc)
    identity = (
        lax.broadcasted_iota(jnp.int32, (32, 32), 0) == lax.broadcasted_iota(jnp.int32, (32, 32), 1)
    ).astype(f32)
    turned = lax.dot_general(
        identity, sums[32:64], (((1,), (1,)), ((), ())), precision=HIGH, preferred_element_type=f32
    )
    whole = sums[0:32] + sums[32:64] + turned
    sums_out[...] = jnp.concatenate([whole[8 * i : 8 * i + 8] for i in range(4)], axis=1)


def edges(below, above, edge_in, edge_tail, high_in, low_in, weights, mean_in, sums_in):
    parts = jax.ShapeDtypeStruct((NZ, 8 * M, 256), bf16)
    return pl.pallas_call(
        edge_kernel,
        out_shape=(
            parts,
            parts,
            jax.ShapeDtypeStruct(mean_in.shape, f32),
            jax.ShapeDtypeStruct((8, LANES), f32),
        ),
        in_specs=[VMEM] * 9,
        out_specs=(VMEM,) * 4,
        scratch_shapes=[
            pltpu.VMEM((2, 8 * M, LANES), f32),
            pltpu.VMEM((512, 256), f32),
        ],
        compiler_params=params(16),
        cost_estimate=cost(10**9, 10**7),
        name="edges",
    )(below, above, edge_in, edge_tail, high_in, low_in, weights, mean_in, sums_in)


def factor_and_map(sums, cell_count):
    whole = jnp.concatenate([sums[:, 32 * i : 32 * i + 32] for i in range(4)], axis=0)
    inner = whole * (1.0 / cell_count)
    row = lax.broadcasted_iota(jnp.int32, (M, 2 * M), 0)
    column = lax.broadcasted_iota(jnp.int32, (M, 2 * M), 1)
    update = jnp.where(
        column < M,
        jnp.where(column == row, 1.0, 0.0) - time_step * inner[M : 2 * M, :],
        jnp.where(column == row + M, time_step, 0.0),
    )
    half_way = jnp.dot(update, inner, precision=HIGH, preferred_element_type=f32)
    gram = lax.dot_general(
        half_way, update, (((1,), (1,)), ((), ())), precision=HIGH, preferred_element_type=f32
    )
    row_g = lax.broadcasted_iota(jnp.int32, (M, M), 0)
    column_g = lax.broadcasted_iota(jnp.int32, (M, M), 1)
    left, right = gram, update
    for j in range(M):
        share = jnp.where(row_g[:, 0:1] > j, left[:, j : j + 1] / left[j : j + 1, j : j + 1], 0.0)
        left = left - share * left[j : j + 1, :]
        right = right - share * right[j : j + 1, :]
    diagonal = jnp.sum(jnp.where(column_g == row_g, left, 0.0), axis=1, keepdims=True)
    scale = 1.0 / jnp.sqrt(diagonal)
    return jnp.where(column_g >= row_g, left * scale, 0.0), right * scale


def spread_map(mapping):
    parts = jnp.concatenate(split(mapping), axis=0)
    tall = (
        lax.broadcasted_iota(jnp.int32, (256, 2 * M), 0) // 8
        == lax.broadcasted_iota(jnp.int32, (256, 2 * M), 1)
    ).astype(bf16)
    wide = (
        lax.broadcasted_iota(jnp.int32, (2 * M, 256), 1) // 8
        == lax.broadcasted_iota(jnp.int32, (2 * M, 256), 0)
    ).astype(bf16)
    rows = jnp.dot(tall, parts, preferred_element_type=f32).astype(bf16)
    full = jnp.dot(rows, wide, preferred_element_type=f32)
    row = lax.broadcasted_iota(jnp.int32, (256, 256), 0)
    column = lax.broadcasted_iota(jnp.int32, (256, 256), 1)
    return jnp.where(row % 8 == column % 8, full, 0.0).astype(bf16)


def make_apply_kernel(cell_count):
    def apply_kernel(sums, *refs):
        parts, (out, factor_out, maps, new, sems) = refs[:8], refs[8:]
        factor, mapping = factor_and_map(sums[...], cell_count)
        factor_out[...] = factor
        maps[...] = spread_map(mapping)
        low_rows = lax.broadcasted_iota(jnp.int32, (M, 8, 256), 1) < 4

        def put(group, slot):
            return pltpu.make_async_copy(
                new.at[slot], out.at[:, pl.ds(GROUP * group, GROUP)], sems.at[slot]
            )

        for group in range(NZ // GROUP):
            slot = group % SLOTS
            if group >= SLOTS:
                put(group - SLOTS, slot).wait()
            for k in range(GROUP):
                z = GROUP * group + k
                results = []
                for i in (0, 4):
                    high = both(parts[i], parts[i + 2], z)
                    low = both(parts[i + 1], parts[i + 3], z)
                    first = jnp.dot(maps[...], high, preferred_element_type=f32)
                    second = jnp.dot(maps[0:128, :], low, preferred_element_type=f32)
                    results.append((first[0:128] + first[128:256] + second).reshape(M, 8, 256))
                inner, edge = results
                new[slot, :, k, 0:8, :] = jnp.where(low_rows, edge, inner)
                new[slot, :, k, 8:16, :] = jnp.where(low_rows, inner, edge)
            put(group, slot).start()
        for group in range(NZ // GROUP - SLOTS, NZ // GROUP):
            put(group, group % SLOTS).wait()

    return apply_kernel


def apply_map(sums, parts, cell_count):
    return pl.pallas_call(
        make_apply_kernel(cell_count),
        out_shape=(
            jax.ShapeDtypeStruct((M, NZ, BX, 256), f32),
            jax.ShapeDtypeStruct((M, M), f32),
        ),
        in_specs=[VMEM] * 9,
        out_specs=(ANY, VMEM),
        scratch_shapes=[
            pltpu.VMEM((256, 256), bf16),
            pltpu.VMEM((SLOTS, M, GROUP, BX, 256), f32),
            pltpu.SemaphoreType.DMA((SLOTS,)),
        ],
        compiler_params=params(16),
        cost_estimate=cost(10**9, 13 * 10**6),
        name="apply",
    )(sums, *parts)


def onward(value, axis):
    size = lax.axis_size(axis)
    return lax.ppermute(value, axis, [(i, i + 1) for i in range(size - 1)])


def backward(value, axis):
    size = lax.axis_size(axis)
    return lax.ppermute(value, axis, [(i + 1, i) for i in range(size - 1)])


def exchanged(value, axes, distance):
    size = lax.axis_size(axes)
    return lax.ppermute(value, axes, [(i, i ^ distance) for i in range(size)])


def shards(
    mean_field, mode_fields, velocity_east, velocity_north, flag_east, flag_north, ocean_mask
):
    axes = ("gx", "gy")
    (
        mean_field, mode_fields, velocity_east, velocity_north, flag_east, flag_north, ocean_mask
    ) = (
        pltpu.with_memory_space_constraint(value, pltpu.HBM)
        for value in (
            mean_field, mode_fields, velocity_east, velocity_north, flag_east, flag_north,
            ocean_mask,
        )
    )
    up, down, east_send, west_send, cells = pack(
        mode_fields, mean_field, velocity_east, velocity_north, flag_east, flag_north, ocean_mask
    )
    west = onward(east_send, "gy")
    east = backward(west_send, "gy")
    below = onward(up, "gx")
    above = backward(down, "gx")
    high_x, low_x, high_xe, low_xe, edge, *planes = prepare(
        cells, velocity_east, velocity_north, flag_east, flag_north, ocean_mask
    )
    high_t, low_t, edge_tail, weights, mean_part, sums_i = interior(
        cells, planes, high_x, low_x, west, east, east_send, west_send
    )
    high_te, low_te, mean_next, sums = edges(
        below, above, edge, edge_tail, high_xe, low_xe, weights, mean_part, sums_i
    )
    sums = sums + exchanged(sums, axes, 1)
    for first in (8, 32, 2):
        near, far, both = (exchanged(sums, axes, first * i) for i in (1, 2, 3))
        sums = (sums + near) + (far + both)
    cell_count = float(NZ * BX * 256 * lax.axis_size("gx") * lax.axis_size("gy"))
    parts = high_x, low_x, high_t, low_t, high_xe, low_xe, high_te, low_te
    modes_next, factor = apply_map(sums, parts, cell_count)
    return (mean_next, modes_next, factor)


def solution(mesh):
    plane = P(None, "gx", "gy")
    return jax.shard_map(
        shards,
        mesh=mesh,
        in_specs=(plane, P(None, None, "gx", "gy"), plane, plane, plane, plane, plane),
        out_specs=(plane, P(None, None, "gx", "gy"), P()),
        check_vma=False,
    )
```
